256 devices in a mesh: ta: 16 (over z_lo, y, core), ha: 16 (over z_hi, x).
Axes of the slice: x: 4, y: 4, z: 8 (z_hi: 4, z_lo: 2; z = z_hi * 2 + z_lo), core: 2. Of those that a mesh axis runs over, the one named last changes fastest.
Arguments:
- queries: bfloat16 [64, 64, 16, 1536], P('ta', 'ha'), may hold values from -5 to 5
- keys_values: bfloat16 [2, 64, 64, 16, 1536], P(None, 'ta', 'ha'), may hold values from -5 to 5
- upstream: bfloat16 [64, 64, 16, 1536], P('ta', 'ha'), may hold values from -6 to 6
- out_weight: bfloat16 [1536, 1536], P('ha'), may hold values from -0.15625 to 0.15625
- windows: int32 [12, 3], replicated, may hold values from 1 to 3, as said below
- bucket_owner: int32 [48], replicated, may hold values from 0 to 15, as said below
Outputs:
- d_queries: bfloat16 [64, 64, 16, 1536], P('ta', 'ha')
- d_keys_values: bfloat16 [2, 64, 64, 16, 1536], P(None, 'ta', 'ha')
- d_weight_owned: float32 [96, 32, 1536], P('ha', 'ta')
The draws below stay inside these ranges and needn't reach their ends.
Inputs may be any that keep to these rules, and one draw needn't show every extreme that they name: `windows`: sizes are odd; some head, drawn from the seed, has 3 along all three dimensions, and some other head has 1 along at least one dimension. `bucket_owner`: each owner holds at most 6 buckets and some owner holds exactly 6.
All inputs are finite; a program needn't handle non-finite values.
Results may differ from the reference program's by a relative error of at most 0.007.
Values may be sent and summed in bfloat16 or wider, within the bound.
A program may use at most 128 MiB of HBM per device.

```python
import math
import jax
import jax.numpy as jnp
from jax import lax

HEADS = 12
HEAD_DIM = 128
INNER = 1536
D_OUT = 1536
FRAMES_DEV = 4
ROWS_DEV = 4
COLUMNS = 16
TILE_W = 8
BUCKET_ROWS = 32
BUCKETS = 48
CAP = 6
FRAMES = 64
HEIGHT = 64
N_TA = 16
N_HA = 16


def draw_queries(key, part):
    key = jax.random.fold_in(key, 11)
    shape = (FRAMES, HEIGHT, COLUMNS, INNER)
    base = jnp.clip(jax.random.normal(key, shape, jnp.float32), -5.0, 5.0)
    return base.astype(jnp.bfloat16)


def draw_keys_values(key, part):
    key = jax.random.fold_in(key, 12)
    shape = (2, FRAMES, HEIGHT, COLUMNS, INNER)
    base = jnp.clip(jax.random.normal(key, shape, jnp.float32), -5.0, 5.0)
    return base.astype(jnp.bfloat16)


def draw_windows(key, part):
    key = jax.random.fold_in(key, 21)
    first_key, second_key, third_key, fourth_key = jax.random.split(key, 4)
    sizes = 2 * jax.random.randint(first_key, (HEADS, 3), 0, 2) + 1
    chosen = jax.random.randint(second_key, (), 0, HEADS)
    narrow = (chosen + 1 + jax.random.randint(third_key, (), 0, HEADS - 1)) % HEADS
    narrow_dim = jax.random.randint(fourth_key, (), 0, 3)
    head_ids = jnp.arange(HEADS)[:, None]
    dim_ids = jnp.arange(3)[None, :]
    sizes = jnp.where((head_ids == narrow) & (dim_ids == narrow_dim), 1, sizes)
    return jnp.where(head_ids == chosen, 3, sizes).astype(jnp.int32)


def draw_bucket_owner(key, part):
    key = jax.random.fold_in(key, 31)
    first_key, second_key, third_key = jax.random.split(key, 3)
    busiest = jax.random.randint(first_key, (), 0, N_HA)
    others = (busiest + 1 + jnp.arange(N_HA - 1)) % N_HA
    spread = jax.random.permutation(second_key, jnp.repeat(others, CAP, total_repeat_length=(N_HA - 1) * CAP))
    owners = jnp.concatenate([jnp.full((CAP,), busiest), spread[:BUCKETS - CAP]])
    return jax.random.permutation(third_key, owners).astype(jnp.int32)


def shard_levels(rng, shape, cuts, least, top_value):
    factor_of, own = 1.0, jax.random.fold_in(rng, 6)
    for dim, shards_of in cuts:
        steps = jnp.exp(jax.random.uniform(jax.random.fold_in(own, dim), (shards_of,), jnp.float32, least / len(cuts), top_value / len(cuts)))
        factor_of = factor_of * jnp.repeat(steps, shape[dim] // shards_of).reshape([-1 if axis == dim else 1 for axis in range(len(shape))])
    return factor_of


def normal_values(own_key, shape, scale, limit, cuts=(), kind=jnp.bfloat16):
    values = jax.random.normal(own_key, shape, jnp.float32) * scale
    if len(cuts) > 0:
        values = shard_levels(own_key, shape, cuts, -0.22, 0.18) * values
    return jnp.clip(values, min=-limit, max=limit).astype(kind)


def setup_inputs(seed: int = 0) -> dict:
    splits = jax.random.split(jax.random.key(seed), 7)
    return {
        "queries": draw_queries(jax.random.fold_in(splits[6], 71), 0),
        "keys_values": draw_keys_values(jax.random.fold_in(splits[6], 71), 0),
        "upstream": normal_values(splits[2], (FRAMES, HEIGHT, COLUMNS, D_OUT), 1.0, 6.0, ((0, 16), (1, 16))),
        "out_weight": normal_values(splits[3], (INNER, D_OUT), INNER ** -0.5, 0.15625, ((0, 16),)),
        "windows": draw_windows(jax.random.fold_in(splits[6], 71), 0),
        "bucket_owner": draw_bucket_owner(jax.random.fold_in(splits[6], 71), 0),
    }


def window_mask(windows, time_index, height_index, frames_dev, rows_dev, columns, all_frames, all_rows):
    query_count = frames_dev * rows_dev * columns
    key_count = (frames_dev + 2) * (rows_dev + 2) * columns
    query_ids = jnp.arange(query_count, dtype=jnp.int32)
    key_ids = jnp.arange(key_count, dtype=jnp.int32)
    query_frame = query_ids // (rows_dev * columns)
    query_row = query_ids // columns % rows_dev
    query_tile = query_ids % columns // TILE_W
    key_frame = key_ids // ((rows_dev + 2) * columns)
    key_row = key_ids // columns % (rows_dev + 2)
    key_tile = key_ids % columns // TILE_W
    time_gap = jnp.abs(query_frame[:, None] - key_frame[None, :] + 1)
    row_gap = jnp.abs(query_row[:, None] - key_row[None, :] + 1)
    tile_gap = jnp.abs(query_tile[:, None] - key_tile[None, :])
    global_frame = time_index * frames_dev + key_frame - 1
    global_row = height_index * rows_dev + key_row - 1
    present = (global_frame >= 0) & (global_frame < all_frames) & (global_row >= 0) & (global_row < all_rows)
    reaches = (windows - 1) // 2
    allowed = (time_gap[None] <= reaches[:, 0, None, None]) & (row_gap[None] <= reaches[:, 1, None, None])
    allowed = allowed & (tile_gap[None] <= reaches[:, 2, None, None]) & present[None, None, :]
    return allowed

def attend(query_block, key_block, value_block, grad_block, allowed):
    query_count = query_block.shape[0]
    key_count = key_block.shape[0]
    scaling = HEAD_DIM ** (-0.5)
    query3 = query_block.reshape(query_count, HEADS, HEAD_DIM).astype(jnp.float32)
    key3 = key_block.reshape(key_count, HEADS, HEAD_DIM).astype(jnp.float32)
    value3 = value_block.reshape(key_count, HEADS, HEAD_DIM).astype(jnp.float32)
    grad3 = grad_block.reshape(query_count, HEADS, HEAD_DIM).astype(jnp.float32)
    scores = jnp.einsum('qhd,khd->hqk', query3, key3) * scaling
    scores = jnp.where(allowed, scores, -1e+30)
    highest = lax.optimization_barrier(jnp.max(scores, axis=2, keepdims=True))
    weights = jnp.exp(scores - highest)
    probs = weights / lax.optimization_barrier(jnp.sum(weights, axis=2, keepdims=True))
    probs_low = lax.optimization_barrier(probs.astype(jnp.bfloat16)).astype(jnp.float32)
    attn_out = jnp.einsum('hqk,khd->qhd', probs_low, value3).reshape(query_count, HEADS * HEAD_DIM).astype(jnp.bfloat16)
    grad_probs = jnp.einsum('qhd,khd->hqk', grad3, value3)
    delta = lax.optimization_barrier(jnp.sum(probs * grad_probs, axis=2, keepdims=True))
    grad_scores = (probs * (grad_probs - delta) * scaling).astype(jnp.bfloat16)
    grad_scores = lax.optimization_barrier(grad_scores).astype(jnp.float32)
    grad_query = jnp.einsum('hqk,khd->qhd', grad_scores, key3).reshape(query_count, HEADS * HEAD_DIM).astype(jnp.bfloat16)
    grad_key = jnp.einsum('hqk,qhd->khd', grad_scores, query3).reshape(key_count, HEADS * HEAD_DIM).astype(jnp.bfloat16)
    grad_value = jnp.einsum('hqk,qhd->khd', probs_low, grad3).reshape(key_count, HEADS * HEAD_DIM).astype(jnp.bfloat16)
    return (attn_out, grad_query, grad_key, grad_value)

def reference(queries, keys_values, upstream, out_weight, windows, bucket_owner):
    all_frames, all_rows, columns, inner_width = queries.shape
    out_width = upstream.shape[3]
    frames_dev = FRAMES_DEV
    rows_dev = ROWS_DEV
    query_count = frames_dev * rows_dev * columns
    key_count = (frames_dev + 2) * (rows_dev + 2) * columns
    grad_out = jnp.dot(upstream.reshape(-1, out_width), out_weight.T, preferred_element_type=jnp.float32)
    grad_out = grad_out.astype(jnp.bfloat16).reshape(all_frames, all_rows, columns, inner_width)
    padded = jnp.pad(keys_values, ((0, 0), (1, 1), (1, 1), (0, 0), (0, 0)))
    anchor = jnp.zeros((), jnp.int32)

    def visit(block, carry):
        grad_queries, grad_total, weight_total = carry
        time_index = (block // N_HA).astype(jnp.int32)
        height_index = (block % N_HA).astype(jnp.int32)
        frame_start = (time_index * frames_dev).astype(jnp.int32)
        row_start = (height_index * rows_dev).astype(jnp.int32)
        query_block = lax.dynamic_slice(queries, (frame_start, row_start, anchor, anchor), (frames_dev, rows_dev, columns, inner_width)).reshape(query_count, inner_width)
        grad_block = lax.dynamic_slice(grad_out, (frame_start, row_start, anchor, anchor), (frames_dev, rows_dev, columns, inner_width)).reshape(query_count, inner_width)
        upstream_block = lax.dynamic_slice(upstream, (frame_start, row_start, anchor, anchor), (frames_dev, rows_dev, columns, out_width)).reshape(query_count, out_width)
        key_block = lax.dynamic_slice(padded, (anchor, frame_start, row_start, anchor, anchor), (2, frames_dev + 2, rows_dev + 2, columns, inner_width)).reshape(2, key_count, inner_width)
        allowed = window_mask(windows, time_index, height_index, frames_dev, rows_dev, columns, all_frames, all_rows)
        attn_out, grad_query, grad_key, grad_value = attend(query_block, key_block[0], key_block[1], grad_block, allowed)
        grad_queries = lax.dynamic_update_slice(grad_queries, grad_query.reshape(frames_dev, rows_dev, columns, inner_width), (frame_start, row_start, anchor, anchor))
        stacked = jnp.stack([grad_key, grad_value]).astype(jnp.float32).reshape(2, frames_dev + 2, rows_dev + 2, columns, inner_width)
        corner = (anchor, frame_start, row_start, anchor, anchor)
        grad_total = lax.dynamic_update_slice(grad_total, lax.dynamic_slice(grad_total, corner, stacked.shape) + stacked, corner)
        weight_total = weight_total + jnp.dot(attn_out.T, upstream_block, preferred_element_type=jnp.float32)
        return (grad_queries, grad_total, weight_total)
    initial = (jnp.zeros(queries.shape, jnp.bfloat16), jnp.zeros(padded.shape, jnp.float32), jnp.zeros((inner_width, out_width), jnp.float32))
    grad_queries, grad_total, weight_total = lax.fori_loop(0, N_TA * N_HA, visit, initial)
    grad_pairs = grad_total[:, 1:-1, 1:-1].astype(jnp.bfloat16)
    weight_grad = weight_total / math.sqrt(all_frames * all_rows * columns)
    bucket_ids = jnp.arange(BUCKETS, dtype=jnp.int32)
    same_owner = bucket_owner[None, :] == bucket_owner[:, None]
    earlier = bucket_ids[None, :] < bucket_ids[:, None]
    ranking = lax.optimization_barrier(jnp.sum((same_owner & earlier).astype(jnp.int32), axis=1)).astype(jnp.int32)
    slot = (bucket_owner * CAP + ranking).astype(jnp.int32)
    owned = jnp.zeros((N_HA * CAP, BUCKET_ROWS, out_width), jnp.float32)
    owned = owned.at[slot].set(weight_grad.reshape(BUCKETS, BUCKET_ROWS, out_width))
    return (grad_queries, grad_pairs, owned)
```

```python
import jax
import jax.numpy as jnp
from jax import lax
from jax.experimental import pallas as pl
from jax.experimental.pallas import tpu as pltpu
from jax.sharding import PartitionSpec as P

HEADS = 12
HEAD_DIM = 128
TILE_W = 8
BUCKET_ROWS = 32


def with_halo(cells, sides, width):
    for axis, dim in sides:
        count = lax.axis_size(axis)
        ends = count - 1
        head = lax.slice_in_dim(cells, 0, width, axis=dim)
        tail = lax.slice_in_dim(cells, cells.shape[dim] - width, cells.shape[dim], axis=dim)
        cells = jnp.concatenate(
            [
                lax.ppermute(tail, axis, [(i, (i + 1) % count) for i in range(ends)]),
                cells,
                lax.ppermute(head, axis, [((i + 1) % count, i) for i in range(ends)]),
            ],
            axis=dim,
        )
    return cells


def window_mask(
    windows, time_index, height_index, frames_dev, rows_dev, columns, all_frames, all_rows
):
    query_count = frames_dev * rows_dev * columns
    key_count = (frames_dev + 2) * (rows_dev + 2) * columns
    query_ids = jnp.arange(query_count, dtype=jnp.int32)
    key_ids = jnp.arange(key_count, dtype=jnp.int32)
    query_frame = query_ids // (rows_dev * columns)
    query_row = query_ids // columns % rows_dev
    query_tile = query_ids % columns // TILE_W
    key_frame = key_ids // ((rows_dev + 2) * columns)
    key_row = key_ids // columns % (rows_dev + 2)
    key_tile = key_ids % columns // TILE_W
    time_gap = jnp.abs(query_frame[:, None] - key_frame[None, :] + 1)
    row_gap = jnp.abs(query_row[:, None] - key_row[None, :] + 1)
    tile_gap = jnp.abs(query_tile[:, None] - key_tile[None, :])
    global_frame = time_index * frames_dev + key_frame - 1
    global_row = height_index * rows_dev + key_row - 1
    present = (
        (global_frame >= 0)
        & (global_frame < all_frames)
        & (global_row >= 0)
        & (global_row < all_rows)
    )
    reaches = (windows - 1) // 2
    allowed = (time_gap[None] <= reaches[:, 0, None, None]) & (
        row_gap[None] <= reaches[:, 1, None, None]
    )
    allowed = allowed & (tile_gap[None] <= reaches[:, 2, None, None]) & present[None, None, :]
    return allowed


def attend(query_block, key_block, value_block, grad_block, allowed):
    query_count = query_block.shape[0]
    key_count = key_block.shape[0]
    scaling = HEAD_DIM ** (-0.5)
    query3 = query_block.reshape(query_count, HEADS, HEAD_DIM)
    key3 = key_block.reshape(key_count, HEADS, HEAD_DIM)
    value3 = value_block.reshape(key_count, HEADS, HEAD_DIM)
    grad3 = grad_block.reshape(query_count, HEADS, HEAD_DIM)
    scores = jnp.einsum("qhd,khd->hqk", query3, key3, preferred_element_type=jnp.float32) * scaling
    scores = jnp.where(allowed, scores, -1e30)
    highest = jnp.max(scores, axis=2, keepdims=True)
    weights = jnp.exp(scores - highest)
    probs = weights / jnp.sum(weights, axis=2, keepdims=True)
    probs_low = probs.astype(jnp.bfloat16)
    attn_out = jnp.einsum("hqk,khd->qhd", probs_low, value3, preferred_element_type=jnp.float32)
    attn_out = attn_out.reshape(query_count, HEADS * HEAD_DIM).astype(jnp.bfloat16)
    grad_probs = jnp.einsum("qhd,khd->hqk", grad3, value3, preferred_element_type=jnp.float32)
    delta = jnp.sum(probs * grad_probs, axis=2, keepdims=True)
    grad_scores = (probs * (grad_probs - delta) * scaling).astype(jnp.bfloat16)
    grad_query = jnp.einsum("hqk,khd->qhd", grad_scores, key3, preferred_element_type=jnp.float32)
    grad_query = grad_query.reshape(query_count, HEADS * HEAD_DIM).astype(jnp.bfloat16)
    grad_key = jnp.einsum("hqk,qhd->khd", grad_scores, query3, preferred_element_type=jnp.float32)
    grad_key = grad_key.reshape(key_count, HEADS * HEAD_DIM).astype(jnp.bfloat16)
    grad_value = jnp.einsum("hqk,qhd->khd", probs_low, grad3, preferred_element_type=jnp.float32)
    grad_value = grad_value.reshape(key_count, HEADS * HEAD_DIM).astype(jnp.bfloat16)
    return (attn_out, grad_query, grad_key, grad_value)


def place():
    ta, ha = lax.axis_index("ta"), lax.axis_index("ha")
    return ta // 8, ta // 2 % 4, ta % 2, ha // 4, ha % 4


def at_place(z_lo, y, core, z_hi, x):
    return {"ta": z_lo * 8 + y * 2 + core, "ha": z_hi * 4 + x}


class Ring:
    def __init__(self, src, pos, after, before, bufs, send, recv):
        self.src, self.pos, self.after, self.before = src, pos, after, before
        self.left, self.right, self.via_left, self.via_right, self.stage = bufs
        self.send, self.recv = send, recv
        self.copies = []

    def copy(self, src, dst, index, device):
        made = pltpu.make_async_remote_copy(
            src_ref=src,
            dst_ref=dst,
            send_sem=self.send.at[index],
            recv_sem=self.recv.at[index],
            device_id=device,
            device_id_type=pl.DeviceIdType.MESH,
        )
        made.start()
        self.copies.append(made)

    def start(self):
        pos, src = self.pos, self.src
        far = (pos + 2) % 4
        self.copy(src.at[far, 0], self.via_left, 0, self.after)
        self.copy(src.at[far, 1], self.via_right, 1, self.before)
        self.copy(src.at[(pos + 1) % 4, 1], self.left.at[1], 2, self.after)
        self.copy(src.at[(pos + 3) % 4, 0], self.right.at[0], 3, self.before)

    def middle(self):
        pos, src = self.pos, self.src
        for index, (via, goal, dst, device) in enumerate(
            (
                (self.via_left, (pos + 1) % 4, self.left, self.after),
                (self.via_right, (pos + 3) % 4, self.right, self.before),
            )
        ):
            self.copies[index].wait_recv()
            total = via[...].astype(jnp.float32) + src[goal, index].astype(jnp.float32)
            self.stage[index] = total.astype(self.stage.dtype)
            self.copy(self.stage.at[index], dst.at[index], 4 + index, device)

    def end(self, half):
        for index in ((3, 4), (2, 5))[half]:
            self.copies[index].wait_recv()
        return (
            self.src[self.pos, half].astype(jnp.float32)
            + self.left[half].astype(jnp.float32)
            + self.right[half].astype(jnp.float32)
        )

    def drain(self):
        for made in self.copies:
            made.wait_send()


def ring_buffers(rows, columns):
    return [
        pltpu.VMEM((2, rows, columns), jnp.bfloat16),
        pltpu.VMEM((2, rows, columns), jnp.bfloat16),
        pltpu.VMEM((rows, columns), jnp.bfloat16),
        pltpu.VMEM((rows, columns), jnp.bfloat16),
        pltpu.VMEM((2, rows, columns), jnp.bfloat16),
    ]


def weight_kernel(at, up, fin, *refs):
    at_in, up_in, first_a, first_b, second_a, second_b, pair, pair_in, tall, tall_in = refs[:10]
    rings = [refs[10 + 5 * i : 15 + 5 * i] for i in range(4)]
    ring_send, ring_recv, send, recv = refs[30:]
    z_lo, y, core, z_hi, x = place()
    partner = at_place(z_lo, y, 1 - core, z_hi, x)
    y_after, y_before = (at_place(z_lo, (y + s) % 4, core, z_hi, x) for s in (1, 3))
    x_peers = [at_place(z_lo, y, core, z_hi, (x + s) % 4) for s in (1, 2, 3)]
    low_peer = at_place(1 - z_lo, y, core, z_hi, x)
    high_peers = [at_place(z_lo, y, core, (z_hi + s) % 4, x) for s in (1, 2, 3)]
    peers = [partner, y_after, y_before, *x_peers, low_peer, *high_peers]
    barrier = pltpu.get_barrier_semaphore()
    for peer in peers:
        pl.semaphore_signal(barrier, inc=1, device_id=peer, device_id_type=pl.DeviceIdType.MESH)
    pl.semaphore_wait(barrier, len(peers))

    def copy(src, dst, index, device):
        made = pltpu.make_async_remote_copy(
            src_ref=src,
            dst_ref=dst,
            send_sem=send.at[index],
            recv_sem=recv.at[index],
            device_id=device,
            device_id_type=pl.DeviceIdType.MESH,
        )
        made.start()
        return made

    others = [copy(at.at[1 - core], at_in, 0, partner), copy(up, up_in, 1, partner)]
    for made in others:
        made.wait_recv()

    def product(part, start, width):
        mine = jnp.dot(at[core, part], up[:, start : start + width], preferred_element_type=jnp.float32)
        theirs = jnp.dot(at_in[part], up_in[:, start : start + width], preferred_element_type=jnp.float32)
        return (mine + theirs).astype(jnp.bfloat16)

    ring_a = Ring(first_a, y, y_after, y_before, rings[0], ring_send.at[0], ring_recv.at[0])
    ring_b = Ring(first_b, x, x_peers[0], x_peers[2], rings[1], ring_send.at[1], ring_recv.at[1])
    for half in range(2):
        block = product(0, half * 768, 768)
        for goal in range(4):
            first_a[goal, half] = block[goal * 96 : goal * 96 + 96]
    ring_a.start()
    for goal in range(4):
        block = product(1, goal * 384, 384)
        for half in range(2):
            first_b[goal, half] = block[half * 192 : half * 192 + 192]
    ring_b.start()
    ring_a.middle()
    ring_b.middle()
    ring_c = Ring(second_a, x, x_peers[0], x_peers[2], rings[2], ring_send.at[2], ring_recv.at[2])
    ring_d = Ring(second_b, y, y_after, y_before, rings[3], ring_send.at[3], ring_recv.at[3])
    for half in range(2):
        block = ring_a.end(half).astype(jnp.bfloat16)
        for goal in range(2):
            for row in range(2):
                second_a[half * 2 + goal, row] = block[row * 48 : row * 48 + 48, goal * 384 : goal * 384 + 384]
    ring_c.start()
    for half in range(2):
        block = ring_b.end(half).astype(jnp.bfloat16)
        for goal in range(2):
            for row in range(2):
                begin = goal * 96 + row * 48
                second_b[half * 2 + goal, row] = block[begin : begin + 48]
    ring_d.start()
    ring_c.middle()
    ring_d.middle()
    for part, ring in enumerate((ring_c, ring_d)):
        for row in range(2):
            pair[part, row * 48 : row * 48 + 48] = ring.end(row).astype(jnp.bfloat16)
    low = copy(pair.at[1 - z_lo], pair_in, 2, low_peer)
    low.wait_recv()
    total = pair[z_lo].astype(jnp.float32) + pair_in[...].astype(jnp.float32)
    tall[...] = total.astype(jnp.bfloat16)
    highs = [copy(tall, tall_in.at[i], 3 + i, high_peers[i]) for i in range(3)]
    for i in range(3):
        highs[i].wait_recv()
        total += tall_in[i].astype(jnp.float32)
    fin[x] = (total * 0.00390625).astype(jnp.bfloat16)
    lasts = [copy(fin.at[x], fin.at[x], 6 + i, x_peers[i]) for i in range(3)]
    for made in lasts:
        made.wait_recv()
    for made in (*others, low, *highs, *lasts):
        made.wait_send()
    for ring in (ring_a, ring_b, ring_c, ring_d):
        ring.drain()


def weight_sum(at, up):
    bf16 = jnp.bfloat16
    vmem = pl.BlockSpec(memory_space=pltpu.VMEM)
    return pl.pallas_call(
        weight_kernel,
        out_shape=jax.ShapeDtypeStruct((4, 96, 384), bf16),
        in_specs=[vmem, vmem],
        out_specs=vmem,
        scratch_shapes=[
            pltpu.VMEM((2, 384, 256), bf16),
            pltpu.VMEM((256, 1536), bf16),
            pltpu.VMEM((4, 2, 96, 768), bf16),
            pltpu.VMEM((4, 2, 192, 384), bf16),
            pltpu.VMEM((4, 2, 48, 384), bf16),
            pltpu.VMEM((4, 2, 48, 384), bf16),
            pltpu.VMEM((2, 96, 384), bf16),
            pltpu.VMEM((96, 384), bf16),
            pltpu.VMEM((96, 384), bf16),
            pltpu.VMEM((3, 96, 384), bf16),
            *ring_buffers(96, 768),
            *ring_buffers(192, 384),
            *ring_buffers(48, 384),
            *ring_buffers(48, 384),
            pltpu.SemaphoreType.DMA((4, 6)),
            pltpu.SemaphoreType.DMA((4, 6)),
            pltpu.SemaphoreType.DMA((9,)),
            pltpu.SemaphoreType.DMA((9,)),
        ],
        compiler_params=pltpu.CompilerParams(
            collective_id=1, has_side_effects=True, vmem_limit_bytes=40 * 1024 * 1024
        ),
    )(at, up)


def owned_slots(fin, bucket_owner, height_index):
    bucket_ids = jnp.arange(48, dtype=jnp.int32)
    same_owner = bucket_owner[None, :] == bucket_owner[:, None]
    ranking = jnp.sum((same_owner & (bucket_ids[None, :] < bucket_ids[:, None])).astype(jnp.int32), axis=1)
    slot = jnp.where(bucket_owner == height_index, ranking, -1)
    chosen = jnp.repeat(slot * 2, 2) + jnp.tile(jnp.arange(2, dtype=jnp.int32), 48)
    pick = (chosen[None, :] == jnp.arange(12, dtype=jnp.int32)[:, None]).astype(jnp.bfloat16)
    owned = jnp.einsum("sr,xrc->sxc", pick, fin, preferred_element_type=jnp.float32)
    return owned.reshape(6, 2, 1536)


def per_device(queries, keys_values, upstream, out_weight, windows, bucket_owner):
    frames, height_rows, columns, inner_width = queries.shape
    out_width = upstream.shape[3]
    time_count = lax.axis_size("ta")
    height_count = lax.axis_size("ha")
    time_index = lax.axis_index("ta")
    height_index = lax.axis_index("ha")
    query_count = frames * height_rows * columns
    key_count = (frames + 2) * (height_rows + 2) * columns
    padded = with_halo(keys_values, (("ta", 1), ("ha", 2)), 1)
    upstream_flat = upstream.reshape(query_count, out_width)
    grad_out = lax.dot_general(
        upstream_flat,
        lax.all_gather(out_weight, "ha", axis=0, tiled=True),
        (((1,), (1,)), ((), ())),
        preferred_element_type=jnp.float32,
    ).astype(jnp.bfloat16)
    allowed = window_mask(
        windows,
        time_index,
        height_index,
        frames,
        height_rows,
        columns,
        frames * time_count,
        height_rows * height_count,
    )
    key_flat = padded.reshape(2, key_count, inner_width)
    attn_out, grad_query, grad_key, grad_value = attend(
        queries.reshape(query_count, inner_width), key_flat[0], key_flat[1], grad_out, allowed
    )
    grads = jnp.stack([grad_key, grad_value]).reshape(
        2, frames + 2, height_rows + 2, columns, inner_width
    )
    lifted = grads[:, 1:-1].at[:, 0].set(grads[:, 0]).at[:, frames - 1].set(grads[:, frames + 1])
    from_time = with_halo(lifted, (("ta", 1),), 1)
    lower_rim = from_time[:, 0]
    upper_rim = from_time[:, frames + 1]
    carried = jnp.zeros((2, frames, height_rows + 2, columns, inner_width), jnp.bfloat16)
    carried = carried.at[:, 0].set(lower_rim).at[:, frames - 1].set(upper_rim)
    packed = jnp.stack([grads[:, 1:-1], carried])
    outgoing = (
        packed[:, :, :, 1:-1]
        .at[:, :, :, 0]
        .set(packed[:, :, :, 0])
        .at[:, :, :, height_rows - 1]
        .set(packed[:, :, :, height_rows + 1])
    )
    from_height = with_halo(outgoing, (("ha", 3),), 1)
    summed = grads[:, 1:-1, 1:-1].astype(jnp.float32)
    summed = summed.at[:, 0].add(lower_rim[:, 1:-1].astype(jnp.float32))
    summed = summed.at[:, frames - 1].add(upper_rim[:, 1:-1].astype(jnp.float32))
    below = from_height[0, :, :, 0].astype(jnp.float32) + from_height[1, :, :, 0].astype(
        jnp.float32
    )
    above = from_height[0, :, :, height_rows + 1].astype(jnp.float32) + from_height[
        1, :, :, height_rows + 1
    ].astype(jnp.float32)
    summed = summed.at[:, :, 0].add(below).at[:, :, height_rows - 1].add(above)
    grad_pairs = summed.astype(jnp.bfloat16)
    at = attn_out.reshape(256, 48, 2, 4, 2, 2).transpose(4, 2, 3, 1, 5, 0).reshape(2, 2, 384, 256)
    owned = owned_slots(weight_sum(at, upstream_flat), bucket_owner, height_index)
    return (
        grad_query.reshape(frames, height_rows, columns, inner_width),
        grad_pairs,
        owned,
    )


def solution(mesh):
    return jax.shard_map(
        per_device,
        mesh=mesh,
        in_specs=(
            P("ta", "ha", None, None),
            P(None, "ta", "ha", None, None),
            P("ta", "ha", None, None),
            P("ha", None),
            P(),
            P(),
        ),
        out_specs=(P("ta", "ha", None, None), P(None, "ta", "ha", None, None), P("ha", "ta", None)),
        check_vma=False,
    )
```

```python
import jax
import jax.numpy as jnp
from jax import lax
from jax.experimental import pallas as pl
from jax.experimental.pallas import tpu as pltpu
from jax.sharding import PartitionSpec as P

HEADS = 12
HEAD_DIM = 128
TILE_W = 8
BUCKET_ROWS = 32


def with_halo(cells, sides, width):
    for axis, dim in sides:
        count = lax.axis_size(axis)
        ends = count - 1
        head = lax.slice_in_dim(cells, 0, width, axis=dim)
        tail = lax.slice_in_dim(cells, cells.shape[dim] - width, cells.shape[dim], axis=dim)
        cells = jnp.concatenate(
            [
                lax.ppermute(tail, axis, [(i, (i + 1) % count) for i in range(ends)]),
                cells,
                lax.ppermute(head, axis, [((i + 1) % count, i) for i in range(ends)]),
            ],
            axis=dim,
        )
    return cells


def attend_kernel(q, kv, up, weight, windows, dq, dkv, at, need):
    time_index, height_index = lax.axis_index("ta"), lax.axis_index("ha")
    key = lax.broadcasted_iota(jnp.int32, (96, 256), 0)
    token = lax.broadcasted_iota(jnp.int32, (96, 256), 1)
    row_gap = jnp.abs((token >> 4 & 3) - (key >> 4) + 1)
    tile_gap = jnp.abs((token >> 3 & 1) - (key >> 3 & 1))
    row = height_index * 4 + (key >> 4) - 1
    base = jnp.where((row_gap > 1) | (row < 0) | (row >= 64), 8, row_gap * 2 + tile_gap * 4)
    for f in range(6):
        time_gap = jnp.abs((token >> 6) - f + 1)
        frame = time_index * 4 + f - 1
        outside = (time_gap > 1) | (frame < 0) | (frame >= 64)
        need[f * 96 : f * 96 + 96] = base | jnp.where(outside, 8, time_gap)
    out_row = lax.broadcasted_iota(jnp.int32, (128, 128), 0)
    feature = lax.broadcasted_iota(jnp.int32, (128, 128), 1)
    group = out_row >> 3
    piece = (group >> 2 & 1) * 8 + (group & 3) * 2 + (group >> 3)
    wanted = (out_row >> 1 & 3) * 32 + piece * 2 + (out_row & 1)
    order = (wanted == feature).astype(jnp.bfloat16)
    eye = (out_row == feature).astype(jnp.bfloat16)
    scaling = HEAD_DIM ** (-0.5)
    across = (((1,), (1,)), ((), ()))
    f32, bf16 = jnp.float32, jnp.bfloat16

    def visit(pair, carry):
        both = pl.ds(pl.multiple_of(pair * 256, 256), 256)
        grad_pair = lax.dot_general(up[...], weight[both, :], across, preferred_element_type=f32).astype(bf16)
        outs = []
        for side in range(2):
            head = pair * 2 + side
            cols = pl.ds(pl.multiple_of(head * 128, 128), 128)
            query, keys, values = q[:, cols], kv[0, :, cols], kv[1, :, cols]
            grad = grad_pair[:, side * 128 : side * 128 + 128]
            block = 15 - sum(((windows[head, a] - 1) // 2) << a for a in range(3))
            scores = lax.dot_general(keys, query, across, preferred_element_type=f32)
            scores = jnp.where((need[...] & block) == 0, scores, -1e30)
            highest = jnp.max(scores, axis=0, keepdims=True)
            weights = jnp.exp2((scores - highest) * (scaling * 1.4426950408889634))
            inverse = 1.0 / jnp.sum(weights, axis=0, keepdims=True)
            probs = weights * inverse
            probs_low = probs.astype(bf16)
            grad_probs = lax.dot_general(values, grad, across, preferred_element_type=f32)
            delta = jnp.sum(probs * grad_probs, axis=0, keepdims=True)
            grad_scores = (probs * (grad_probs - delta) * scaling).astype(bf16)
            values_t = lax.dot_general(order, values, across, preferred_element_type=f32).astype(bf16)
            outs.append(jnp.dot(values_t, probs_low, preferred_element_type=f32).reshape(16, 8, 256))
            keys_t = lax.dot_general(eye, keys, across, preferred_element_type=f32).astype(bf16)
            dq[:, cols] = jnp.dot(keys_t, grad_scores, preferred_element_type=f32).T.astype(bf16)
            dkv[0, :, cols] = jnp.dot(grad_scores, query, preferred_element_type=f32).astype(bf16)
            dkv[1, :, cols] = jnp.dot(probs_low, grad, preferred_element_type=f32).astype(bf16)
        at[:, pl.ds(pl.multiple_of(pair * 16, 16), 16), :] = jnp.concatenate(outs, axis=1).astype(bf16)
        return carry

    lax.fori_loop(0, 6, visit, 0)


def attend(q, kv, up, weight, windows):
    bf16 = jnp.bfloat16
    vmem = pl.BlockSpec(memory_space=pltpu.VMEM)
    return pl.pallas_call(
        attend_kernel,
        out_shape=[
            jax.ShapeDtypeStruct((256, 1536), bf16),
            jax.ShapeDtypeStruct((2, 576, 1536), bf16),
            jax.ShapeDtypeStruct((16, 96, 256), bf16),
        ],
        in_specs=[vmem, vmem, vmem, vmem, pl.BlockSpec(memory_space=pltpu.SMEM)],
        out_specs=[vmem, vmem, vmem],
        scratch_shapes=[pltpu.VMEM((576, 256), jnp.int32)],
        compiler_params=pltpu.CompilerParams(vmem_limit_bytes=48 * 1024 * 1024),
    )(q, kv, up, weight, windows)


def place():
    ta, ha = lax.axis_index("ta"), lax.axis_index("ha")
    return ta // 8, ta // 2 % 4, ta % 2, ha // 4, ha % 4


def at_place(z_lo, y, core, z_hi, x):
    return {"ta": z_lo * 8 + y * 2 + core, "ha": z_hi * 4 + x}


class Ring:
    def __init__(self, src, pos, after, before, bufs, send, recv):
        self.src, self.pos, self.after, self.before = src, pos, after, before
        self.left, self.right, self.via_left, self.via_right, self.stage = bufs
        self.send, self.recv = send, recv
        self.copies = []

    def copy(self, src, dst, index, device):
        made = pltpu.make_async_remote_copy(
            src_ref=src,
            dst_ref=dst,
            send_sem=self.send.at[index],
            recv_sem=self.recv.at[index],
            device_id=device,
            device_id_type=pl.DeviceIdType.MESH,
        )
        made.start()
        self.copies.append(made)

    def start(self):
        pos, src = self.pos, self.src
        far = (pos + 2) % 4
        self.copy(src.at[far, 0], self.via_left, 0, self.after)
        self.copy(src.at[far, 1], self.via_right, 1, self.before)
        self.copy(src.at[(pos + 1) % 4, 1], self.left.at[1], 2, self.after)
        self.copy(src.at[(pos + 3) % 4, 0], self.right.at[0], 3, self.before)

    def middle(self):
        pos, src = self.pos, self.src
        for index, (via, goal, dst, device) in enumerate(
            (
                (self.via_left, (pos + 1) % 4, self.left, self.after),
                (self.via_right, (pos + 3) % 4, self.right, self.before),
            )
        ):
            self.copies[index].wait_recv()
            total = via[...].astype(jnp.float32) + src[goal, index].astype(jnp.float32)
            self.stage[index] = total.astype(self.stage.dtype)
            self.copy(self.stage.at[index], dst.at[index], 4 + index, device)

    def end(self, half):
        for index in ((3, 4), (2, 5))[half]:
            self.copies[index].wait_recv()
        return (
            self.src[self.pos, half].astype(jnp.float32)
            + self.left[half].astype(jnp.float32)
            + self.right[half].astype(jnp.float32)
        )

    def drain(self):
        for made in self.copies:
            made.wait_send()


def ring_buffers(rows, columns):
    return [
        pltpu.VMEM((2, rows, columns), jnp.bfloat16),
        pltpu.VMEM((2, rows, columns), jnp.bfloat16),
        pltpu.VMEM((rows, columns), jnp.bfloat16),
        pltpu.VMEM((rows, columns), jnp.bfloat16),
        pltpu.VMEM((2, rows, columns), jnp.bfloat16),
    ]


def weight_kernel(at, up, fin, *refs):
    at_in, up_in, first_a, first_b, second_a, second_b, pair, pair_in, tall, tall_in = refs[:10]
    rings = [refs[10 + 5 * i : 15 + 5 * i] for i in range(4)]
    ring_send, ring_recv, send, recv = refs[30:]
    z_lo, y, core, z_hi, x = place()
    partner = at_place(z_lo, y, 1 - core, z_hi, x)
    y_after, y_before = (at_place(z_lo, (y + s) % 4, core, z_hi, x) for s in (1, 3))
    x_peers = [at_place(z_lo, y, core, z_hi, (x + s) % 4) for s in (1, 2, 3)]
    low_peer = at_place(1 - z_lo, y, core, z_hi, x)
    high_peers = [at_place(z_lo, y, core, (z_hi + s) % 4, x) for s in (1, 2, 3)]
    peers = [partner, y_after, y_before, *x_peers, low_peer, *high_peers]
    barrier = pltpu.get_barrier_semaphore()
    for peer in peers:
        pl.semaphore_signal(barrier, inc=1, device_id=peer, device_id_type=pl.DeviceIdType.MESH)
    pl.semaphore_wait(barrier, len(peers))

    def copy(src, dst, index, device):
        made = pltpu.make_async_remote_copy(
            src_ref=src,
            dst_ref=dst,
            send_sem=send.at[index],
            recv_sem=recv.at[index],
            device_id=device,
            device_id_type=pl.DeviceIdType.MESH,
        )
        made.start()
        return made

    others = [copy(at.at[1 - core], at_in, 0, partner), copy(up, up_in, 1, partner)]
    for made in others:
        made.wait_recv()

    def product(part, start, width):
        mine = jnp.dot(at[core, part], up[:, start : start + width], preferred_element_type=jnp.float32)
        theirs = jnp.dot(at_in[part], up_in[:, start : start + width], preferred_element_type=jnp.float32)
        return (mine + theirs).astype(jnp.bfloat16)

    ring_a = Ring(first_a, y, y_after, y_before, rings[0], ring_send.at[0], ring_recv.at[0])
    ring_b = Ring(first_b, x, x_peers[0], x_peers[2], rings[1], ring_send.at[1], ring_recv.at[1])
    for half in range(2):
        block = product(0, half * 768, 768)
        for goal in range(4):
            first_a[goal, half] = block[goal * 96 : goal * 96 + 96]
    ring_a.start()
    for goal in range(4):
        block = product(1, goal * 384, 384)
        for half in range(2):
            first_b[goal, half] = block[half * 192 : half * 192 + 192]
    ring_b.start()
    ring_a.middle()
    ring_b.middle()
    ring_c = Ring(second_a, x, x_peers[0], x_peers[2], rings[2], ring_send.at[2], ring_recv.at[2])
    ring_d = Ring(second_b, y, y_after, y_before, rings[3], ring_send.at[3], ring_recv.at[3])
    for half in range(2):
        block = ring_a.end(half).astype(jnp.bfloat16)
        for goal in range(2):
            for row in range(2):
                second_a[half * 2 + goal, row] = block[row * 48 : row * 48 + 48, goal * 384 : goal * 384 + 384]
    ring_c.start()
    for half in range(2):
        block = ring_b.end(half).astype(jnp.bfloat16)
        for goal in range(2):
            for row in range(2):
                begin = goal * 96 + row * 48
                second_b[half * 2 + goal, row] = block[begin : begin + 48]
    ring_d.start()
    ring_c.middle()
    ring_d.middle()
    for part, ring in enumerate((ring_c, ring_d)):
        for row in range(2):
            pair[part, row * 48 : row * 48 + 48] = ring.end(row).astype(jnp.bfloat16)
    low = copy(pair.at[1 - z_lo], pair_in, 2, low_peer)
    low.wait_recv()
    total = pair[z_lo].astype(jnp.float32) + pair_in[...].astype(jnp.float32)
    tall[...] = total.astype(jnp.bfloat16)
    highs = [copy(tall, tall_in.at[i], 3 + i, high_peers[i]) for i in range(3)]
    for i in range(3):
        highs[i].wait_recv()
        total += tall_in[i].astype(jnp.float32)
    fin[x] = (total * 0.00390625).astype(jnp.bfloat16)
    lasts = [copy(fin.at[x], fin.at[x], 6 + i, x_peers[i]) for i in range(3)]
    for made in lasts:
        made.wait_recv()
    for made in (*others, low, *highs, *lasts):
        made.wait_send()
    for ring in (ring_a, ring_b, ring_c, ring_d):
        ring.drain()


def weight_sum(at, up):
    bf16 = jnp.bfloat16
    vmem = pl.BlockSpec(memory_space=pltpu.VMEM)
    return pl.pallas_call(
        weight_kernel,
        out_shape=jax.ShapeDtypeStruct((4, 96, 384), bf16),
        in_specs=[vmem, vmem],
        out_specs=vmem,
        scratch_shapes=[
            pltpu.VMEM((2, 384, 256), bf16),
            pltpu.VMEM((256, 1536), bf16),
            pltpu.VMEM((4, 2, 96, 768), bf16),
            pltpu.VMEM((4, 2, 192, 384), bf16),
            pltpu.VMEM((4, 2, 48, 384), bf16),
            pltpu.VMEM((4, 2, 48, 384), bf16),
            pltpu.VMEM((2, 96, 384), bf16),
            pltpu.VMEM((96, 384), bf16),
            pltpu.VMEM((96, 384), bf16),
            pltpu.VMEM((3, 96, 384), bf16),
            *ring_buffers(96, 768),
            *ring_buffers(192, 384),
            *ring_buffers(48, 384),
            *ring_buffers(48, 384),
            pltpu.SemaphoreType.DMA((4, 6)),
            pltpu.SemaphoreType.DMA((4, 6)),
            pltpu.SemaphoreType.DMA((9,)),
            pltpu.SemaphoreType.DMA((9,)),
        ],
        compiler_params=pltpu.CompilerParams(
            collective_id=1, has_side_effects=True, vmem_limit_bytes=40 * 1024 * 1024
        ),
    )(at, up)


def owned_slots(fin, bucket_owner, height_index):
    bucket_ids = jnp.arange(48, dtype=jnp.int32)
    same_owner = bucket_owner[None, :] == bucket_owner[:, None]
    ranking = jnp.sum((same_owner & (bucket_ids[None, :] < bucket_ids[:, None])).astype(jnp.int32), axis=1)
    slot = jnp.where(bucket_owner == height_index, ranking, -1)
    chosen = jnp.repeat(slot * 2, 2) + jnp.tile(jnp.arange(2, dtype=jnp.int32), 48)
    pick = (chosen[None, :] == jnp.arange(12, dtype=jnp.int32)[:, None]).astype(jnp.bfloat16)
    owned = jnp.einsum("sr,xrc->sxc", pick, fin, preferred_element_type=jnp.float32)
    return owned.reshape(6, 2, 1536)


def per_device(queries, keys_values, upstream, out_weight, windows, bucket_owner):
    frames, height_rows, columns, inner_width = queries.shape
    out_width = upstream.shape[3]
    height_index = lax.axis_index("ha")
    query_count = frames * height_rows * columns
    key_count = (frames + 2) * (height_rows + 2) * columns
    padded = with_halo(keys_values, (("ta", 1), ("ha", 2)), 1)
    upstream_flat = upstream.reshape(query_count, out_width)
    weight = lax.all_gather(out_weight, "ha", axis=0, tiled=True)
    grad_query, grads, at = attend(
        queries.reshape(query_count, inner_width),
        padded.reshape(2, key_count, inner_width),
        upstream_flat,
        weight,
        windows,
    )
    grads = grads.reshape(2, frames + 2, height_rows + 2, columns, inner_width)
    lifted = grads[:, 1:-1].at[:, 0].set(grads[:, 0]).at[:, frames - 1].set(grads[:, frames + 1])
    from_time = with_halo(lifted, (("ta", 1),), 1)
    lower_rim = from_time[:, 0]
    upper_rim = from_time[:, frames + 1]
    carried = jnp.zeros((2, frames, height_rows + 2, columns, inner_width), jnp.bfloat16)
    carried = carried.at[:, 0].set(lower_rim).at[:, frames - 1].set(upper_rim)
    packed = jnp.stack([grads[:, 1:-1], carried])
    outgoing = (
        packed[:, :, :, 1:-1]
        .at[:, :, :, 0]
        .set(packed[:, :, :, 0])
        .at[:, :, :, height_rows - 1]
        .set(packed[:, :, :, height_rows + 1])
    )
    from_height = with_halo(outgoing, (("ha", 3),), 1)
    summed = grads[:, 1:-1, 1:-1].astype(jnp.float32)
    summed = summed.at[:, 0].add(lower_rim[:, 1:-1].astype(jnp.float32))
    summed = summed.at[:, frames - 1].add(upper_rim[:, 1:-1].astype(jnp.float32))
    below = from_height[0, :, :, 0].astype(jnp.float32) + from_height[1, :, :, 0].astype(
        jnp.float32
    )
    above = from_height[0, :, :, height_rows + 1].astype(jnp.float32) + from_height[
        1, :, :, height_rows + 1
    ].astype(jnp.float32)
    summed = summed.at[:, :, 0].add(below).at[:, :, height_rows - 1].add(above)
    grad_pairs = summed.astype(jnp.bfloat16)
    at = at.reshape(2, 2, 384, 256)
    owned = owned_slots(weight_sum(at, upstream_flat), bucket_owner, height_index)
    return (
        grad_query.reshape(frames, height_rows, columns, inner_width),
        grad_pairs,
        owned,
    )


def solution(mesh):
    return jax.shard_map(
        per_device,
        mesh=mesh,
        in_specs=(
            P("ta", "ha", None, None),
            P(None, "ta", "ha", None, None),
            P("ta", "ha", None, None),
            P("ha", None),
            P(),
            P(),
        ),
        out_specs=(P("ta", "ha", None, None), P(None, "ta", "ha", None, None), P("ha", "ta", None)),
        check_vma=False,
    )
```

```python
import jax
import jax.numpy as jnp
from jax import lax
from jax.experimental import pallas as pl
from jax.experimental.pallas import tpu as pltpu
from jax.sharding import PartitionSpec as P

HEADS = 12
HEAD_DIM = 128
ACROSS = (((1,), (1,)), ((), ()))


def place():
    ta, ha = lax.axis_index("ta"), lax.axis_index("ha")
    return ta // 8, ta // 2 % 4, ta % 2, ha // 4, ha % 4


def at_place(z_lo, y, core, z_hi, x):
    return {"ta": z_lo * 8 + y * 2 + core, "ha": z_hi * 4 + x}


class Copies:
    def __init__(self, send, recv):
        self.send, self.recv, self.made = send, recv, []

    def start(self, src, dst, device):
        index = len(self.made)
        made = pltpu.make_async_remote_copy(
            src_ref=src,
            dst_ref=dst,
            send_sem=self.send.at[index],
            recv_sem=self.recv.at[index],
            device_id=device,
            device_id_type=pl.DeviceIdType.MESH,
        )
        made.start()
        self.made.append(made)
        return made

    def drain(self):
        for made in self.made:
            made.wait_send()


class RingSum:
    def __init__(self, copies, src, pos, after, before, bufs):
        self.copies, self.src, self.pos, self.after, self.before = copies, src, pos, after, before
        self.left, self.right, self.via_left, self.via_right, self.stage = bufs

    def start(self):
        pos, src, start = self.pos, self.src, self.copies.start
        far = (pos + 2) % 4
        self.first = [
            start(src.at[far, 0], self.via_left, self.after),
            start(src.at[far, 1], self.via_right, self.before),
        ]
        self.left_1 = start(src.at[(pos + 1) % 4, 1], self.left.at[1], self.after)
        self.right_0 = start(src.at[(pos + 3) % 4, 0], self.right.at[0], self.before)

    def middle(self):
        pos, src = self.pos, self.src
        made = []
        for index, (via, goal, dst, device) in enumerate(
            (
                (self.via_left, (pos + 1) % 4, self.left, self.after),
                (self.via_right, (pos + 3) % 4, self.right, self.before),
            )
        ):
            self.first[index].wait_recv()
            total = via[...].astype(jnp.float32) + src[goal, index].astype(jnp.float32)
            self.stage[index] = total.astype(self.stage.dtype)
            made.append(self.copies.start(self.stage.at[index], dst.at[index], device))
        self.left_0, self.right_1 = made

    def end(self, half):
        for made in ((self.right_0, self.left_0), (self.left_1, self.right_1))[half]:
            made.wait_recv()
        return (
            self.src[self.pos, half].astype(jnp.float32)
            + self.left[half].astype(jnp.float32)
            + self.right[half].astype(jnp.float32)
        )


def ring_buffers(rows, columns):
    return [
        pltpu.VMEM((2, rows, columns), jnp.bfloat16),
        pltpu.VMEM((2, rows, columns), jnp.bfloat16),
        pltpu.VMEM((rows, columns), jnp.bfloat16),
        pltpu.VMEM((rows, columns), jnp.bfloat16),
        pltpu.VMEM((2, rows, columns), jnp.bfloat16),
    ]


class RingGather:
    def __init__(self, copies, block, pos, after, before):
        self.copies, self.block, self.pos, self.after, self.before = copies, block, pos, after, before

    def start(self):
        own = self.block(self.pos, 0, 4)
        self.from_before = self.copies.start(own, own, self.after)
        self.from_after = self.copies.start(own, own, self.before)

    def middle(self):
        self.from_before.wait_recv()
        part = self.block((self.pos + 3) % 4, 0, 2)
        self.far_before = self.copies.start(part, part, self.after)
        self.from_after.wait_recv()
        part = self.block((self.pos + 1) % 4, 2, 2)
        self.far_after = self.copies.start(part, part, self.before)

    def end(self):
        self.far_before.wait_recv()
        self.far_after.wait_recv()


def window_bits(need):
    time_index, height_index = lax.axis_index("ta"), lax.axis_index("ha")
    key = lax.broadcasted_iota(jnp.int32, (96, 256), 0)
    token = lax.broadcasted_iota(jnp.int32, (96, 256), 1)
    row_gap = jnp.abs((token >> 4 & 3) - (key >> 4) + 1)
    tile_gap = jnp.abs((token >> 3 & 1) - (key >> 3 & 1))
    row = height_index * 4 + (key >> 4) - 1
    base = jnp.where((row_gap > 1) | (row < 0) | (row >= 64), 8, row_gap * 2 + tile_gap * 4)
    for f in range(6):
        time_gap = jnp.abs((token >> 6) - f + 1)
        frame = time_index * 4 + f - 1
        outside = (time_gap > 1) | (frame < 0) | (frame >= 64)
        need[f * 96 : f * 96 + 96] = base | jnp.where(outside, 8, time_gap)


def block_kernel(q, kv_in, up, weight_in, windows, dq, dkv_out, fin, *refs):
    f32, bf16 = jnp.float32, jnp.bfloat16
    kv, dkv, weight, probs_all, need, at, at_in, up_in = refs[:8]
    from_left, from_right, from_above, from_below = refs[8:12]
    first_a, first_b, second_a, second_b, pair_sums, pair_in, tall, tall_in = refs[12:20]
    rings = [refs[20 + 5 * i : 25 + 5 * i] for i in range(4)]
    send, recv, local_sem = refs[40:]
    z_lo, y, core, z_hi, x = place()
    ta, ha = lax.axis_index("ta"), lax.axis_index("ha")
    partner = at_place(z_lo, y, 1 - core, z_hi, x)
    y_after, y_before = (at_place(z_lo, (y + s) % 4, core, z_hi, x) for s in (1, 3))
    x_peers = [at_place(z_lo, y, core, z_hi, (x + s) % 4) for s in (1, 2, 3)]
    x_after, _, x_before = x_peers
    low_peer = at_place(1 - z_lo, y, core, z_hi, x)
    high_peers = [at_place(z_lo, y, core, (z_hi + s) % 4, x) for s in (1, 2, 3)]
    next_row, last_row = ({"ta": ta, "ha": (ha + s) % 16} for s in (1, 15))
    next_frame, last_frame = ({"ta": (ta + s) % 16, "ha": ha} for s in (1, 15))

    own_copy = pltpu.make_async_copy(kv_in, kv.at[:, pl.ds(1, 4), pl.ds(1, 4)], local_sem)
    own_copy.start()
    peers = [partner, y_after, y_before, *x_peers, low_peer, *high_peers]
    peers += [next_row, last_row, next_frame, last_frame]
    barrier = pltpu.get_barrier_semaphore()
    for peer in peers:
        pl.semaphore_signal(barrier, inc=1, device_id=peer, device_id_type=pl.DeviceIdType.MESH)
    window_bits(need)
    pl.semaphore_wait(barrier, len(peers))

    copies = Copies(send, recv)
    start = copies.start
    mine = pl.ds(1, 4)
    rows_in = [
        start(kv_in.at[:, :, 3], kv.at[:, mine, 0], next_row),
        start(kv_in.at[:, :, 0], kv.at[:, mine, 5], last_row),
    ]
    frames_in = [
        start(kv_in.at[:, 3], kv.at[:, 0, mine], next_frame),
        start(kv_in.at[:, 0], kv.at[:, 5, mine], last_frame),
    ]
    quarter = pl.ds(pl.multiple_of(y * 384, 384), 384)
    piece = weight_in.at[pl.ds(pl.multiple_of(core * 48, 16), 48), quarter]
    weight[z_hi, x, core, :, quarter] = weight_in[pl.ds(pl.multiple_of(core * 48, 16), 48), quarter]
    pieces_in = [start(piece, weight.at[z_hi, x, core, :, quarter], peer) for peer in high_peers]
    up_swap = start(up, up_in, partner)

    def over_x(p, begin, size):
        return weight.at[pl.ds(begin, size), p, core, :, quarter]

    def over_y(p, begin, size):
        return weight.at[pl.ds(begin, size), :, core, :, pl.ds(pl.multiple_of(p * 384, 384), 384)]

    gather_x = RingGather(copies, over_x, x, x_after, x_before)
    gather_y = RingGather(copies, over_y, y, y_after, y_before)
    for made in pieces_in:
        made.wait_recv()
    gather_x.start()
    for made in rows_in:
        made.wait_recv()
    corners_in = []
    for frame, goal, device in ((4, 0, next_frame), (1, 5, last_frame)):
        for row in (0, 5):
            corners_in.append(start(kv.at[:, frame, row], kv.at[:, goal, row], device))
    gather_x.middle()
    gather_x.end()
    gather_y.start()
    swaps = [start(over_y(y, 0, 4), over_y(y, 0, 4), partner)]
    own_copy.wait()
    for made in (*frames_in, *corners_in):
        made.wait_recv()

    out_row = lax.broadcasted_iota(jnp.int32, (128, 128), 0)
    feature = lax.broadcasted_iota(jnp.int32, (128, 128), 1)
    group = out_row >> 3
    turn = (group >> 2 & 1) * 8 + (group & 3) * 2 + (group >> 3)
    wanted = (out_row >> 1 & 3) * 32 + turn * 2 + (out_row & 1)
    order = (wanted == feature).astype(bf16)
    eye = (out_row == feature).astype(bf16)
    scaling = HEAD_DIM ** (-0.5)

    def forward(pair, carry):
        outs = []
        for side in range(2):
            head = pair * 2 + side
            cols = pl.ds(pl.multiple_of(head * 128, 128), 128)
            keys, values = (kv[i, :, :, :, cols].reshape(576, 128) for i in range(2))
            block = 15 - sum(((windows[head, a] - 1) // 2) << a for a in range(3))
            scores = lax.dot_general(keys, q[:, cols], ACROSS, preferred_element_type=f32)
            scores = jnp.where((need[...] & block) == 0, scores, -1e30)
            highest = jnp.max(scores, axis=0, keepdims=True)
            weights = jnp.exp2((scores - highest) * (scaling * 1.4426950408889634))
            probs = weights * (1.0 / jnp.sum(weights, axis=0, keepdims=True))
            probs_all[head] = probs
            values_t = lax.dot_general(order, values, ACROSS, preferred_element_type=f32).astype(bf16)
            out = jnp.dot(values_t, probs.astype(bf16), preferred_element_type=f32)
            outs.append(out.reshape(16, 8, 256))
        at[:, pl.ds(pl.multiple_of(pair * 16, 16), 16), :] = jnp.concatenate(outs, axis=1).astype(bf16)
        return carry

    def backward(pair, carry):
        begin = pl.multiple_of(pair * 256, 16)
        rows = weight_rows[pl.ds(begin, 256), :]
        grad_pair = lax.dot_general(up[...], rows, ACROSS, preferred_element_type=f32).astype(bf16)
        for side in range(2):
            head = pair * 2 + side
            cols = pl.ds(pl.multiple_of(head * 128, 128), 128)
            keys, values = (kv[i, :, :, :, cols].reshape(576, 128) for i in range(2))
            grad = grad_pair[:, side * 128 : side * 128 + 128]
            probs = probs_all[head]
            grad_probs = lax.dot_general(values, grad, ACROSS, preferred_element_type=f32)
            delta = jnp.sum(probs * grad_probs, axis=0, keepdims=True)
            grad_scores = (probs * (grad_probs - delta) * scaling).astype(bf16)
            keys_t = lax.dot_general(eye, keys, ACROSS, preferred_element_type=f32).astype(bf16)
            dq[:, cols] = jnp.dot(keys_t, grad_scores, preferred_element_type=f32).T.astype(bf16)
            grad_keys = jnp.dot(grad_scores, q[:, cols], preferred_element_type=f32).astype(bf16)
            grad_values = jnp.dot(probs.astype(bf16), grad, preferred_element_type=f32).astype(bf16)
            dkv[0, :, :, :, cols] = grad_keys.reshape(6, 6, 16, 128)
            dkv[1, :, :, :, cols] = grad_values.reshape(6, 6, 16, 128)
        return carry

    lax.fori_loop(0, 6, forward, 0)
    at_swap = start(at.at[pl.ds((1 - core) * 8, 8)], at_in, partner)
    gather_y.middle()
    for step in (3, 1):
        part = over_y((y + step) % 4, 0, 4)
        swaps.append(start(part, part, partner))
    up_swap.wait_recv()
    at_swap.wait_recv()

    def product(part, begin, width):
        a = at[pl.ds(core * 8 + part * 4, 4)].reshape(384, 256)
        b = at_in[part * 4 : part * 4 + 4].reshape(384, 256)
        total = jnp.dot(a, up[:, begin : begin + width], preferred_element_type=f32)
        total += jnp.dot(b, up_in[:, begin : begin + width], preferred_element_type=f32)
        return total.astype(bf16)

    ring_a = RingSum(copies, first_a, y, y_after, y_before, rings[0])
    ring_b = RingSum(copies, first_b, x, x_after, x_before, rings[1])
    ring_c = RingSum(copies, second_a, x, x_after, x_before, rings[2])
    ring_d = RingSum(copies, second_b, y, y_after, y_before, rings[3])
    for goal in range(4):
        block = product(1, goal * 384, 384)
        for half in range(2):
            first_b[goal, half] = block[half * 192 : half * 192 + 192]
    ring_b.start()
    for half in range(2):
        block = product(0, half * 768, 768)
        for goal in range(4):
            first_a[goal, half] = block[goal * 96 : goal * 96 + 96]
    ring_a.start()
    gather_y.end()
    part = over_y((y + 2) % 4, 0, 4)
    swaps.append(start(part, part, partner))
    for made in swaps:
        made.wait_recv()
    weight_rows = weight.reshape(1536, 1536)
    lax.fori_loop(0, 3, backward, 0)
    ring_b.middle()
    ring_a.middle()
    lax.fori_loop(3, 6, backward, 0)
    sides = [
        start(dkv.at[:, 5], from_left, next_frame),
        start(dkv.at[:, 0], from_right, last_frame),
    ]
    inner = pl.ds(1, 2)
    outer = [
        start(dkv.at[:, pl.ds(2, 2), 5], from_above.at[:, inner], next_row),
        start(dkv.at[:, pl.ds(2, 2), 0], from_below.at[:, inner], last_row),
    ]
    for half in range(2):
        block = ring_b.end(half).astype(bf16)
        for goal in range(2):
            for row in range(2):
                begin = goal * 96 + row * 48
                second_b[half * 2 + goal, row] = block[begin : begin + 48]
    ring_d.start()
    for half in range(2):
        block = ring_a.end(half).astype(bf16)
        for goal in range(2):
            for row in range(2):
                second_a[half * 2 + goal, row] = block[row * 48 : row * 48 + 48, goal * 384 : goal * 384 + 384]
    ring_c.start()
    for made, frame, came, first in ((sides[0], 1, from_left, 0), (sides[1], 4, from_right, 3)):
        made.wait_recv()
        for i in range(2):
            total = dkv[i, frame].astype(f32) + came[i].astype(f32)
            came[i] = total.astype(bf16)
        outer.append(start(came.at[:, 5], from_above.at[:, first], next_row))
        outer.append(start(came.at[:, 0], from_below.at[:, first], last_row))
    ring_d.middle()
    ring_c.middle()
    for part, ring in ((1, ring_d), (0, ring_c)):
        for row in range(2):
            pair_sums[part, row * 48 : row * 48 + 48] = ring.end(row).astype(bf16)
    low = start(pair_sums.at[1 - z_lo], pair_in, low_peer)
    low.wait_recv()
    total = pair_sums[z_lo].astype(f32) + pair_in[...].astype(f32)
    tall[...] = total.astype(bf16)
    highs = [start(tall, tall_in.at[i], high_peers[i]) for i in range(3)]
    for i in range(2):
        dkv_out[i, :, 1:3] = dkv[i, 1:5, 2:4]
        for f in (1, 2):
            for r in (0, 3):
                dkv_out[i, f, r] = dkv[i, f + 1, r + 1]
        for f, came in ((0, from_left), (3, from_right)):
            dkv_out[i, f] = came[i, 1:5]
    for made in outer:
        made.wait_recv()
    for i in range(2):
        for f in range(4):
            for r, came in ((0, from_above), (3, from_below)):
                dkv_out[i, f, r] = (dkv_out[i, f, r].astype(f32) + came[i, f].astype(f32)).astype(bf16)
    for i in range(3):
        highs[i].wait_recv()
        total += tall_in[i].astype(f32)
    fin[x] = (total * 0.00390625).astype(bf16)
    lasts = [start(fin.at[x], fin.at[x], peer) for peer in x_peers]
    for made in lasts:
        made.wait_recv()
    copies.drain()


def run_block(q, kv, up, weight, windows):
    bf16 = jnp.bfloat16
    vmem = pl.BlockSpec(memory_space=pltpu.VMEM)
    return pl.pallas_call(
        block_kernel,
        out_shape=[
            jax.ShapeDtypeStruct((256, 1536), bf16),
            jax.ShapeDtypeStruct((2, 4, 4, 16, 1536), bf16),
            jax.ShapeDtypeStruct((4, 96, 384), bf16),
        ],
        in_specs=[vmem, pl.BlockSpec(memory_space=pl.ANY), vmem, vmem, pl.BlockSpec(memory_space=pltpu.SMEM)],
        out_specs=[vmem, vmem, vmem],
        scratch_shapes=[
            pltpu.VMEM((2, 6, 6, 16, 1536), bf16),
            pltpu.VMEM((2, 6, 6, 16, 1536), bf16),
            pltpu.VMEM((4, 4, 2, 48, 1536), bf16),
            pltpu.VMEM((12, 576, 256), jnp.float32),
            pltpu.VMEM((576, 256), jnp.int32),
            pltpu.VMEM((16, 96, 256), bf16),
            pltpu.VMEM((8, 96, 256), bf16),
            pltpu.VMEM((256, 1536), bf16),
            pltpu.VMEM((2, 6, 16, 1536), bf16),
            pltpu.VMEM((2, 6, 16, 1536), bf16),
            pltpu.VMEM((2, 4, 16, 1536), bf16),
            pltpu.VMEM((2, 4, 16, 1536), bf16),
            pltpu.VMEM((4, 2, 96, 768), bf16),
            pltpu.VMEM((4, 2, 192, 384), bf16),
            pltpu.VMEM((4, 2, 48, 384), bf16),
            pltpu.VMEM((4, 2, 48, 384), bf16),
            pltpu.VMEM((2, 96, 384), bf16),
            pltpu.VMEM((96, 384), bf16),
            pltpu.VMEM((96, 384), bf16),
            pltpu.VMEM((3, 96, 384), bf16),
            *ring_buffers(96, 768),
            *ring_buffers(192, 384),
            *ring_buffers(48, 384),
            *ring_buffers(48, 384),
            pltpu.SemaphoreType.DMA((64,)),
            pltpu.SemaphoreType.DMA((64,)),
            pltpu.SemaphoreType.DMA,
        ],
        compiler_params=pltpu.CompilerParams(
            collective_id=1, has_side_effects=True, vmem_limit_bytes=56 * 1024 * 1024
        ),
    )(q, kv, up, weight, windows)


def owned_slots(fin, bucket_owner, height_index):
    bucket_ids = jnp.arange(48, dtype=jnp.int32)
    same_owner = bucket_owner[None, :] == bucket_owner[:, None]
    ranking = jnp.sum((same_owner & (bucket_ids[None, :] < bucket_ids[:, None])).astype(jnp.int32), axis=1)
    slot = jnp.where(bucket_owner == height_index, ranking, -1)
    chosen = jnp.repeat(slot * 2, 2) + jnp.tile(jnp.arange(2, dtype=jnp.int32), 48)
    pick = (chosen[None, :] == jnp.arange(12, dtype=jnp.int32)[:, None]).astype(jnp.bfloat16)
    owned = jnp.einsum("sr,xrc->sxc", pick, fin, preferred_element_type=jnp.float32)
    return owned.reshape(6, 2, 1536)


def per_device(queries, keys_values, upstream, out_weight, windows, bucket_owner):
    grad_query, grad_pairs, fin = run_block(
        queries.reshape(256, 1536), keys_values, upstream.reshape(256, 1536), out_weight, windows
    )
    owned = owned_slots(fin, bucket_owner, lax.axis_index("ha"))
    return grad_query.reshape(queries.shape), grad_pairs, owned


def solution(mesh):
    return jax.shard_map(
        per_device,
        mesh=mesh,
        in_specs=(
            P("ta", "ha", None, None),
            P(None, "ta", "ha", None, None),
            P("ta", "ha", None, None),
            P("ha", None),
            P(),
            P(),
        ),
        out_specs=(P("ta", "ha", None, None), P(None, "ta", "ha", None, None), P("ha", "ta", None)),
        check_vma=False,
    )
```

```python
import jax
import jax.numpy as jnp
from jax import lax
from jax.experimental import pallas as pl
from jax.experimental.pallas import tpu as pltpu
from jax.sharding import PartitionSpec as P

HEADS = 12
HEAD_DIM = 128
ACROSS = (((1,), (1,)), ((), ()))


def place():
    ta, ha = lax.axis_index("ta"), lax.axis_index("ha")
    return ta // 8, ta // 2 % 4, ta % 2, ha // 4, ha % 4


def at_place(z_lo, y, core, z_hi, x):
    return {"ta": z_lo * 8 + y * 2 + core, "ha": z_hi * 4 + x}


class Copies:
    def __init__(self, send, recv):
        self.send, self.recv, self.made = send, recv, []

    def make(self, src, dst, device, index):
        return pltpu.make_async_remote_copy(
            src_ref=src,
            dst_ref=dst,
            send_sem=self.send.at[index],
            recv_sem=self.recv.at[index],
            device_id=device,
            device_id_type=pl.DeviceIdType.MESH,
        )

    def reserve(self, src, dst, device):
        self.made.append(self.make(src, dst, device, len(self.made)))
        return self.made[-1]

    def start(self, src, dst, device):
        made = self.reserve(src, dst, device)
        made.start()
        return made

    def drain(self):
        for made in self.made:
            made.wait_send()


class RowSwap:
    def __init__(self, copies, relay_sems, spot, up, down, relay):
        self.x, next_row, last_row, x_after, x_before, high_after, high_before = spot
        self.relay = relay
        index = len(copies.made)
        self.up = copies.reserve(*up, next_row)
        self.down = copies.reserve(*down, last_row)
        self.waits = (self.up, self.down)
        if relay is None:
            self.up.start()
            self.down.start()
            return
        self.up_forward = copies.make(relay, up[1], x_after, index)
        self.down_forward = copies.make(relay, down[1], x_before, index + 1)
        self.up_relay, self.down_relay = (
            pltpu.make_async_remote_copy(
                src_ref=src,
                dst_ref=relay,
                send_sem=relay_sems.at[0],
                recv_sem=relay_sems.at[1],
                device_id=device,
                device_id_type=pl.DeviceIdType.MESH,
            )
            for src, device in ((up[0], high_after), (down[0], high_before))
        )
        for edge, direct, relayed in ((3, self.up, self.up_relay), (0, self.down, self.down_relay)):
            pl.when(self.x == edge)(relayed.start)
            pl.when(self.x != edge)(direct.start)

    def forward(self):
        for edge, relayed, onward in (
            (3, self.up_relay, self.up_forward),
            (0, self.down_relay, self.down_forward),
        ):

            @pl.when(self.x == edge)
            def _():
                relayed.wait_recv()
                onward.start()

    def wait(self):
        for made in self.waits:
            made.wait_recv()

    def drain(self):
        for edge, relayed in ((3, self.up_relay), (0, self.down_relay)):
            pl.when(self.x == edge)(relayed.wait_send)


class RingSum:
    def __init__(self, copies, src, pos, after, before, bufs):
        self.copies, self.src, self.pos, self.after, self.before = copies, src, pos, after, before
        self.left, self.right, self.via_left, self.via_right, self.stage = bufs

    def start(self):
        pos, src, start = self.pos, self.src, self.copies.start
        far = (pos + 2) % 4
        self.first = [
            start(src.at[far, 0], self.via_left, self.after),
            start(src.at[far, 1], self.via_right, self.before),
        ]
        self.left_1 = start(src.at[(pos + 1) % 4, 1], self.left.at[1], self.after)
        self.right_0 = start(src.at[(pos + 3) % 4, 0], self.right.at[0], self.before)

    def middle(self):
        pos, src = self.pos, self.src
        made = []
        for index, (via, goal, dst, device) in enumerate(
            (
                (self.via_left, (pos + 1) % 4, self.left, self.after),
                (self.via_right, (pos + 3) % 4, self.right, self.before),
            )
        ):
            self.first[index].wait_recv()
            total = via[...].astype(jnp.float32) + src[goal, index].astype(jnp.float32)
            self.stage[index] = total.astype(self.stage.dtype)
            made.append(self.copies.start(self.stage.at[index], dst.at[index], device))
        self.left_0, self.right_1 = made

    def end(self, half):
        for made in ((self.right_0, self.left_0), (self.left_1, self.right_1))[half]:
            made.wait_recv()
        return (
            self.src[self.pos, half].astype(jnp.float32)
            + self.left[half].astype(jnp.float32)
            + self.right[half].astype(jnp.float32)
        )


def ring_buffers(rows, columns):
    return [
        pltpu.VMEM((2, rows, columns), jnp.bfloat16),
        pltpu.VMEM((2, rows, columns), jnp.bfloat16),
        pltpu.VMEM((rows, columns), jnp.bfloat16),
        pltpu.VMEM((rows, columns), jnp.bfloat16),
        pltpu.VMEM((2, rows, columns), jnp.bfloat16),
    ]


class RingGather:
    def __init__(self, copies, block, pos, after, before):
        self.copies, self.block, self.pos, self.after, self.before = copies, block, pos, after, before

    def start(self):
        own = self.block(self.pos, 0, 4)
        self.from_before = self.copies.start(own, own, self.after)
        self.from_after = self.copies.start(own, own, self.before)

    def middle(self):
        self.from_before.wait_recv()
        part = self.block((self.pos + 3) % 4, 0, 2)
        self.far_before = self.copies.start(part, part, self.after)
        self.from_after.wait_recv()
        part = self.block((self.pos + 1) % 4, 2, 2)
        self.far_after = self.copies.start(part, part, self.before)

    def end(self):
        self.far_before.wait_recv()
        self.far_after.wait_recv()


def window_bits(need):
    time_index, height_index = lax.axis_index("ta"), lax.axis_index("ha")
    key = lax.broadcasted_iota(jnp.int32, (96, 256), 0)
    token = lax.broadcasted_iota(jnp.int32, (96, 256), 1)
    row_gap = jnp.abs((token >> 4 & 3) - (key >> 4) + 1)
    tile_gap = jnp.abs((token >> 3 & 1) - (key >> 3 & 1))
    row = height_index * 4 + (key >> 4) - 1
    base = jnp.where((row_gap > 1) | (row < 0) | (row >= 64), 8, row_gap * 2 + tile_gap * 4)
    for f in range(6):
        time_gap = jnp.abs((token >> 6) - f + 1)
        frame = time_index * 4 + f - 1
        outside = (time_gap > 1) | (frame < 0) | (frame >= 64)
        need[f * 96 : f * 96 + 96] = base | jnp.where(outside, 8, time_gap)


def block_kernel(q, kv_in, up, weight_in, windows, pick, dq, dkv_out, owned, *refs):
    f32, bf16 = jnp.float32, jnp.bfloat16
    kv, dkv, weight, probs_all, need, at, at_in, up_in = refs[:8]
    from_left, from_right, from_above, from_below = refs[8:12]
    first_a, first_b, second_a, second_b, pair_sums, pair_in, tall, tall_out, tall_in = refs[12:21]
    last_out, last_in, relay_kv, relay_grad = refs[21:25]
    rings = [refs[25 + 5 * i : 30 + 5 * i] for i in range(4)]
    send, recv, relay_sems, local_sem = refs[45:]
    z_lo, y, core, z_hi, x = place()
    ta, ha = lax.axis_index("ta"), lax.axis_index("ha")
    partner = at_place(z_lo, y, 1 - core, z_hi, x)
    y_after, y_before = (at_place(z_lo, (y + s) % 4, core, z_hi, x) for s in (1, 3))
    x_peers = [at_place(z_lo, y, core, z_hi, (x + s) % 4) for s in (1, 2, 3)]
    x_after, _, x_before = x_peers
    low_peer = at_place(1 - z_lo, y, core, z_hi, x)
    high_peers = [at_place(z_lo, y, core, (z_hi + s) % 4, x) for s in (1, 2, 3)]
    next_row, last_row = ({"ta": ta, "ha": (ha + s) % 16} for s in (1, 15))
    next_frame, last_frame = ({"ta": (ta + s) % 16, "ha": ha} for s in (1, 15))
    spot = (x, next_row, last_row, x_after, x_before, high_peers[0], high_peers[2])

    own_copy = pltpu.make_async_copy(kv_in, kv.at[:, pl.ds(1, 4), pl.ds(1, 4)], local_sem)
    own_copy.start()
    peers = [partner, y_after, y_before, *x_peers, low_peer, *high_peers]
    peers += [next_row, last_row, next_frame, last_frame]
    barrier = pltpu.get_barrier_semaphore()
    for peer in peers:
        pl.semaphore_signal(barrier, inc=1, device_id=peer, device_id_type=pl.DeviceIdType.MESH)
    window_bits(need)
    pl.semaphore_wait(barrier, len(peers))

    copies = Copies(send, recv)
    start = copies.start
    mine = pl.ds(1, 4)
    half_rows = pl.ds(pl.multiple_of(core * 48, 16), 48)
    shared = pl.ds(0, 1024)
    direct = pl.ds(1024, 512)

    def quarter(p):
        return pl.ds(pl.multiple_of(p * 256, 256), 256)

    pieces_in = []
    for cols in (quarter(y), direct):
        piece = weight_in.at[half_rows, cols]
        pieces_in.append([start(piece, weight.at[z_hi, x, core, :, cols], peer) for peer in high_peers])
    near, far = pl.ds(0, 896), pl.ds(896, 640)
    rows_in = [
        RowSwap(
            copies,
            relay_sems.at[i],
            spot,
            (kv_in.at[:, :, 3, :, cols], kv.at[:, mine, 0, :, cols]),
            (kv_in.at[:, :, 0, :, cols], kv.at[:, mine, 5, :, cols]),
            relay,
        )
        for i, (cols, relay) in enumerate(((far, relay_kv), (near, None)))
    ]
    frames_in = [
        start(kv_in.at[:, 3], kv.at[:, 0, mine], next_frame),
        start(kv_in.at[:, 0], kv.at[:, 5, mine], last_frame),
    ]
    up_swap = start(up, up_in, partner)
    weight[z_hi, x, core, :, quarter(y)] = weight_in[half_rows, quarter(y)]
    weight[z_hi, x, core, :, direct] = weight_in[half_rows, direct]

    def over_x(p, begin, size):
        return weight.at[pl.ds(begin, size), p, core, :, quarter(y)]

    def over_x_direct(p, begin, size):
        return weight.at[pl.ds(begin, size), p, core, :, direct]

    def over_y(p, begin, size):
        return weight.at[pl.ds(begin, size), :, core, :, quarter(p)]

    gather_x = RingGather(copies, over_x, x, x_after, x_before)
    gather_d = RingGather(copies, over_x_direct, x, x_after, x_before)
    gather_y = RingGather(copies, over_y, y, y_after, y_before)
    for made in pieces_in[0]:
        made.wait_recv()
    gather_x.start()
    for made in pieces_in[1]:
        made.wait_recv()
    gather_d.start()
    gather_x.middle()
    rows_in[0].forward()
    gather_x.end()
    gather_y.start()
    swaps = [start(over_y(y, 0, 4), over_y(y, 0, 4), partner)]
    for swap in rows_in:
        swap.wait()
    own_copy.wait()
    corners_in = []
    for frame, goal, device in ((4, 0, next_frame), (1, 5, last_frame)):
        for row in (0, 5):
            corners_in.append(start(kv.at[:, frame, row], kv.at[:, goal, row], device))
    gather_d.middle()
    for made in (*frames_in, *corners_in):
        made.wait_recv()

    out_row = lax.broadcasted_iota(jnp.int32, (128, 128), 0)
    feature = lax.broadcasted_iota(jnp.int32, (128, 128), 1)
    group = out_row >> 3
    turn = (group >> 2 & 1) * 8 + (group & 3) * 2 + (group >> 3)
    wanted = (out_row >> 1 & 3) * 32 + turn * 2 + (out_row & 1)
    order = (wanted == feature).astype(bf16)
    eye = (out_row == feature).astype(bf16)
    scaling = HEAD_DIM ** (-0.5)

    def forward(pair, carry):
        outs = []
        for side in range(2):
            head = pair * 2 + side
            cols = pl.ds(pl.multiple_of(head * 128, 128), 128)
            keys, values = (kv[i, :, :, :, cols].reshape(576, 128) for i in range(2))
            block = 15 - sum(((windows[head, a] - 1) // 2) << a for a in range(3))
            scores = lax.dot_general(keys, q[:, cols], ACROSS, preferred_element_type=f32)
            scores = jnp.where((need[...] & block) == 0, scores, -1e30)
            highest = jnp.max(scores, axis=0, keepdims=True)
            weights = jnp.exp2((scores - highest) * (scaling * 1.4426950408889634))
            probs = weights * (1.0 / jnp.sum(weights, axis=0, keepdims=True))
            probs_all[head] = probs
            values_t = lax.dot_general(order, values, ACROSS, preferred_element_type=f32).astype(bf16)
            out = jnp.dot(values_t, probs.astype(bf16), preferred_element_type=f32)
            outs.append(out.reshape(16, 8, 256))
        at[:, pl.ds(pl.multiple_of(pair * 16, 16), 16), :] = jnp.concatenate(outs, axis=1).astype(bf16)
        return carry

    def backward(pair, carry):
        begin = pl.multiple_of(pair * 256, 16)
        rows = weight_rows[pl.ds(begin, 256), :]
        grad_pair = lax.dot_general(up[...], rows, ACROSS, preferred_element_type=f32).astype(bf16)
        for side in range(2):
            head = pair * 2 + side
            cols = pl.ds(pl.multiple_of(head * 128, 128), 128)
            keys, values = (kv[i, :, :, :, cols].reshape(576, 128) for i in range(2))
            grad = grad_pair[:, side * 128 : side * 128 + 128]
            probs = probs_all[head]
            grad_probs = lax.dot_general(values, grad, ACROSS, preferred_element_type=f32)
            delta = jnp.sum(probs * grad_probs, axis=0, keepdims=True)
            grad_scores = (probs * (grad_probs - delta) * scaling).astype(bf16)
            keys_t = lax.dot_general(eye, keys, ACROSS, preferred_element_type=f32).astype(bf16)
            dq[:, cols] = jnp.dot(keys_t, grad_scores, preferred_element_type=f32).T.astype(bf16)
            grad_keys = jnp.dot(grad_scores, q[:, cols], preferred_element_type=f32).astype(bf16)
            grad_values = jnp.dot(probs.astype(bf16), grad, preferred_element_type=f32).astype(bf16)
            dkv[0, :, :, :, cols] = grad_keys.reshape(6, 6, 16, 128)
            dkv[1, :, :, :, cols] = grad_values.reshape(6, 6, 16, 128)
        return carry

    lax.fori_loop(0, 3, forward, 0)
    gather_y.middle()
    for step in (3, 1):
        part = over_y((y + step) % 4, 0, 4)
        swaps.append(start(part, part, partner))
    gather_d.end()
    part = weight.at[:, :, core, :, direct]
    swaps.append(start(part, part, partner))
    lax.fori_loop(3, 6, forward, 0)
    at_swap = start(at.at[pl.ds((1 - core) * 8, 8)], at_in, partner)
    gather_y.end()
    part = over_y((y + 2) % 4, 0, 4)
    swaps.append(start(part, part, partner))
    up_swap.wait_recv()
    at_swap.wait_recv()

    def product(part, begin, width):
        a = at[pl.ds(core * 8 + part * 4, 4)].reshape(384, 256)
        b = at_in[part * 4 : part * 4 + 4].reshape(384, 256)
        total = jnp.dot(a, up[:, begin : begin + width], preferred_element_type=f32)
        total += jnp.dot(b, up_in[:, begin : begin + width], preferred_element_type=f32)
        return total.astype(bf16)

    ring_a = RingSum(copies, first_a, y, y_after, y_before, rings[0])
    ring_b = RingSum(copies, first_b, x, x_after, x_before, rings[1])
    ring_c = RingSum(copies, second_a, x, x_after, x_before, rings[2])
    ring_d = RingSum(copies, second_b, y, y_after, y_before, rings[3])
    for goal in range(4):
        block = product(1, goal * 384, 384)
        for half in range(2):
            first_b[goal, half] = block[half * 192 : half * 192 + 192]
    ring_b.start()
    for half in range(2):
        block = product(0, half * 768, 768)
        for goal in range(4):
            first_a[goal, half] = block[goal * 96 : goal * 96 + 96]
    ring_a.start()
    for made in swaps:
        made.wait_recv()
    weight_rows = weight.reshape(1536, 1536)
    inner, outer = pl.ds(2, 2), pl.ds(1, 2)

    def frames_out(half):
        cols = pl.ds(half * 768, 768)
        sides = (
            start(dkv.at[:, 5, :, :, cols], from_left.at[:, :, :, cols], next_frame),
            start(dkv.at[:, 0, :, :, cols], from_right.at[:, :, :, cols], last_frame),
        )
        rows = RowSwap(
            copies,
            relay_sems.at[2 + half],
            spot,
            (dkv.at[:, inner, 5, :, cols], from_above.at[:, outer, :, cols]),
            (dkv.at[:, inner, 0, :, cols], from_below.at[:, outer, :, cols]),
            relay_grad.at[half],
        )
        return sides, rows

    def rows_out(half, sides):
        cols = pl.ds(half * 768, 768)
        made = []
        for side, frame, came, goal in ((sides[0], 1, from_left, 0), (sides[1], 4, from_right, 3)):
            side.wait_recv()
            total = dkv[:, frame, :, :, cols].astype(f32) + came[:, :, :, cols].astype(f32)
            came[:, :, :, cols] = total.astype(bf16)
            made.append(start(came.at[:, 5, :, cols], from_above.at[:, goal, :, cols], next_row))
            made.append(start(came.at[:, 0, :, cols], from_below.at[:, goal, :, cols], last_row))
        return made

    lax.fori_loop(0, 3, backward, 0)
    sides_0, inner_0 = frames_out(0)
    ring_b.middle()
    ring_a.middle()
    lax.fori_loop(3, 5, backward, 0)
    for half in range(2):
        block = ring_b.end(half).astype(bf16)
        for goal in range(2):
            for row in range(2):
                begin = goal * 96 + row * 48
                second_b[half * 2 + goal, row] = block[begin : begin + 48]
    ring_d.start()
    for half in range(2):
        block = ring_a.end(half).astype(bf16)
        for goal in range(2):
            for row in range(2):
                second_a[half * 2 + goal, row] = block[row * 48 : row * 48 + 48, goal * 384 : goal * 384 + 384]
    ring_c.start()
    lax.fori_loop(5, 6, backward, 0)
    sides_1, inner_1 = frames_out(1)
    outer_out = rows_out(0, sides_0)
    ring_d.middle()
    ring_c.middle()
    inner_0.forward()
    for part, ring in ((1, ring_d), (0, ring_c)):
        for row in range(2):
            pair_sums[part, row * 48 : row * 48 + 48] = ring.end(row).astype(bf16)
    low = start(pair_sums.at[1 - z_lo], pair_in, low_peer)
    outer_out += rows_out(1, sides_1)
    low.wait_recv()
    total = pair_sums[z_lo].astype(f32) + pair_in[...].astype(f32)
    tall[...] = total.astype(bf16)
    highs = []
    for i in range(3):
        chosen = pick[pl.ds(pl.multiple_of((z_hi + i + 1) % 4 * 48, 16), 48), :]
        tall_out[i] = jnp.dot(chosen, tall[...], preferred_element_type=f32).astype(bf16)
        highs.append(start(tall_out.at[i], tall_in.at[i], high_peers[i]))
    inner_1.forward()
    for i in range(2):
        dkv_out[i, :, 1:3] = dkv[i, 1:5, 2:4]
        for f, came in ((0, from_left), (3, from_right)):
            dkv_out[i, f, 1:3] = came[i, 2:4]
    chosen = pick[pl.ds(pl.multiple_of(z_hi * 48, 16), 48), :]
    total = jnp.dot(chosen, tall[...], preferred_element_type=f32)
    for i in range(3):
        highs[i].wait_recv()
        total += tall_in[i].astype(f32)
    total = total * 0.00390625
    for goal in range(4):
        last_out[goal, 0:12] = total[goal * 12 : goal * 12 + 12]
        last_out[goal, 12:16] = jnp.zeros((4, 384), f32)
    lasts = [start(last_out.at[(x + i + 1) % 4], last_in.at[x], x_peers[i]) for i in range(3)]
    last_in[x] = last_out[x]
    inner_0.wait()
    inner_1.wait()
    for made in outer_out:
        made.wait_recv()
    for i in range(2):
        for f, own in ((0, from_left), (1, None), (2, None), (3, from_right)):
            for r, came in ((0, from_above), (3, from_below)):
                base = dkv[i, f + 1, r + 1] if own is None else own[i, r + 1]
                dkv_out[i, f, r] = (base.astype(f32) + came[i, f].astype(f32)).astype(bf16)
    for made in lasts:
        made.wait_recv()
    for goal in range(4):
        owned[:, goal * 384 : goal * 384 + 384] = last_in[goal, 0:12]
    copies.drain()
    for swap in (rows_in[0], inner_0, inner_1):
        swap.drain()


def run_block(q, kv, up, weight, windows, pick):
    bf16 = jnp.bfloat16
    vmem = pl.BlockSpec(memory_space=pltpu.VMEM)
    return pl.pallas_call(
        block_kernel,
        out_shape=[
            jax.ShapeDtypeStruct((256, 1536), bf16),
            jax.ShapeDtypeStruct((2, 4, 4, 16, 1536), bf16),
            jax.ShapeDtypeStruct((12, 1536), jnp.float32),
        ],
        in_specs=[vmem, pl.BlockSpec(memory_space=pl.ANY), vmem, vmem, pl.BlockSpec(memory_space=pltpu.SMEM), vmem],
        out_specs=[vmem, vmem, vmem],
        scratch_shapes=[
            pltpu.VMEM((2, 6, 6, 16, 1536), bf16),
            pltpu.VMEM((2, 6, 6, 16, 1536), bf16),
            pltpu.VMEM((4, 4, 2, 48, 1536), bf16),
            pltpu.VMEM((12, 576, 256), jnp.float32),
            pltpu.VMEM((576, 256), jnp.int32),
            pltpu.VMEM((16, 96, 256), bf16),
            pltpu.VMEM((8, 96, 256), bf16),
            pltpu.VMEM((256, 1536), bf16),
            pltpu.VMEM((2, 6, 16, 1536), bf16),
            pltpu.VMEM((2, 6, 16, 1536), bf16),
            pltpu.VMEM((2, 4, 16, 1536), bf16),
            pltpu.VMEM((2, 4, 16, 1536), bf16),
            pltpu.VMEM((4, 2, 96, 768), bf16),
            pltpu.VMEM((4, 2, 192, 384), bf16),
            pltpu.VMEM((4, 2, 48, 384), bf16),
            pltpu.VMEM((4, 2, 48, 384), bf16),
            pltpu.VMEM((2, 96, 384), bf16),
            pltpu.VMEM((96, 384), bf16),
            pltpu.VMEM((96, 384), bf16),
            pltpu.VMEM((3, 48, 384), bf16),
            pltpu.VMEM((3, 48, 384), bf16),
            pltpu.VMEM((4, 16, 384), jnp.float32),
            pltpu.VMEM((4, 16, 384), jnp.float32),
            pltpu.VMEM((2, 4, 16, 640), bf16),
            pltpu.VMEM((2, 2, 2, 16, 768), bf16),
            *ring_buffers(96, 768),
            *ring_buffers(192, 384),
            *ring_buffers(48, 384),
            *ring_buffers(48, 384),
            pltpu.SemaphoreType.DMA((90,)),
            pltpu.SemaphoreType.DMA((90,)),
            pltpu.SemaphoreType.DMA((4, 2)),
            pltpu.SemaphoreType.DMA,
        ],
        compiler_params=pltpu.CompilerParams(
            collective_id=1, has_side_effects=True, vmem_limit_bytes=56 * 1024 * 1024
        ),
    )(q, kv, up, weight, windows, pick)


def slot_picks(bucket_owner):
    bucket_ids = jnp.arange(48, dtype=jnp.int32)
    same_owner = bucket_owner[None, :] == bucket_owner[:, None]
    ranking = jnp.sum((same_owner & (bucket_ids[None, :] < bucket_ids[:, None])).astype(jnp.int32), axis=1)
    slot = bucket_owner * 6 + ranking
    chosen = jnp.repeat(slot * 2, 2) + jnp.tile(jnp.arange(2, dtype=jnp.int32), 48)
    return (chosen[None, :] == jnp.arange(192, dtype=jnp.int32)[:, None]).astype(jnp.bfloat16)


def per_device(queries, keys_values, upstream, out_weight, windows, bucket_owner):
    grad_query, grad_pairs, owned = run_block(
        queries.reshape(256, 1536),
        keys_values,
        upstream.reshape(256, 1536),
        out_weight,
        windows,
        slot_picks(bucket_owner),
    )
    return grad_query.reshape(queries.shape), grad_pairs, owned.reshape(6, 2, 1536)


def solution(mesh):
    return jax.shard_map(
        per_device,
        mesh=mesh,
        in_specs=(
            P("ta", "ha", None, None),
            P(None, "ta", "ha", None, None),
            P("ta", "ha", None, None),
            P("ha", None),
            P(),
            P(),
        ),
        out_specs=(P("ta", "ha", None, None), P(None, "ta", "ha", None, None), P("ha", "ta", None)),
        check_vma=False,
    )
```

```python
import jax
import jax.numpy as jnp
from jax import lax
from jax.experimental import pallas as pl
from jax.experimental.pallas import tpu as pltpu
from jax.sharding import PartitionSpec as P

HEADS = 12
HEAD_DIM = 128
ACROSS = (((1,), (1,)), ((), ()))


def place():
    ta, ha = lax.axis_index("ta"), lax.axis_index("ha")
    return ta // 8, ta // 2 % 4, ta % 2, ha // 4, ha % 4


def at_place(z_lo, y, core, z_hi, x):
    return {"ta": z_lo * 8 + y * 2 + core, "ha": z_hi * 4 + x}


class Copies:
    def __init__(self, send, recv):
        self.send, self.recv, self.made, self.count = send, recv, [], 0

    def make(self, src, dst, device, send=None, recv=None):
        self.count += recv is None
        return pltpu.make_async_remote_copy(
            src_ref=src,
            dst_ref=dst,
            send_sem=self.send.at[self.count - 1] if send is None else send,
            recv_sem=self.recv.at[self.count - 1] if recv is None else recv,
            device_id=device,
            device_id_type=pl.DeviceIdType.MESH,
        )

    def start(self, src, dst, device):
        made = self.make(src, dst, device)
        made.start()
        self.made.append(made)
        return made

    def drain(self):
        for made in self.made:
            made.wait_send()


class RowSwap:
    def __init__(self, copies, relay_sems, spot, up, down, relay):
        self.x, next_row, last_row, x_after, x_before, high_after, high_before = spot
        self.relayed = relay is not None
        if not self.relayed:
            self.up, self.down = copies.start(*up, next_row), copies.start(*down, last_row)
            return
        self.up, self.down = copies.make(*up, next_row), copies.make(*down, last_row)
        out, back, onward = (relay_sems.at[i] for i in range(3))
        recv = copies.count - 2
        self.up_relay = copies.make(up[0], relay, x_after, out, back)
        self.down_relay = copies.make(down[0], relay, x_before, out, back)
        self.up_forward = copies.make(relay, up[1], high_after, onward, copies.recv.at[recv])
        self.down_forward = copies.make(relay, down[1], high_before, onward, copies.recv.at[recv + 1])
        for edge, direct, relayed in ((3, self.up, self.up_relay), (0, self.down, self.down_relay)):
            pl.when(self.x == edge)(relayed.start)
            pl.when(self.x != edge)(direct.start)

    def forward(self):
        for edge, relayed, onward in (
            (0, self.up_relay, self.up_forward),
            (3, self.down_relay, self.down_forward),
        ):

            @pl.when(self.x == edge)
            def _():
                relayed.wait_recv()
                onward.start()

    def wait(self):
        self.up.wait_recv()
        self.down.wait_recv()

    def drain(self):
        pl.when(self.x != 3)(self.up.wait_send)
        pl.when(self.x != 0)(self.down.wait_send)
        for edge, made in (
            (3, self.up_relay),
            (0, self.down_relay),
            (0, self.up_forward),
            (3, self.down_forward),
        ):
            pl.when(self.x == edge)(made.wait_send)


class RingSum:
    def __init__(self, copies, src, pos, after, before, bufs):
        self.copies, self.src, self.pos, self.after, self.before = copies, src, pos, after, before
        self.left, self.right, self.via_left, self.via_right, self.stage = bufs

    def start(self):
        pos, src, start = self.pos, self.src, self.copies.start
        far = (pos + 2) % 4
        self.first = [
            start(src.at[far, 0], self.via_left, self.after),
            start(src.at[far, 1], self.via_right, self.before),
        ]
        self.left_1 = start(src.at[(pos + 1) % 4, 1], self.left.at[1], self.after)
        self.right_0 = start(src.at[(pos + 3) % 4, 0], self.right.at[0], self.before)

    def middle(self):
        pos, src = self.pos, self.src
        made = []
        for index, (via, goal, dst, device) in enumerate(
            (
                (self.via_left, (pos + 1) % 4, self.left, self.after),
                (self.via_right, (pos + 3) % 4, self.right, self.before),
            )
        ):
            self.first[index].wait_recv()
            total = via[...].astype(jnp.float32) + src[goal, index].astype(jnp.float32)
            self.stage[index] = total.astype(self.stage.dtype)
            made.append(self.copies.start(self.stage.at[index], dst.at[index], device))
        self.left_0, self.right_1 = made

    def end(self, half):
        for made in ((self.right_0, self.left_0), (self.left_1, self.right_1))[half]:
            made.wait_recv()
        return (
            self.src[self.pos, half].astype(jnp.float32)
            + self.left[half].astype(jnp.float32)
            + self.right[half].astype(jnp.float32)
        )


def ring_buffers(rows, columns):
    return [
        pltpu.VMEM((2, rows, columns), jnp.bfloat16),
        pltpu.VMEM((2, rows, columns), jnp.bfloat16),
        pltpu.VMEM((rows, columns), jnp.bfloat16),
        pltpu.VMEM((rows, columns), jnp.bfloat16),
        pltpu.VMEM((2, rows, columns), jnp.bfloat16),
    ]


class RingGather:
    def __init__(self, copies, block, pos, after, before):
        self.copies, self.block, self.pos, self.after, self.before = copies, block, pos, after, before

    def start(self):
        own = self.block(self.pos, 0, 4)
        self.from_before = self.copies.start(own, own, self.after)
        self.from_after = self.copies.start(own, own, self.before)

    def middle(self):
        self.from_before.wait_recv()
        part = self.block((self.pos + 3) % 4, 0, 2)
        self.far_before = self.copies.start(part, part, self.after)
        self.from_after.wait_recv()
        part = self.block((self.pos + 1) % 4, 2, 2)
        self.far_after = self.copies.start(part, part, self.before)

    def end(self):
        self.far_before.wait_recv()
        self.far_after.wait_recv()


def window_bits(need):
    time_index, height_index = lax.axis_index("ta"), lax.axis_index("ha")
    key = lax.broadcasted_iota(jnp.int32, (96, 256), 0)
    token = lax.broadcasted_iota(jnp.int32, (96, 256), 1)
    row_gap = jnp.abs((token >> 4 & 3) - (key >> 4) + 1)
    tile_gap = jnp.abs((token >> 3 & 1) - (key >> 3 & 1))
    row = height_index * 4 + (key >> 4) - 1
    base = jnp.where((row_gap > 1) | (row < 0) | (row >= 64), 8, row_gap * 2 + tile_gap * 4)
    for f in range(6):
        time_gap = jnp.abs((token >> 6) - f + 1)
        frame = time_index * 4 + f - 1
        outside = (time_gap > 1) | (frame < 0) | (frame >= 64)
        need[f * 96 : f * 96 + 96] = base | jnp.where(outside, 8, time_gap)


def window_blocks(windows, blocks):
    axis = lax.broadcasted_iota(jnp.int32, (3, HEADS), 0)
    bits = jnp.sum(jnp.where(windows[...] > 1, 1 << axis, 0), axis=0, keepdims=True)
    row = lax.broadcasted_iota(jnp.int32, (HEADS, HEADS), 0)
    lane = lax.broadcasted_iota(jnp.int32, (HEADS, HEADS), 1)
    down = jnp.sum(jnp.where(row == lane, bits, 0), axis=1, keepdims=True)
    blocks[...] = jnp.broadcast_to(15 - down, (HEADS, 256))


def slot_picks(bucket_owner, pick):
    owners = bucket_owner[...].reshape(1, 48)
    row = lax.broadcasted_iota(jnp.int32, (48, 48), 0)
    lane = lax.broadcasted_iota(jnp.int32, (48, 48), 1)
    down = jnp.sum(jnp.where(row == lane, owners, 0), axis=1, keepdims=True)
    row = lax.broadcasted_iota(jnp.int32, (48, 96), 0)
    lane = lax.broadcasted_iota(jnp.int32, (48, 96), 1)
    along = jnp.sum(jnp.where(row == lane >> 1, down, 0), axis=0, keepdims=True)
    earlier = (down == along) & (row < lane >> 1)
    ranking = jnp.sum(jnp.where(earlier, 1, 0), axis=0, keepdims=True)
    chosen = along * 12 + ranking * 2 + (lane[0:1] & 1)
    row = lax.broadcasted_iota(jnp.int32, (192, 96), 0)
    pick[...] = jnp.where(row == chosen, 1.0, 0.0).astype(jnp.bfloat16)


def block_kernel(q_in, kv_in, up_hbm, weight_in, windows, bucket_owner, dq_out, dkv_hbm, owned, *refs):
    f32, bf16 = jnp.float32, jnp.bfloat16
    kv, dkv, weight, probs_all, need, at, at_in, up_in = refs[:8]
    from_left, from_right, from_above, from_below = refs[8:12]
    first_a, first_b, second_a, second_b, pair_sums, pair_in, tall, tall_out, tall_in = refs[12:21]
    last_out, last_in, relay_kv, relay_grad = refs[21:25]
    rings = [refs[25 + 5 * i : 30 + 5 * i] for i in range(4)]
    q, up, dq, dkv_out, pick, blocks = refs[45:51]
    send, recv, relay_sems, local_sem = refs[51:]
    z_lo, y, core, z_hi, x = place()
    ta, ha = lax.axis_index("ta"), lax.axis_index("ha")
    partner = at_place(z_lo, y, 1 - core, z_hi, x)
    y_after, y_before = (at_place(z_lo, (y + s) % 4, core, z_hi, x) for s in (1, 3))
    x_peers = [at_place(z_lo, y, core, z_hi, (x + s) % 4) for s in (1, 2, 3)]
    x_after, _, x_before = x_peers
    low_peer = at_place(1 - z_lo, y, core, z_hi, x)
    high_peers = [at_place(z_lo, y, core, (z_hi + s) % 4, x) for s in (1, 2, 3)]
    next_row, last_row = ({"ta": ta, "ha": (ha + s) % 16} for s in (1, 15))
    next_frame, last_frame = ({"ta": (ta + s) % 16, "ha": ha} for s in (1, 15))
    spot = (x, next_row, last_row, x_after, x_before, high_peers[0], high_peers[2])

    own_copies = [
        pltpu.make_async_copy(src, dst, local_sem.at[i])
        for i, (src, dst) in enumerate(((kv_in, kv.at[:, pl.ds(1, 4), pl.ds(1, 4)]), (q_in, q), (up_hbm, up)))
    ]
    half_rows = pl.ds(pl.multiple_of(core * 48, 16), 48)
    shared = pl.ds(pl.multiple_of(y * 256, 256), 256)
    direct = pl.ds(1024, 512)
    own_copies += [
        pltpu.make_async_copy(
            weight_in.at[half_rows, cols], weight.at[z_hi, x, core, :, cols], local_sem.at[3 + i]
        )
        for i, cols in enumerate((shared, direct))
    ]
    for made in own_copies:
        made.start()
    peers = [partner, y_after, y_before, *x_peers, low_peer, *high_peers]
    peers += [next_row, last_row, next_frame, last_frame]
    barrier = pltpu.get_barrier_semaphore()
    for peer in peers:
        pl.semaphore_signal(barrier, inc=1, device_id=peer, device_id_type=pl.DeviceIdType.MESH)
    window_bits(need)
    window_blocks(windows, blocks)
    slot_picks(bucket_owner, pick)
    pl.semaphore_wait(barrier, len(peers))

    copies = Copies(send, recv)
    start = copies.start
    mine = pl.ds(1, 4)

    def quarter(p):
        return pl.ds(pl.multiple_of(p * 256, 256), 256)

    def pieces(cols):
        piece = weight_in.at[half_rows, cols]
        return [start(piece, weight.at[z_hi, x, core, :, cols], peer) for peer in high_peers]

    def over_x(p, begin, size):
        return weight.at[pl.ds(begin, size), p, core, :, quarter(y)]

    def over_x_direct(p, begin, size):
        return weight.at[pl.ds(begin, size), p, core, :, direct]

    def over_y(p, begin, size):
        return weight.at[pl.ds(begin, size), :, core, :, quarter(p)]

    gather_x = RingGather(copies, over_x, x, x_after, x_before)
    gather_d = RingGather(copies, over_x_direct, x, x_after, x_before)
    gather_y = RingGather(copies, over_y, y, y_after, y_before)
    shared_in = pieces(shared)
    near, far = pl.ds(0, 896), pl.ds(896, 640)
    rows_in = [
        RowSwap(
            copies,
            relay_sems.at[i],
            spot,
            (kv_in.at[:, :, 3, :, cols], kv.at[:, mine, 0, :, cols]),
            (kv_in.at[:, :, 0, :, cols], kv.at[:, mine, 5, :, cols]),
            relay,
        )
        for i, (cols, relay) in enumerate(((far, relay_kv), (near, None)))
    ]
    frames_in = [
        start(kv_in.at[:, 3], kv.at[:, 0, mine], next_frame),
        start(kv_in.at[:, 0], kv.at[:, 5, mine], last_frame),
    ]
    up_swap = start(up_hbm, up_in, partner)
    for made in shared_in:
        made.wait_recv()
    own_copies[3].wait()
    gather_x.start()
    gather_x.middle()
    rows_in[0].forward()
    for swap in rows_in:
        swap.wait()
    for made in (*own_copies[:3], own_copies[4]):
        made.wait()
    corners_in = []
    for frame, goal, device in ((4, 0, next_frame), (1, 5, last_frame)):
        for row in (0, 5):
            corners_in.append(start(kv.at[:, frame, row], kv.at[:, goal, row], device))
    direct_in = pieces(direct)
    gather_x.end()
    gather_y.start()
    swaps = [start(over_y(y, 0, 4), over_y(y, 0, 4), partner)]
    for made in (*frames_in, *corners_in):
        made.wait_recv()

    out_row = lax.broadcasted_iota(jnp.int32, (128, 128), 0)
    feature = lax.broadcasted_iota(jnp.int32, (128, 128), 1)
    group = out_row >> 3
    turn = (group >> 2 & 1) * 8 + (group & 3) * 2 + (group >> 3)
    wanted = (out_row >> 1 & 3) * 32 + turn * 2 + (out_row & 1)
    order = (wanted == feature).astype(bf16)
    eye = (out_row == feature).astype(bf16)
    scaling = HEAD_DIM ** (-0.5)

    def forward(pair, carry):
        outs = []
        for side in range(2):
            head = pair * 2 + side
            cols = pl.ds(pl.multiple_of(head * 128, 128), 128)
            keys, values = (kv[i, :, :, :, cols].reshape(576, 128) for i in range(2))
            block = blocks[pl.ds(head, 1), :]
            scores = lax.dot_general(keys, q[:, cols], ACROSS, preferred_element_type=f32)
            scores = jnp.where((need[...] & block) == 0, scores, -1e30)
            highest = jnp.max(scores, axis=0, keepdims=True)
            weights = jnp.exp2((scores - highest) * (scaling * 1.4426950408889634))
            probs = weights * (1.0 / jnp.sum(weights, axis=0, keepdims=True))
            probs_all[head] = probs
            values_t = lax.dot_general(order, values, ACROSS, preferred_element_type=f32).astype(bf16)
            out = jnp.dot(values_t, probs.astype(bf16), preferred_element_type=f32)
            outs.append(out.reshape(16, 8, 256))
        at[:, pl.ds(pl.multiple_of(pair * 16, 16), 16), :] = jnp.concatenate(outs, axis=1).astype(bf16)
        return carry

    def backward(pair, carry):
        begin = pl.multiple_of(pair * 256, 16)
        rows = weight_rows[pl.ds(begin, 256), :]
        grad_pair = lax.dot_general(up[...], rows, ACROSS, preferred_element_type=f32).astype(bf16)
        for side in range(2):
            head = pair * 2 + side
            cols = pl.ds(pl.multiple_of(head * 128, 128), 128)
            keys, values = (kv[i, :, :, :, cols].reshape(576, 128) for i in range(2))
            grad = grad_pair[:, side * 128 : side * 128 + 128]
            probs = probs_all[head]
            grad_probs = lax.dot_general(values, grad, ACROSS, preferred_element_type=f32)
            delta = jnp.sum(probs * grad_probs, axis=0, keepdims=True)
            grad_scores = (probs * (grad_probs - delta) * scaling).astype(bf16)
            keys_t = lax.dot_general(eye, keys, ACROSS, preferred_element_type=f32).astype(bf16)
            dq[:, cols] = jnp.dot(keys_t, grad_scores, preferred_element_type=f32).T.astype(bf16)
            grad_keys = jnp.dot(grad_scores, q[:, cols], preferred_element_type=f32).astype(bf16)
            grad_values = jnp.dot(probs.astype(bf16), grad, preferred_element_type=f32).astype(bf16)
            dkv[0, :, :, :, cols] = grad_keys.reshape(6, 6, 16, 128)
            dkv[1, :, :, :, cols] = grad_values.reshape(6, 6, 16, 128)
        return carry

    for made in direct_in:
        made.wait_recv()
    gather_d.start()
    lax.fori_loop(0, 3, forward, 0)
    gather_y.middle()
    for step in (3, 1):
        part = over_y((y + step) % 4, 0, 4)
        swaps.append(start(part, part, partner))
    lax.fori_loop(3, 6, forward, 0)
    at_swap = start(at.at[pl.ds((1 - core) * 8, 8)], at_in, partner)
    gather_d.middle()
    up_swap.wait_recv()
    at_swap.wait_recv()

    def product(part, begin, width):
        a = at[pl.ds(core * 8 + part * 4, 4)].reshape(384, 256)
        b = at_in[part * 4 : part * 4 + 4].reshape(384, 256)
        total = jnp.dot(a, up[:, begin : begin + width], preferred_element_type=f32)
        total += jnp.dot(b, up_in[:, begin : begin + width], preferred_element_type=f32)
        return total.astype(bf16)

    ring_a = RingSum(copies, first_a, y, y_after, y_before, rings[0])
    ring_b = RingSum(copies, first_b, x, x_after, x_before, rings[1])
    ring_c = RingSum(copies, second_a, x, x_after, x_before, rings[2])
    ring_d = RingSum(copies, second_b, y, y_after, y_before, rings[3])
    for goal in range(4):
        block = product(1, goal * 384, 384)
        for half in range(2):
            first_b[goal, half] = block[half * 192 : half * 192 + 192]
    ring_b.start()
    for half in range(2):
        block = product(0, half * 768, 768)
        for goal in range(4):
            first_a[goal, half] = block[goal * 96 : goal * 96 + 96]
    ring_a.start()
    gather_d.end()
    part = weight.at[:, :, core, :, direct]
    swaps.append(start(part, part, partner))
    gather_y.end()
    part = over_y((y + 2) % 4, 0, 4)
    swaps.append(start(part, part, partner))
    for made in swaps:
        made.wait_recv()
    weight_rows = weight.reshape(1536, 1536)
    inner, outer = pl.ds(2, 2), pl.ds(1, 2)

    def frames_out(half):
        cols = pl.ds(half * 768, 768)
        sides = (
            start(dkv.at[:, 5, :, :, cols], from_left.at[:, :, :, cols], next_frame),
            start(dkv.at[:, 0, :, :, cols], from_right.at[:, :, :, cols], last_frame),
        )
        rows = RowSwap(
            copies,
            relay_sems.at[2 + half],
            spot,
            (dkv.at[:, inner, 5, :, cols], from_above.at[:, outer, :, cols]),
            (dkv.at[:, inner, 0, :, cols], from_below.at[:, outer, :, cols]),
            relay_grad.at[half],
        )
        return sides, rows

    def rows_out(half, sides):
        cols = pl.ds(half * 768, 768)
        made = []
        for side, frame, came, goal in ((sides[0], 1, from_left, 0), (sides[1], 4, from_right, 3)):
            side.wait_recv()
            total = dkv[:, frame, :, :, cols].astype(f32) + came[:, :, :, cols].astype(f32)
            came[:, :, :, cols] = total.astype(bf16)
            made.append(start(came.at[:, 5, :, cols], from_above.at[:, goal, :, cols], next_row))
            made.append(start(came.at[:, 0, :, cols], from_below.at[:, goal, :, cols], last_row))
        return made

    lax.fori_loop(0, 2, backward, 0)
    ring_b.middle()
    ring_a.middle()
    lax.fori_loop(2, 3, backward, 0)
    sides_0, inner_0 = frames_out(0)
    lax.fori_loop(3, 4, backward, 0)
    for half in range(2):
        block = ring_b.end(half).astype(bf16)
        for goal in range(2):
            for row in range(2):
                begin = goal * 96 + row * 48
                second_b[half * 2 + goal, row] = block[begin : begin + 48]
    ring_d.start()
    for half in range(2):
        block = ring_a.end(half).astype(bf16)
        for goal in range(2):
            for row in range(2):
                second_a[half * 2 + goal, row] = block[row * 48 : row * 48 + 48, goal * 384 : goal * 384 + 384]
    ring_c.start()
    lax.fori_loop(4, 5, backward, 0)
    outer_out = rows_out(0, sides_0)
    ring_d.middle()
    ring_c.middle()
    lax.fori_loop(5, 6, backward, 0)
    sides_1, inner_1 = frames_out(1)
    results = [pltpu.make_async_copy(dq, dq_out, local_sem.at[5])]
    results[0].start()
    for part, ring in ((1, ring_d), (0, ring_c)):
        for row in range(2):
            pair_sums[part, row * 48 : row * 48 + 48] = ring.end(row).astype(bf16)
    low = start(pair_sums.at[1 - z_lo], pair_in, low_peer)
    inner_0.forward()
    outer_out += rows_out(1, sides_1)
    low.wait_recv()
    total = pair_sums[z_lo].astype(f32) + pair_in[...].astype(f32)
    tall[...] = total.astype(bf16)
    highs = []
    for i in range(3):
        chosen = pick[pl.ds(pl.multiple_of((z_hi + i + 1) % 4 * 48, 16), 48), :]
        tall_out[i] = jnp.dot(chosen, tall[...], preferred_element_type=f32).astype(bf16)
        highs.append(start(tall_out.at[i], tall_in.at[i], high_peers[i]))
    inner_1.forward()
    for i in range(2):
        dkv_out[i, :, 1:3] = dkv[i, 1:5, 2:4]
        for f, came in ((0, from_left), (3, from_right)):
            dkv_out[i, f, 1:3] = came[i, 2:4]

    def result(index, rows):
        made = pltpu.make_async_copy(dkv_out.at[:, :, rows], dkv_hbm.at[:, :, rows], local_sem.at[index])
        made.start()
        results.append(made)

    result(6, pl.ds(1, 2))
    chosen = pick[pl.ds(pl.multiple_of(z_hi * 48, 16), 48), :]
    total = jnp.dot(chosen, tall[...], preferred_element_type=f32)
    for i in range(3):
        highs[i].wait_recv()
        total += tall_in[i].astype(f32)
    total = total * 0.00390625
    for goal in range(4):
        last_out[goal, 0:12] = total[goal * 12 : goal * 12 + 12]
        last_out[goal, 12:16] = jnp.zeros((4, 384), f32)
    lasts = [start(last_out.at[(x + i + 1) % 4], last_in.at[x], x_peers[i]) for i in range(3)]
    last_in[x] = last_out[x]
    inner_0.wait()
    inner_1.wait()
    for made in outer_out:
        made.wait_recv()
    for i in range(2):
        for f, own in ((0, from_left), (1, None), (2, None), (3, from_right)):
            for r, came in ((0, from_above), (3, from_below)):
                base = dkv[i, f + 1, r + 1] if own is None else own[i, r + 1]
                dkv_out[i, f, r] = (base.astype(f32) + came[i, f].astype(f32)).astype(bf16)
    result(7, pl.ds(0, 1))
    result(8, pl.ds(3, 1))
    for made in lasts:
        made.wait_recv()
    for goal in range(4):
        for slot in range(6):
            owned[slot, :, goal * 384 : goal * 384 + 384] = last_in[goal, slot * 2 : slot * 2 + 2]
    for made in results:
        made.wait()
    copies.drain()
    for swap in (rows_in[0], inner_0, inner_1):
        swap.drain()


def run_block(q, kv, up, weight, windows, bucket_owner):
    bf16 = jnp.bfloat16
    vmem = pl.BlockSpec(memory_space=pltpu.VMEM)
    anywhere = pl.BlockSpec(memory_space=pl.ANY)
    return pl.pallas_call(
        block_kernel,
        out_shape=[
            jax.ShapeDtypeStruct((256, 1536), bf16),
            jax.ShapeDtypeStruct((2, 4, 4, 16, 1536), bf16),
            jax.ShapeDtypeStruct((6, 2, 1536), jnp.float32),
        ],
        in_specs=[anywhere, anywhere, anywhere, anywhere, vmem, vmem],
        out_specs=[anywhere, anywhere, vmem],
        scratch_shapes=[
            pltpu.VMEM((2, 6, 6, 16, 1536), bf16),
            pltpu.VMEM((2, 6, 6, 16, 1536), bf16),
            pltpu.VMEM((4, 4, 2, 48, 1536), bf16),
            pltpu.VMEM((12, 576, 256), jnp.float32),
            pltpu.VMEM((576, 256), jnp.int32),
            pltpu.VMEM((16, 96, 256), bf16),
            pltpu.VMEM((8, 96, 256), bf16),
            pltpu.VMEM((256, 1536), bf16),
            pltpu.VMEM((2, 6, 16, 1536), bf16),
            pltpu.VMEM((2, 6, 16, 1536), bf16),
            pltpu.VMEM((2, 4, 16, 1536), bf16),
            pltpu.VMEM((2, 4, 16, 1536), bf16),
            pltpu.VMEM((4, 2, 96, 768), bf16),
            pltpu.VMEM((4, 2, 192, 384), bf16),
            pltpu.VMEM((4, 2, 48, 384), bf16),
            pltpu.VMEM((4, 2, 48, 384), bf16),
            pltpu.VMEM((2, 96, 384), bf16),
            pltpu.VMEM((96, 384), bf16),
            pltpu.VMEM((96, 384), bf16),
            pltpu.VMEM((3, 48, 384), bf16),
            pltpu.VMEM((3, 48, 384), bf16),
            pltpu.VMEM((4, 16, 384), jnp.float32),
            pltpu.VMEM((4, 16, 384), jnp.float32),
            pltpu.VMEM((2, 4, 16, 640), bf16),
            pltpu.VMEM((2, 2, 2, 16, 768), bf16),
            *ring_buffers(96, 768),
            *ring_buffers(192, 384),
            *ring_buffers(48, 384),
            *ring_buffers(48, 384),
            pltpu.VMEM((256, 1536), bf16),
            pltpu.VMEM((256, 1536), bf16),
            pltpu.VMEM((256, 1536), bf16),
            pltpu.VMEM((2, 4, 4, 16, 1536), bf16),
            pltpu.VMEM((192, 96), bf16),
            pltpu.VMEM((HEADS, 256), jnp.int32),
            pltpu.SemaphoreType.DMA((90,)),
            pltpu.SemaphoreType.DMA((90,)),
            pltpu.SemaphoreType.DMA((4, 3)),
            pltpu.SemaphoreType.DMA((9,)),
        ],
        compiler_params=pltpu.CompilerParams(
            collective_id=1, has_side_effects=True, vmem_limit_bytes=56 * 1024 * 1024
        ),
    )(q, kv, up, weight, windows, bucket_owner)


def per_device(queries, keys_values, upstream, out_weight, windows, bucket_owner):
    grad_query, grad_pairs, owned = run_block(
        queries.reshape(256, 1536),
        keys_values,
        upstream.reshape(256, 1536),
        out_weight,
        windows.T,
        bucket_owner,
    )
    return grad_query.reshape(queries.shape), grad_pairs, owned


def solution(mesh):
    return jax.shard_map(
        per_device,
        mesh=mesh,
        in_specs=(
            P("ta", "ha", None, None),
            P(None, "ta", "ha", None, None),
            P("ta", "ha", None, None),
            P("ha", None),
            P(),
            P(),
        ),
        out_specs=(P("ta", "ha", None, None), P(None, "ta", "ha", None, None), P("ha", "ta", None)),
        check_vma=False,
    )
```

```python
import jax
import jax.numpy as jnp
from jax import lax
from jax.experimental import pallas as pl
from jax.experimental.pallas import tpu as pltpu
from jax.sharding import PartitionSpec as P

HEADS = 12
HEAD_DIM = 128
NEAR, FAR = 896, 640
ACROSS = (((1,), (1,)), ((), ()))


def place():
    ta, ha = lax.axis_index("ta"), lax.axis_index("ha")
    return ta // 8, ta // 2 % 4, ta % 2, ha // 4, ha % 4


def at_place(z_lo, y, core, z_hi, x):
    return {"ta": z_lo * 8 + y * 2 + core, "ha": z_hi * 4 + x}


class Copies:
    def __init__(self, send, recv):
        self.send, self.recv, self.made, self.count = send, recv, [], 0

    def make(self, src, dst, device, send=None, recv=None):
        self.count += recv is None
        return pltpu.make_async_remote_copy(
            src_ref=src,
            dst_ref=dst,
            send_sem=self.send.at[self.count - 1] if send is None else send,
            recv_sem=self.recv.at[self.count - 1] if recv is None else recv,
            device_id=device,
            device_id_type=pl.DeviceIdType.MESH,
        )

    def start(self, src, dst, device):
        made = self.make(src, dst, device)
        made.start()
        self.made.append(made)
        return made

    def drain(self):
        for made in self.made:
            made.wait_send()


class RowSwap:
    def __init__(self, copies, relay_sems, spot, up, down, relay):
        self.x, next_row, last_row, x_after, x_before, high_after, high_before = spot
        self.relayed = relay is not None
        if not self.relayed:
            self.up, self.down = copies.start(*up, next_row), copies.start(*down, last_row)
            return
        self.up, self.down = copies.make(*up, next_row), copies.make(*down, last_row)
        out, back, onward = (relay_sems.at[i] for i in range(3))
        recv = copies.count - 2
        self.up_relay = copies.make(up[0], relay, x_after, out, back)
        self.down_relay = copies.make(down[0], relay, x_before, out, back)
        self.up_forward = copies.make(relay, up[1], high_after, onward, copies.recv.at[recv])
        self.down_forward = copies.make(relay, down[1], high_before, onward, copies.recv.at[recv + 1])
        for edge, direct, relayed in ((3, self.up, self.up_relay), (0, self.down, self.down_relay)):
            pl.when(self.x == edge)(relayed.start)
            pl.when(self.x != edge)(direct.start)

    def forward(self):
        for edge, relayed, onward in (
            (0, self.up_relay, self.up_forward),
            (3, self.down_relay, self.down_forward),
        ):

            @pl.when(self.x == edge)
            def _():
                relayed.wait_recv()
                onward.start()

    def wait(self):
        self.up.wait_recv()
        self.down.wait_recv()

    def drain(self):
        pl.when(self.x != 3)(self.up.wait_send)
        pl.when(self.x != 0)(self.down.wait_send)
        for edge, made in (
            (3, self.up_relay),
            (0, self.down_relay),
            (0, self.up_forward),
            (3, self.down_forward),
        ):
            pl.when(self.x == edge)(made.wait_send)


class RingSum:
    def __init__(self, copies, src, pos, after, before, bufs):
        self.copies, self.src, self.pos, self.after, self.before = copies, src, pos, after, before
        self.left, self.right, self.via_left, self.via_right, self.stage = bufs

    def start(self):
        pos, src, start = self.pos, self.src, self.copies.start
        far = (pos + 2) % 4
        self.first = [
            start(src.at[far, 0], self.via_left, self.after),
            start(src.at[far, 1], self.via_right, self.before),
        ]
        self.left_1 = start(src.at[(pos + 1) % 4, 1], self.left.at[1], self.after)
        self.right_0 = start(src.at[(pos + 3) % 4, 0], self.right.at[0], self.before)

    def middle(self):
        pos, src = self.pos, self.src
        made = []
        for index, (via, goal, dst, device) in enumerate(
            (
                (self.via_left, (pos + 1) % 4, self.left, self.after),
                (self.via_right, (pos + 3) % 4, self.right, self.before),
            )
        ):
            self.first[index].wait_recv()
            total = via[...].astype(jnp.float32) + src[goal, index].astype(jnp.float32)
            self.stage[index] = total.astype(self.stage.dtype)
            made.append(self.copies.start(self.stage.at[index], dst.at[index], device))
        self.left_0, self.right_1 = made

    def end(self, half):
        for made in ((self.right_0, self.left_0), (self.left_1, self.right_1))[half]:
            made.wait_recv()
        return (
            self.src[self.pos, half].astype(jnp.float32)
            + self.left[half].astype(jnp.float32)
            + self.right[half].astype(jnp.float32)
        )


class DirectSum:
    def __init__(self, copies, src, pos, peers, came):
        self.copies, self.src, self.pos, self.peers, self.came = copies, src, pos, peers, came

    def start(self):
        self.made = [
            self.copies.start(self.src.at[(self.pos + i + 1) % 4], self.came.at[i], self.peers[i])
            for i in range(3)
        ]

    def end(self):
        total = self.src[self.pos].astype(jnp.float32)
        for i in range(3):
            self.made[i].wait_recv()
            total += self.came[i].astype(jnp.float32)
        return total


def ring_buffers(rows, columns):
    return [
        pltpu.VMEM((2, rows, columns), jnp.bfloat16),
        pltpu.VMEM((2, rows, columns), jnp.bfloat16),
        pltpu.VMEM((rows, columns), jnp.bfloat16),
        pltpu.VMEM((rows, columns), jnp.bfloat16),
        pltpu.VMEM((2, rows, columns), jnp.bfloat16),
    ]


class RingGather:
    def __init__(self, copies, blocks, pos, after, before):
        self.copies, self.blocks, self.pos, self.after, self.before = copies, blocks, pos, after, before

    def send(self, step, begin, size, device):
        parts = self.blocks((self.pos + step) % 4, begin, size)
        return [self.copies.start(part, part, device) for part in parts]

    def start(self):
        self.from_before = self.send(0, 0, 4, self.after)
        self.from_after = self.send(0, 0, 4, self.before)

    def middle(self):
        for made in self.from_before:
            made.wait_recv()
        self.far = self.send(3, 0, 2, self.after)
        for made in self.from_after:
            made.wait_recv()
        self.far += self.send(1, 2, 2, self.before)

    def end(self):
        for made in self.far:
            made.wait_recv()


def window_bits(need):
    time_index, height_index = lax.axis_index("ta"), lax.axis_index("ha")
    key = lax.broadcasted_iota(jnp.int32, (96, 256), 0)
    token = lax.broadcasted_iota(jnp.int32, (96, 256), 1)
    row_gap = jnp.abs((token >> 4 & 3) - (key >> 4) + 1)
    tile_gap = jnp.abs((token >> 3 & 1) - (key >> 3 & 1))
    row = height_index * 4 + (key >> 4) - 1
    base = jnp.where((row_gap > 1) | (row < 0) | (row >= 64), 8, row_gap * 2 + tile_gap * 4)
    for f in range(6):
        time_gap = jnp.abs((token >> 6) - f + 1)
        frame = time_index * 4 + f - 1
        outside = (time_gap > 1) | (frame < 0) | (frame >= 64)
        need[f * 96 : f * 96 + 96] = base | jnp.where(outside, 8, time_gap)


def window_blocks(windows, blocks):
    axis = lax.broadcasted_iota(jnp.int32, (3, HEADS), 0)
    bits = jnp.sum(jnp.where(windows[...] > 1, 1 << axis, 0), axis=0, keepdims=True)
    row = lax.broadcasted_iota(jnp.int32, (HEADS, HEADS), 0)
    lane = lax.broadcasted_iota(jnp.int32, (HEADS, HEADS), 1)
    down = jnp.sum(jnp.where(row == lane, bits, 0), axis=1, keepdims=True)
    blocks[...] = jnp.broadcast_to(15 - down, (HEADS, 256))


def slot_picks(bucket_owner, pick):
    owners = bucket_owner[...].reshape(1, 48)
    row = lax.broadcasted_iota(jnp.int32, (48, 48), 0)
    lane = lax.broadcasted_iota(jnp.int32, (48, 48), 1)
    down = jnp.sum(jnp.where(row == lane, owners, 0), axis=1, keepdims=True)
    row = lax.broadcasted_iota(jnp.int32, (48, 96), 0)
    lane = lax.broadcasted_iota(jnp.int32, (48, 96), 1)
    along = jnp.sum(jnp.where(row == lane >> 1, down, 0), axis=0, keepdims=True)
    earlier = (down == along) & (row < lane >> 1)
    ranking = jnp.sum(jnp.where(earlier, 1, 0), axis=0, keepdims=True)
    chosen = along * 16 + ranking * 2 + (lane[0:1] & 1)
    row = lax.broadcasted_iota(jnp.int32, (256, 96), 0)
    pick[...] = jnp.where(row == chosen, 1.0, 0.0).astype(jnp.bfloat16)


def block_kernel(q_in, kv_in, up_hbm, weight_in, windows, bucket_owner, dq_out, dkv_hbm, owned, *refs):
    f32, bf16 = jnp.float32, jnp.bfloat16
    kv, dkv, weight, probs_all, need, at, at_in, up_in = refs[:8]
    from_left, from_right, from_above, from_below = refs[8:12]
    first_a, first_b, second_a, second_b, came_a, came_b, pair_sums, pair_in = refs[12:20]
    slots_out, slots_in, relay_kv, relay_grad = refs[20:24]
    rings = [refs[24 + 5 * i : 29 + 5 * i] for i in range(2)]
    q, up, dq, dkv_out, pick, blocks = refs[34:40]
    send, recv, relay_sems, local_sem = refs[40:]
    z_lo, y, core, z_hi, x = place()
    ta, ha = lax.axis_index("ta"), lax.axis_index("ha")
    partner = at_place(z_lo, y, 1 - core, z_hi, x)
    y_after, y_before = (at_place(z_lo, (y + s) % 4, core, z_hi, x) for s in (1, 3))
    x_peers = [at_place(z_lo, y, core, z_hi, (x + s) % 4) for s in (1, 2, 3)]
    x_after, _, x_before = x_peers
    low_peer = at_place(1 - z_lo, y, core, z_hi, x)
    high_peers = [at_place(z_lo, y, core, (z_hi + s) % 4, x) for s in (1, 2, 3)]
    next_row, last_row = ({"ta": ta, "ha": (ha + s) % 16} for s in (1, 15))
    next_frame, last_frame = ({"ta": (ta + s) % 16, "ha": ha} for s in (1, 15))
    spot = (x, next_row, last_row, x_after, x_before, high_peers[0], high_peers[2])

    own_copies = [
        pltpu.make_async_copy(src, dst, local_sem.at[i])
        for i, (src, dst) in enumerate(((kv_in, kv.at[:, pl.ds(1, 4), pl.ds(1, 4)]), (q_in, q), (up_hbm, up)))
    ]
    half_rows = pl.ds(pl.multiple_of(core * 48, 16), 48)
    tiles = [
        pl.multiple_of(jnp.where(z_hi % 2 == 0, even, odd) * 128, 128)
        for even, odd in ((y * 2, y), (y * 2 + 1, y * 2 + 4), (y + 8, y * 2 + 5))
    ]
    places = [(weight_in.at[half_rows, pl.ds(c, 128)], weight.at[z_hi // 2, z_hi % 2, x, core, :, pl.ds(c, 128)]) for c in tiles]
    weight_copies = [pltpu.make_async_copy(*place, local_sem.at[9 + i]) for i, place in enumerate(places)]
    for made in weight_copies:
        made.start()
    for made in own_copies:
        made.start()
    others = [{"ta": ta, "ha": (ha + s) % 16} for s in range(1, 16)]
    y_far = at_place(z_lo, (y + 2) % 4, core, z_hi, x)
    peers = [partner, y_after, y_far, y_before, low_peer, next_frame, last_frame, *others]
    barrier = pltpu.get_barrier_semaphore()
    for peer in peers:
        pl.semaphore_signal(barrier, inc=1, device_id=peer, device_id_type=pl.DeviceIdType.MESH)
    window_bits(need)
    window_blocks(windows, blocks)
    slot_picks(bucket_owner, pick)
    pl.semaphore_wait(barrier, len(peers))

    copies = Copies(send, recv)
    start = copies.start
    mine = pl.ds(1, 4)

    def share(p, first, width):
        return pl.ds(pl.multiple_of(first + p * width, 128), width)

    def over_x(p, begin, size):
        zs = pl.ds(begin // 2, size // 2)
        return (weight.at[zs, 0, p, core, :, share(y, 0, 256)], weight.at[zs, 1, p, core, :, share(y, 0, 128)])

    def over_y_direct(p, begin, size):
        zs = pl.ds(begin // 2, size // 2)
        return (weight.at[zs, 0, x, core, :, share(p, 1024, 128)], weight.at[zs, 1, x, core, :, share(p, 512, 256)])

    def over_y(group):
        def blocks(p, begin, size):
            xs = pl.ds(begin, size)
            return (
                weight.at[group, 0, xs, core, :, share(p, 0, 256)],
                weight.at[group, 1, xs, core, :, share(p, 0, 128)],
            )

        return blocks

    def over_x_direct(group):
        def blocks(p, begin, size):
            return (
                weight.at[group, 0, p, core, :, pl.ds(1024 + begin * 128, size * 128)],
                weight.at[group, 1, p, core, :, pl.ds(512 + begin * 256, size * 256)],
            )

        return blocks

    gather_x = RingGather(copies, over_x, x, x_after, x_before)
    gather_e = RingGather(copies, over_y_direct, y, y_after, y_before)
    gather_y = [RingGather(copies, over_y(g), y, y_after, y_before) for g in range(2)]
    gather_d = [RingGather(copies, over_x_direct(g), x, x_after, x_before) for g in range(2)]
    swaps = [[], []]

    def swap_parts(group, parts):
        swaps[group].extend(start(part, part, partner) for part in parts)

    def swap_y(group, *steps):
        for step in steps:
            swap_parts(group, gather_y[group].blocks((y + step) % 4, 0, 4))

    def swap_d(group):
        swap_parts(group, (weight.at[group, 0, :, core, :, pl.ds(1024, 512)], weight.at[group, 1, :, core, :, pl.ds(512, 1024)]))

    pieces = [start(src, dst, peer) for src, dst in places for peer in high_peers]
    near, far = pl.ds(0, NEAR), pl.ds(NEAR, FAR)
    rows_in = [
        RowSwap(
            copies,
            relay_sems.at[i],
            spot,
            (kv_in.at[part, :, 3, :, cols], kv.at[part, mine, 0, :, cols]),
            (kv_in.at[part, :, 0, :, cols], kv.at[part, mine, 5, :, cols]),
            relay,
        )
        for i, (part, cols, relay) in enumerate(
            ((0, far, relay_kv.at[0]), (1, far, relay_kv.at[1]), (pl.ds(0, 2), near, None))
        )
    ]
    frames_in = [
        start(kv_in.at[:, 3], kv.at[:, 0, mine], next_frame),
        start(kv_in.at[:, 0], kv.at[:, 5, mine], last_frame),
    ]
    up_swap = start(up_hbm, up_in, partner)
    for made in weight_copies:
        made.wait()
    for made in pieces:
        made.wait_recv()
    gather_x.start()
    gather_e.start()
    rows_in[0].forward()
    rows_in[1].forward()
    gather_e.middle()
    gather_x.middle()
    gather_e.end()
    for swap in rows_in:
        swap.wait()
    for made in own_copies:
        made.wait()
    corners_in = []
    for frame, goal, device in ((4, 0, next_frame), (1, 5, last_frame)):
        for row in (0, 5):
            corners_in.append(start(kv.at[:, frame, row], kv.at[:, goal, row], device))
    gather_d[0].start()
    gather_x.end()
    gather_y[0].start()
    swap_y(0, 0)
    swap_y(1, 0)
    for made in (*frames_in, *corners_in):
        made.wait_recv()

    out_row = lax.broadcasted_iota(jnp.int32, (128, 128), 0)
    feature = lax.broadcasted_iota(jnp.int32, (128, 128), 1)
    group = out_row >> 3
    turn = (group >> 2 & 1) * 8 + (group & 3) * 2 + (group >> 3)
    wanted = (out_row >> 1 & 3) * 32 + turn * 2 + (out_row & 1)
    order = (wanted == feature).astype(bf16)
    scaling = HEAD_DIM ** (-0.5)

    def forward(pair, carry):
        outs = []
        for side in range(2):
            head = pair * 2 + side
            cols = pl.ds(pl.multiple_of(head * 128, 128), 128)
            keys, values = (kv[i, :, :, :, cols].reshape(576, 128) for i in range(2))
            block = blocks[pl.ds(head, 1), :]
            scores = lax.dot_general(keys, q[:, cols], ACROSS, preferred_element_type=f32)
            scores = jnp.where((need[...] & block) == 0, scores, -1e30)
            highest = jnp.max(scores, axis=0, keepdims=True)
            weights = jnp.exp2((scores - highest) * (scaling * 1.4426950408889634))
            probs = weights * (1.0 / jnp.sum(weights, axis=0, keepdims=True))
            probs_all[head] = probs
            values_t = lax.dot_general(order, values, ACROSS, preferred_element_type=f32).astype(bf16)
            out = jnp.dot(values_t, probs.astype(bf16), preferred_element_type=f32)
            outs.append(out.reshape(16, 8, 256))
        at[:, pl.ds(pl.multiple_of(pair * 16, 16), 16), :] = jnp.concatenate(outs, axis=1).astype(bf16)
        return carry

    def backward(pair, carry):
        begin = pl.multiple_of(pair * 256, 16)
        rows = weight_rows[pl.ds(begin, 256), :]
        grad_pair = lax.dot_general(up[...], rows, ACROSS, preferred_element_type=f32).astype(bf16)
        for side in range(2):
            head = pair * 2 + side
            cols = pl.ds(pl.multiple_of(head * 128, 128), 128)
            keys, values = (kv[i, :, :, :, cols].reshape(576, 128) for i in range(2))
            grad = grad_pair[:, side * 128 : side * 128 + 128]
            probs = probs_all[head]
            grad_probs = lax.dot_general(values, grad, ACROSS, preferred_element_type=f32)
            delta = jnp.sum(probs * grad_probs, axis=0, keepdims=True)
            grad_scores = (probs * (grad_probs - delta) * scaling).astype(bf16)
            keys_t = keys.T
            dq[:, cols] = jnp.dot(keys_t, grad_scores, preferred_element_type=f32).T.astype(bf16)
            grad_keys = jnp.dot(grad_scores, q[:, cols], preferred_element_type=f32).astype(bf16)
            grad_values = jnp.dot(probs.astype(bf16), grad, preferred_element_type=f32).astype(bf16)
            dkv[0, :, :, :, cols] = grad_keys.reshape(6, 6, 16, 128)
            dkv[1, :, :, :, cols] = grad_values.reshape(6, 6, 16, 128)
        return carry

    at_swaps = []

    def swap_outputs(half):
        rows = pl.ds(half * 48, 48)
        at_swaps.append(start(at.at[pl.ds((1 - core) * 8, 8), rows], at_in.at[:, rows], partner))

    lax.fori_loop(0, 3, forward, 0)
    swap_outputs(0)
    gather_d[0].middle()
    gather_d[1].start()
    gather_y[0].middle()
    gather_y[1].start()
    swap_y(0, 3, 1)
    lax.fori_loop(3, 6, forward, 0)
    swap_outputs(1)
    gather_d[0].end()
    swap_d(0)
    gather_y[0].end()
    swap_y(0, 2)
    gather_d[1].middle()
    gather_y[1].middle()
    swap_y(1, 3, 1)
    up_swap.wait_recv()
    for made in at_swaps:
        made.wait_recv()

    def product(part, begin, width):
        a = at[pl.ds(core * 8 + part * 4, 4)].reshape(384, 256)
        b = at_in[part * 4 : part * 4 + 4].reshape(384, 256)
        total = jnp.dot(a, up[:, begin : begin + width], preferred_element_type=f32)
        total += jnp.dot(b, up_in[:, begin : begin + width], preferred_element_type=f32)
        return total.astype(bf16)

    ring_a = RingSum(copies, first_a, y, y_after, y_before, rings[0])
    ring_b = RingSum(copies, first_b, x, x_after, x_before, rings[1])
    sum_a = DirectSum(copies, second_a, x, x_peers, came_a)
    y_peers = [at_place(z_lo, (y + s) % 4, core, z_hi, x) for s in (1, 2, 3)]
    sum_b = DirectSum(copies, second_b, y, y_peers, came_b)
    for goal in range(4):
        block = product(1, goal * 384, 384)
        for half in range(2):
            first_b[goal, half] = block[half * 192 : half * 192 + 192]
    ring_b.start()
    for half in range(2):
        block = product(0, half * 768, 768)
        for goal in range(4):
            first_a[goal, half] = block[goal * 96 : goal * 96 + 96]
    ring_a.start()
    for made in swaps[0]:
        made.wait_recv()
    weight_rows = weight.reshape(1536, 1536)
    inner, outer = pl.ds(2, 2), pl.ds(1, 2)

    def frames_out(third):
        cols = pl.ds(third * 512, 512)
        sides = (
            start(dkv.at[:, 5, :, :, cols], from_left.at[:, :, :, cols], next_frame),
            start(dkv.at[:, 0, :, :, cols], from_right.at[:, :, :, cols], last_frame),
        )
        rows = RowSwap(
            copies,
            relay_sems.at[3 + third],
            spot,
            (dkv.at[:, inner, 5, :, cols], from_above.at[:, outer, :, cols]),
            (dkv.at[:, inner, 0, :, cols], from_below.at[:, outer, :, cols]),
            relay_grad.at[third],
        )
        return sides, rows

    def rows_out(third, sides):
        cols = pl.ds(third * 512, 512)
        made = []
        for side, frame, came, goal in ((sides[0], 1, from_left, 0), (sides[1], 4, from_right, 3)):
            side.wait_recv()
            total = dkv[:, frame, :, :, cols].astype(f32) + came[:, :, :, cols].astype(f32)
            came[:, :, :, cols] = total.astype(bf16)
            made.append(start(came.at[:, 5, :, cols], from_above.at[:, goal, :, cols], next_row))
            made.append(start(came.at[:, 0, :, cols], from_below.at[:, goal, :, cols], last_row))
        return made

    lax.fori_loop(0, 2, backward, 0)
    gather_d[1].end()
    swap_d(1)
    gather_y[1].end()
    swap_y(1, 2)
    sides_0, inner_0 = frames_out(0)
    lax.fori_loop(2, 3, backward, 0)
    for made in swaps[1]:
        made.wait_recv()
    lax.fori_loop(3, 4, backward, 0)
    ring_b.middle()
    ring_a.middle()
    sides_1, inner_1 = frames_out(1)
    outer_out = rows_out(0, sides_0)
    inner_0.forward()
    lax.fori_loop(4, 5, backward, 0)
    for half in range(2):
        block = ring_b.end(half).astype(bf16)
        for goal in range(2):
            second_b[half * 2 + goal] = block[goal * 96 : goal * 96 + 96]
    sum_b.start()
    for half in range(2):
        block = ring_a.end(half).astype(bf16)
        for goal in range(2):
            second_a[half * 2 + goal] = block[:, goal * 384 : goal * 384 + 384]
    sum_a.start()
    lax.fori_loop(5, 6, backward, 0)
    sides_2, inner_2 = frames_out(2)
    results = [pltpu.make_async_copy(dq, dq_out, local_sem.at[5])]
    results[0].start()
    outer_out += rows_out(1, sides_1)
    inner_1.forward()
    pair_sums[1] = sum_b.end().astype(bf16)
    pair_sums[0] = sum_a.end().astype(bf16)
    low = start(pair_sums.at[1 - z_lo], pair_in, low_peer)
    outer_out += rows_out(2, sides_2)
    low.wait_recv()
    tall = (pair_sums[z_lo].astype(f32) + pair_in[...].astype(f32)).astype(bf16)
    slots_out[...] = jnp.dot(pick[...], tall, preferred_element_type=f32).astype(bf16).reshape(16, 16, 384)
    lasts = [start(slots_out.at[(ha + i + 1) % 16], slots_in.at[ha], others[i]) for i in range(15)]
    slots_in[ha] = slots_out[ha]
    inner_2.forward()
    for i in range(2):
        dkv_out[i, :, 1:3] = dkv[i, 1:5, 2:4]
        for f, came in ((0, from_left), (3, from_right)):
            dkv_out[i, f, 1:3] = came[i, 2:4]

    def result(index, rows):
        made = pltpu.make_async_copy(dkv_out.at[:, :, rows], dkv_hbm.at[:, :, rows], local_sem.at[index])
        made.start()
        results.append(made)

    result(6, pl.ds(1, 2))
    for swap in (inner_0, inner_1, inner_2):
        swap.wait()
    for made in outer_out:
        made.wait_recv()
    for i in range(2):
        for f, own in ((0, from_left), (1, None), (2, None), (3, from_right)):
            for r, came in ((0, from_above), (3, from_below)):
                base = dkv[i, f + 1, r + 1] if own is None else own[i, r + 1]
                dkv_out[i, f, r] = (base.astype(f32) + came[i, f].astype(f32)).astype(bf16)
    result(7, pl.ds(0, 1))
    result(8, pl.ds(3, 1))
    for made in lasts:
        made.wait_recv()
    for goal in range(4):
        total = sum(slots_in[i * 4 + goal].astype(f32) for i in range(4)) * 0.00390625
        for slot in range(6):
            owned[slot, :, goal * 384 : goal * 384 + 384] = total[slot * 2 : slot * 2 + 2]
    for made in results:
        made.wait()
    copies.drain()
    for swap in (*rows_in[:2], inner_0, inner_1, inner_2):
        swap.drain()


def run_block(q, kv, up, weight, windows, bucket_owner):
    bf16 = jnp.bfloat16
    vmem = pl.BlockSpec(memory_space=pltpu.VMEM)
    anywhere = pl.BlockSpec(memory_space=pl.ANY)
    return pl.pallas_call(
        block_kernel,
        out_shape=[
            jax.ShapeDtypeStruct((256, 1536), bf16),
            jax.ShapeDtypeStruct((2, 4, 4, 16, 1536), bf16),
            jax.ShapeDtypeStruct((6, 2, 1536), jnp.float32),
        ],
        in_specs=[anywhere, anywhere, anywhere, anywhere, vmem, vmem],
        out_specs=[anywhere, anywhere, vmem],
        scratch_shapes=[
            pltpu.VMEM((2, 6, 6, 16, 1536), bf16),
            pltpu.VMEM((2, 6, 6, 16, 1536), bf16),
            pltpu.VMEM((2, 2, 4, 2, 48, 1536), bf16),
            pltpu.VMEM((12, 576, 256), jnp.float32),
            pltpu.VMEM((576, 256), jnp.int32),
            pltpu.VMEM((16, 96, 256), bf16),
            pltpu.VMEM((8, 96, 256), bf16),
            pltpu.VMEM((256, 1536), bf16),
            pltpu.VMEM((2, 6, 16, 1536), bf16),
            pltpu.VMEM((2, 6, 16, 1536), bf16),
            pltpu.VMEM((2, 4, 16, 1536), bf16),
            pltpu.VMEM((2, 4, 16, 1536), bf16),
            pltpu.VMEM((4, 2, 96, 768), bf16),
            pltpu.VMEM((4, 2, 192, 384), bf16),
            pltpu.VMEM((4, 96, 384), bf16),
            pltpu.VMEM((4, 96, 384), bf16),
            pltpu.VMEM((3, 96, 384), bf16),
            pltpu.VMEM((3, 96, 384), bf16),
            pltpu.VMEM((2, 96, 384), bf16),
            pltpu.VMEM((96, 384), bf16),
            pltpu.VMEM((16, 16, 384), bf16),
            pltpu.VMEM((16, 16, 384), bf16),
            pltpu.VMEM((2, 4, 16, FAR), bf16),
            pltpu.VMEM((3, 2, 2, 16, 512), bf16),
            *ring_buffers(96, 768),
            *ring_buffers(192, 384),
            pltpu.VMEM((256, 1536), bf16),
            pltpu.VMEM((256, 1536), bf16),
            pltpu.VMEM((256, 1536), bf16),
            pltpu.VMEM((2, 4, 4, 16, 1536), bf16),
            pltpu.VMEM((256, 96), bf16),
            pltpu.VMEM((HEADS, 256), jnp.int32),
            pltpu.SemaphoreType.DMA((160,)),
            pltpu.SemaphoreType.DMA((160,)),
            pltpu.SemaphoreType.DMA((6, 3)),
            pltpu.SemaphoreType.DMA((12,)),
        ],
        compiler_params=pltpu.CompilerParams(
            collective_id=1, has_side_effects=True, vmem_limit_bytes=56 * 1024 * 1024
        ),
    )(q, kv, up, weight, windows, bucket_owner)


def per_device(queries, keys_values, upstream, out_weight, windows, bucket_owner):
    grad_query, grad_pairs, owned = run_block(
        queries.reshape(256, 1536),
        keys_values,
        upstream.reshape(256, 1536),
        out_weight,
        windows.T,
        bucket_owner,
    )
    return grad_query.reshape(queries.shape), grad_pairs, owned


def solution(mesh):
    return jax.shard_map(
        per_device,
        mesh=mesh,
        in_specs=(
            P("ta", "ha", None, None),
            P(None, "ta", "ha", None, None),
            P("ta", "ha", None, None),
            P("ha", None),
            P(),
            P(),
        ),
        out_specs=(P("ta", "ha", None, None), P(None, "ta", "ha", None, None), P("ha", "ta", None)),
        check_vma=False,
    )
```

```python
import math

import jax
import jax.numpy as jnp
from jax import lax
from jax.experimental import pallas as pl
from jax.experimental.pallas import tpu as pltpu
from jax.sharding import PartitionSpec as P

HEADS = 12
HEAD_DIM = 128
PARTS = ((0, 512), (512, 768), (1280, 256))
MEASURE = 45088
ACROSS = (((1,), (1,)), ((), ()))


def place():
    ta, ha = lax.axis_index("ta"), lax.axis_index("ha")
    return ta // 8, ta // 2 % 4, ta % 2, ha // 4, ha % 4


def at_place(z_lo, y, core, z_hi, x):
    return {"ta": z_lo * 8 + y * 2 + core, "ha": z_hi * 4 + x}


def size_of(ref):
    return math.prod(ref.shape) * (ref.dtype.itemsize // 2)


class Copies:
    def __init__(self, send, recv, measure):
        self.send, self.recv, self.measure, self.sent, self.count = send, recv, measure, 0, 0

    def group(self):
        made = Group(self, self.recv.at[self.count])
        self.count += 1
        return made

    def wait(self, sem, size):
        ref = self.measure.at[pl.ds(0, size // 128)]
        pltpu.make_async_copy(ref, ref, sem).wait()

    def drain(self):
        self.wait(self.send, self.sent)


def remote(src, dst, send, recv, device):
    return pltpu.make_async_remote_copy(
        src_ref=src,
        dst_ref=dst,
        send_sem=send,
        recv_sem=recv,
        device_id=device,
        device_id_type=pl.DeviceIdType.MESH,
    )


class Group:
    def __init__(self, copies, sem):
        self.copies, self.sem, self.size = copies, sem, 0

    def start(self, src, dst, device):
        self.size += size_of(src)
        self.copies.sent += size_of(src)
        remote(src, dst, self.copies.send, self.sem, device).start()

    def wait(self):
        self.copies.wait(self.sem, self.size)


class RowSwap:
    def __init__(self, copies, groups, relay_sems, spot, up, down, relay):
        self.x, next_row, last_row, x_after, x_before, high_after, high_before = spot
        up_group, down_group = groups
        if relay is None:
            up_group.start(*up, next_row)
            down_group.start(*down, last_row)
            return
        first, back, onward = (relay_sems.at[i] for i in range(3))
        up_group.size += size_of(up[0])
        down_group.size += size_of(down[0])
        direct = (
            remote(*up, first, up_group.sem, next_row),
            remote(*down, first, down_group.sem, last_row),
        )
        self.relayed = (
            remote(up[0], relay, first, back, x_after),
            remote(down[0], relay, first, back, x_before),
        )
        self.onward = (
            remote(relay, up[1], onward, up_group.sem, high_after),
            remote(relay, down[1], onward, down_group.sem, high_before),
        )
        self.done = lambda: copies.wait(first, size_of(up[0]) + size_of(down[0]))
        for edge, straight, relayed in zip((3, 0), direct, self.relayed):
            pl.when(self.x == edge)(relayed.start)
            pl.when(self.x != edge)(straight.start)

    def forward(self):
        for edge, relayed, onward in zip((0, 3), self.relayed, self.onward):

            @pl.when(self.x == edge)
            def _():
                relayed.wait_recv()
                onward.start()

    def drain(self):
        self.done()
        for edge, onward in zip((0, 3), self.onward):
            pl.when(self.x == edge)(onward.wait_send)


class RingSum:
    def __init__(self, copies, src, pos, after, before, bufs):
        self.copies, self.src, self.pos, self.after, self.before = copies, src, pos, after, before
        self.left, self.right, self.via_left, self.via_right, self.stage = bufs

    def start(self):
        pos, src = self.pos, self.src
        far = (pos + 2) % 4
        self.first = [self.copies.group(), self.copies.group()]
        self.rest = self.copies.group()
        self.first[0].start(src.at[far, 0], self.via_left, self.after)
        self.first[1].start(src.at[far, 1], self.via_right, self.before)
        self.rest.start(src.at[(pos + 1) % 4, 1], self.left.at[1], self.after)
        self.rest.start(src.at[(pos + 3) % 4, 0], self.right.at[0], self.before)

    def middle(self):
        pos, src = self.pos, self.src
        for index, (via, goal, dst, device) in enumerate(
            (
                (self.via_left, (pos + 1) % 4, self.left, self.after),
                (self.via_right, (pos + 3) % 4, self.right, self.before),
            )
        ):
            self.first[index].wait()
            total = via[...].astype(jnp.float32) + src[goal, index].astype(jnp.float32)
            self.stage[index] = total.astype(self.stage.dtype)
            self.rest.start(self.stage.at[index], dst.at[index], device)

    def end(self):
        self.rest.wait()
        return [
            self.src[self.pos, half].astype(jnp.float32)
            + self.left[half].astype(jnp.float32)
            + self.right[half].astype(jnp.float32)
            for half in range(2)
        ]


class DirectSum:
    def __init__(self, copies, src, pos, peers, came):
        self.copies, self.src, self.pos, self.peers, self.came = copies, src, pos, peers, came

    def start(self):
        self.group = self.copies.group()
        for i in range(3):
            self.group.start(self.src.at[(self.pos + i + 1) % 4], self.came.at[i], self.peers[i])

    def end(self):
        self.group.wait()
        return sum((self.came[i].astype(jnp.float32) for i in range(3)), self.src[self.pos].astype(jnp.float32))


def ring_buffers(rows, columns):
    return [
        pltpu.VMEM((2, rows, columns), jnp.bfloat16),
        pltpu.VMEM((2, rows, columns), jnp.bfloat16),
        pltpu.VMEM((rows, columns), jnp.bfloat16),
        pltpu.VMEM((rows, columns), jnp.bfloat16),
        pltpu.VMEM((2, rows, columns), jnp.bfloat16),
    ]


class RingGather:
    def __init__(self, copies, blocks, pos, after, before):
        self.copies, self.blocks, self.pos, self.after, self.before = copies, blocks, pos, after, before

    def send(self, group, step, begin, size, device):
        for part in self.blocks((self.pos + step) % 4, begin, size):
            group.start(part, part, device)

    def start(self):
        self.from_before, self.from_after, self.far = (self.copies.group() for _ in range(3))
        self.send(self.from_before, 0, 0, 4, self.after)
        self.send(self.from_after, 0, 0, 4, self.before)

    def middle(self):
        self.from_before.wait()
        self.send(self.far, 3, 0, 2, self.after)
        self.from_after.wait()
        self.send(self.far, 1, 2, 2, self.before)

    def end(self):
        self.far.wait()


def window_bits(need):
    time_index, height_index = lax.axis_index("ta"), lax.axis_index("ha")
    key = lax.broadcasted_iota(jnp.int32, (96, 256), 0)
    token = lax.broadcasted_iota(jnp.int32, (96, 256), 1)
    row_gap = jnp.abs((token >> 4 & 3) - (key >> 4) + 1)
    tile_gap = jnp.abs((token >> 3 & 1) - (key >> 3 & 1))
    row = height_index * 4 + (key >> 4) - 1
    base = jnp.where((row_gap > 1) | (row < 0) | (row >= 64), 8, row_gap * 2 + tile_gap * 4)
    for f in range(6):
        time_gap = jnp.abs((token >> 6) - f + 1)
        frame = time_index * 4 + f - 1
        outside = (time_gap > 1) | (frame < 0) | (frame >= 64)
        need[f * 96 : f * 96 + 96] = base | jnp.where(outside, 8, time_gap)


def window_blocks(windows, blocks):
    axis = lax.broadcasted_iota(jnp.int32, (3, HEADS), 0)
    bits = jnp.sum(jnp.where(windows[...] > 1, 1 << axis, 0), axis=0, keepdims=True)
    row = lax.broadcasted_iota(jnp.int32, (HEADS, HEADS), 0)
    lane = lax.broadcasted_iota(jnp.int32, (HEADS, HEADS), 1)
    down = jnp.sum(jnp.where(row == lane, bits, 0), axis=1, keepdims=True)
    blocks[...] = jnp.broadcast_to(15 - down, (HEADS, 256))


def slot_picks(bucket_owner, pick):
    owners = bucket_owner[...].reshape(1, 48)
    row = lax.broadcasted_iota(jnp.int32, (48, 48), 0)
    lane = lax.broadcasted_iota(jnp.int32, (48, 48), 1)
    down = jnp.sum(jnp.where(row == lane, owners, 0), axis=1, keepdims=True)
    row = lax.broadcasted_iota(jnp.int32, (48, 96), 0)
    lane = lax.broadcasted_iota(jnp.int32, (48, 96), 1)
    along = jnp.sum(jnp.where(row == lane >> 1, down, 0), axis=0, keepdims=True)
    earlier = (down == along) & (row < lane >> 1)
    ranking = jnp.sum(jnp.where(earlier, 1, 0), axis=0, keepdims=True)
    chosen = along * 16 + ranking * 2 + (lane[0:1] & 1)
    row = lax.broadcasted_iota(jnp.int32, (256, 96), 0)
    pick[...] = jnp.where(row == chosen, 1.0, 0.0).astype(jnp.bfloat16)


def block_kernel(q_in, kv_in, up_hbm, weight_in, windows, bucket_owner, dq_out, dkv_hbm, owned, *refs):
    f32, bf16 = jnp.float32, jnp.bfloat16
    kv, dkv, weight, probs_all, need, at, at_in, up_in = refs[:8]
    from_left, from_right, from_above, from_below = refs[8:12]
    first_a, first_b, second_a, second_b, came_a, came_b, pair_sums, pair_in = refs[12:20]
    slots_out, slots_in, relay_kv, relay_grad = refs[20:24]
    rings = [refs[24 + 5 * i : 29 + 5 * i] for i in range(2)]
    q, up, dq, dkv_out, pick, blocks = refs[34:40]
    measure, send, recv, relay_sems, local_sem = refs[40:]
    z_lo, y, core, z_hi, x = place()
    ta, ha = lax.axis_index("ta"), lax.axis_index("ha")
    partner = at_place(z_lo, y, 1 - core, z_hi, x)
    y_after, y_before = (at_place(z_lo, (y + s) % 4, core, z_hi, x) for s in (1, 3))
    x_peers = [at_place(z_lo, y, core, z_hi, (x + s) % 4) for s in (1, 2, 3)]
    x_after, _, x_before = x_peers
    low_peer = at_place(1 - z_lo, y, core, z_hi, x)
    high_peers = [at_place(z_lo, y, core, (z_hi + s) % 4, x) for s in (1, 2, 3)]
    next_row, last_row = ({"ta": ta, "ha": (ha + s) % 16} for s in (1, 15))
    next_frame, last_frame = ({"ta": (ta + s) % 16, "ha": ha} for s in (1, 15))
    spot = (x, next_row, last_row, x_after, x_before, high_peers[0], high_peers[2])

    own_copies = [
        pltpu.make_async_copy(src, dst, local_sem.at[i])
        for i, (src, dst) in enumerate(((kv_in, kv.at[:, pl.ds(1, 4), pl.ds(1, 4)]), (q_in, q), (up_hbm, up)))
    ]
    half_rows = pl.ds(pl.multiple_of(core * 48, 16), 48)
    tiles = [
        pl.multiple_of(jnp.where(z_hi % 2 == 0, even, odd) * 128, 128)
        for even, odd in ((y * 2, y), (y * 2 + 1, y * 2 + 4), (y + 8, y * 2 + 5))
    ]
    places = [(weight_in.at[half_rows, pl.ds(c, 128)], weight.at[z_hi // 2, z_hi % 2, x, core, :, pl.ds(c, 128)]) for c in tiles]
    weight_copies = [pltpu.make_async_copy(*place, local_sem.at[9 + i]) for i, place in enumerate(places)]
    for made in weight_copies:
        made.start()
    for made in own_copies:
        made.start()
    others = [{"ta": ta, "ha": (ha + s) % 16} for s in range(1, 16)]
    y_far = at_place(z_lo, (y + 2) % 4, core, z_hi, x)
    peers = [partner, y_after, y_far, y_before, low_peer, next_frame, last_frame, *others]
    barrier = pltpu.get_barrier_semaphore()
    for peer in peers:
        pl.semaphore_signal(barrier, inc=1, device_id=peer, device_id_type=pl.DeviceIdType.MESH)
    window_bits(need)
    window_blocks(windows, blocks)
    slot_picks(bucket_owner, pick)
    pl.semaphore_wait(barrier, len(peers))

    copies = Copies(send, recv, measure)

    def start(src, dst, device):
        group = copies.group()
        group.start(src, dst, device)
        return group

    mine = pl.ds(1, 4)

    def share(p, first, width):
        return pl.ds(pl.multiple_of(first + p * width, 128), width)

    def over_x(p, begin, size):
        zs = pl.ds(begin // 2, size // 2)
        return (weight.at[zs, 0, p, core, :, share(y, 0, 256)], weight.at[zs, 1, p, core, :, share(y, 0, 128)])

    def over_y_direct(p, begin, size):
        zs = pl.ds(begin // 2, size // 2)
        return (weight.at[zs, 0, x, core, :, share(p, 1024, 128)], weight.at[zs, 1, x, core, :, share(p, 512, 256)])

    def over_y(p, begin, size):
        xs = pl.ds(begin, size)
        return (weight.at[:, 0, xs, core, :, share(p, 0, 256)], weight.at[:, 1, xs, core, :, share(p, 0, 128)])

    def over_x_direct(p, begin, size):
        return (
            weight.at[:, 0, p, core, :, pl.ds(1024 + begin * 128, size * 128)],
            weight.at[:, 1, p, core, :, pl.ds(512 + begin * 256, size * 256)],
        )

    gather_x = RingGather(copies, over_x, x, x_after, x_before)
    gather_e = RingGather(copies, over_y_direct, y, y_after, y_before)
    gather_y = RingGather(copies, over_y, y, y_after, y_before)
    gather_d = RingGather(copies, over_x_direct, x, x_after, x_before)
    swaps = copies.group()

    def swap_parts(*steps):
        for step in steps:
            gather_d.send(swaps, step, 0, 4, partner)
            gather_y.send(swaps, step, 0, 4, partner)

    pieces = copies.group()
    for src, dst in places:
        for peer in high_peers:
            pieces.start(src, dst, peer)
    edge_groups, rows_groups = ((copies.group(), copies.group()) for _ in range(2))
    for frame in (3, 0):
        edge_groups[0].start(kv_in.at[:, frame, 3], kv.at[:, frame + 1, 0], next_row)
        edge_groups[1].start(kv_in.at[:, frame, 0], kv.at[:, frame + 1, 5], last_row)
    rows_in = [
        RowSwap(
            copies,
            rows_groups,
            relay_sems.at[i],
            spot,
            (kv_in.at[i, pl.ds(1, 2), 3], kv.at[i, pl.ds(2, 2), 0]),
            (kv_in.at[i, pl.ds(1, 2), 0], kv.at[i, pl.ds(2, 2), 5]),
            relay_kv.at[i],
        )
        for i in range(2)
    ]
    frames_in = copies.group()
    frames_in.start(kv_in.at[:, 3], kv.at[:, 0, mine], next_frame)
    frames_in.start(kv_in.at[:, 0], kv.at[:, 5, mine], last_frame)
    up_swap = start(up_hbm, up_in, partner)
    for made in weight_copies:
        made.wait()
    pieces.wait()
    gather_x.start()
    gather_e.start()
    rows_in[0].forward()
    rows_in[1].forward()
    gather_e.middle()
    gather_x.middle()
    for group in edge_groups:
        group.wait()
    for frame, goal, device in ((4, 0, next_frame), (1, 5, last_frame)):
        for row in (0, 5):
            frames_in.start(kv.at[:, frame, row], kv.at[:, goal, row], device)
    gather_e.end()
    for group in rows_groups:
        group.wait()
    for made in own_copies:
        made.wait()
    gather_x.end()
    gather_y.start()
    gather_d.start()
    swap_parts(0)
    frames_in.wait()

    out_row = lax.broadcasted_iota(jnp.int32, (128, 128), 0)
    feature = lax.broadcasted_iota(jnp.int32, (128, 128), 1)
    group = out_row >> 3
    turn = (group >> 2 & 1) * 8 + (group & 3) * 2 + (group >> 3)
    wanted = (out_row >> 1 & 3) * 32 + turn * 2 + (out_row & 1)
    order = (wanted == feature).astype(bf16)
    scaling = HEAD_DIM ** (-0.5)

    def forward(pair, carry):
        outs = []
        for side in range(2):
            head = pair * 2 + side
            cols = pl.ds(pl.multiple_of(head * 128, 128), 128)
            keys, values = (kv[i, :, :, :, cols].reshape(576, 128) for i in range(2))
            block = blocks[pl.ds(head, 1), :]
            scores = lax.dot_general(keys, q[:, cols], ACROSS, preferred_element_type=f32)
            scores = jnp.where((need[...] & block) == 0, scores, -1e30)
            highest = jnp.max(scores, axis=0, keepdims=True)
            weights = jnp.exp2((scores - highest) * (scaling * 1.4426950408889634))
            probs = weights * (1.0 / jnp.sum(weights, axis=0, keepdims=True))
            probs_all[head] = probs
            values_t = lax.dot_general(order, values, ACROSS, preferred_element_type=f32).astype(bf16)
            out = jnp.dot(values_t, probs.astype(bf16), preferred_element_type=f32)
            outs.append(out.reshape(16, 8, 256))
        at[:, pl.ds(pl.multiple_of(pair * 16, 16), 16), :] = jnp.concatenate(outs, axis=1).astype(bf16)
        return carry

    def backward(pair, carry):
        begin = pl.multiple_of(pair * 256, 16)
        rows = weight_rows[pl.ds(begin, 256), :]
        grad_pair = lax.dot_general(up[...], rows, ACROSS, preferred_element_type=f32).astype(bf16)
        for side in range(2):
            head = pair * 2 + side
            cols = pl.ds(pl.multiple_of(head * 128, 128), 128)
            keys, values = (kv[i, :, :, :, cols].reshape(576, 128) for i in range(2))
            grad = grad_pair[:, side * 128 : side * 128 + 128]
            probs = probs_all[head]
            grad_probs = lax.dot_general(values, grad, ACROSS, preferred_element_type=f32)
            delta = jnp.sum(probs * grad_probs, axis=0, keepdims=True)
            grad_scores = (probs * (grad_probs - delta) * scaling).astype(bf16)
            keys_t = keys.T
            dq[:, cols] = jnp.dot(keys_t, grad_scores, preferred_element_type=f32).T.astype(bf16)
            grad_keys = jnp.dot(grad_scores, q[:, cols], preferred_element_type=f32).astype(bf16)
            grad_values = jnp.dot(probs.astype(bf16), grad, preferred_element_type=f32).astype(bf16)
            dkv[0, :, :, :, cols] = grad_keys.reshape(6, 6, 16, 128)
            dkv[1, :, :, :, cols] = grad_values.reshape(6, 6, 16, 128)
        return carry

    at_swaps = copies.group()

    def swap_outputs(half):
        rows = pl.ds(half * 48, 48)
        at_swaps.start(at.at[pl.ds((1 - core) * 8, 8), rows], at_in.at[:, rows], partner)

    lax.fori_loop(0, 3, forward, 0)
    swap_outputs(0)
    lax.fori_loop(3, 6, forward, 0)
    swap_outputs(1)
    gather_d.middle()
    gather_y.middle()
    swap_parts(3, 1)
    up_swap.wait()
    at_swaps.wait()

    def product(part, begin, width):
        a = at[pl.ds(core * 8 + part * 4, 4)].reshape(384, 256)
        b = at_in[part * 4 : part * 4 + 4].reshape(384, 256)
        total = jnp.dot(a, up[:, begin : begin + width], preferred_element_type=f32)
        total += jnp.dot(b, up_in[:, begin : begin + width], preferred_element_type=f32)
        return total.astype(bf16)

    ring_a = RingSum(copies, first_a, y, y_after, y_before, rings[0])
    ring_b = RingSum(copies, first_b, x, x_after, x_before, rings[1])
    sum_a = DirectSum(copies, second_a, x, x_peers, came_a)
    y_peers = [at_place(z_lo, (y + s) % 4, core, z_hi, x) for s in (1, 2, 3)]
    sum_b = DirectSum(copies, second_b, y, y_peers, came_b)
    for goal in range(4):
        block = product(1, goal * 384, 384)
        for half in range(2):
            first_b[goal, half] = block[half * 192 : half * 192 + 192]
    ring_b.start()
    for half in range(2):
        block = product(0, half * 768, 768)
        for goal in range(4):
            first_a[goal, half] = block[goal * 96 : goal * 96 + 96]
    ring_a.start()
    gather_d.end()
    gather_y.end()
    swap_parts(2)
    swaps.wait()
    weight_rows = weight.reshape(1536, 1536)
    inner, outer = pl.ds(2, 2), pl.ds(1, 2)
    rows_back = copies.group(), copies.group()

    def frames_out(third):
        cols = pl.ds(*PARTS[third])
        sides = (
            start(dkv.at[:, 5, :, :, cols], from_left.at[:, :, :, cols], next_frame),
            start(dkv.at[:, 0, :, :, cols], from_right.at[:, :, :, cols], last_frame),
        )
        rows = RowSwap(
            copies,
            rows_back,
            relay_sems.at[2 + third],
            spot,
            (dkv.at[:, inner, 5, :, cols], from_above.at[:, outer, :, cols]),
            (dkv.at[:, inner, 0, :, cols], from_below.at[:, outer, :, cols]),
            relay_grad.at[third, :, :, :, pl.ds(0, PARTS[third][1])],
        )
        return sides, rows

    def rows_out(third, sides):
        cols = pl.ds(*PARTS[third])
        for side, frame, came, goal in ((sides[0], 1, from_left, 0), (sides[1], 4, from_right, 3)):
            side.wait()
            total = dkv[:, frame, :, :, cols].astype(f32) + came[:, :, :, cols].astype(f32)
            came[:, :, :, cols] = total.astype(bf16)
            rows_back[0].start(came.at[:, 5, :, cols], from_above.at[:, goal, :, cols], next_row)
            rows_back[1].start(came.at[:, 0, :, cols], from_below.at[:, goal, :, cols], last_row)

    lax.fori_loop(0, 2, backward, 0)
    sides_0, inner_0 = frames_out(0)
    lax.fori_loop(2, 3, backward, 0)
    ring_b.middle()
    ring_a.middle()
    lax.fori_loop(3, 5, backward, 0)
    sides_1, inner_1 = frames_out(1)
    rows_out(0, sides_0)
    inner_0.forward()
    lax.fori_loop(5, 6, backward, 0)
    sides_2, inner_2 = frames_out(2)
    results = [pltpu.make_async_copy(dq, dq_out, local_sem.at[5])]
    results[0].start()
    for half, block in enumerate(ring_b.end()):
        for goal in range(2):
            second_b[half * 2 + goal] = block[goal * 96 : goal * 96 + 96].astype(bf16)
    sum_b.start()
    for half, block in enumerate(ring_a.end()):
        for goal in range(2):
            second_a[half * 2 + goal] = block[:, goal * 384 : goal * 384 + 384].astype(bf16)
    sum_a.start()
    rows_out(1, sides_1)
    inner_1.forward()
    pair_sums[1] = sum_b.end().astype(bf16)
    pair_sums[0] = sum_a.end().astype(bf16)
    low = start(pair_sums.at[1 - z_lo], pair_in, low_peer)
    rows_out(2, sides_2)
    low.wait()
    tall = (pair_sums[z_lo].astype(f32) + pair_in[...].astype(f32)).astype(bf16)
    slots_out[...] = jnp.dot(pick[...], tall, preferred_element_type=f32).astype(bf16).reshape(16, 16, 384)
    lasts = copies.group()
    for i in range(15):
        lasts.start(slots_out.at[(ha + i + 1) % 16], slots_in.at[ha], others[i])
    slots_in[ha] = slots_out[ha]
    inner_2.forward()
    for i in range(2):
        dkv_out[i, :, 1:3] = dkv[i, 1:5, 2:4]
        for f, came in ((0, from_left), (3, from_right)):
            dkv_out[i, f, 1:3] = came[i, 2:4]

    def result(index, rows):
        made = pltpu.make_async_copy(dkv_out.at[:, :, rows], dkv_hbm.at[:, :, rows], local_sem.at[index])
        made.start()
        results.append(made)

    result(6, pl.ds(1, 2))
    for group in rows_back:
        group.wait()
    for i in range(2):
        for f, own in ((0, from_left), (1, None), (2, None), (3, from_right)):
            for r, came in ((0, from_above), (3, from_below)):
                base = dkv[i, f + 1, r + 1] if own is None else own[i, r + 1]
                dkv_out[i, f, r] = (base.astype(f32) + came[i, f].astype(f32)).astype(bf16)
    result(7, pl.ds(0, 1))
    result(8, pl.ds(3, 1))
    lasts.wait()
    for goal in range(4):
        total = sum(slots_in[i * 4 + goal].astype(f32) for i in range(4)) * 0.00390625
        for slot in range(6):
            owned[slot, :, goal * 384 : goal * 384 + 384] = total[slot * 2 : slot * 2 + 2]
    for made in results:
        made.wait()
    copies.drain()
    for swap in (*rows_in, inner_0, inner_1, inner_2):
        swap.drain()


def run_block(q, kv, up, weight, windows, bucket_owner):
    bf16 = jnp.bfloat16
    vmem = pl.BlockSpec(memory_space=pltpu.VMEM)
    anywhere = pl.BlockSpec(memory_space=pl.ANY)
    return pl.pallas_call(
        block_kernel,
        out_shape=[
            jax.ShapeDtypeStruct((256, 1536), bf16),
            jax.ShapeDtypeStruct((2, 4, 4, 16, 1536), bf16),
            jax.ShapeDtypeStruct((6, 2, 1536), jnp.float32),
        ],
        in_specs=[anywhere, anywhere, anywhere, anywhere, vmem, vmem],
        out_specs=[anywhere, anywhere, vmem],
        scratch_shapes=[
            pltpu.VMEM((2, 6, 6, 16, 1536), bf16),
            pltpu.VMEM((2, 6, 6, 16, 1536), bf16),
            pltpu.VMEM((2, 2, 4, 2, 48, 1536), bf16),
            pltpu.VMEM((12, 576, 256), jnp.float32),
            pltpu.VMEM((576, 256), jnp.int32),
            pltpu.VMEM((16, 96, 256), bf16),
            pltpu.VMEM((8, 96, 256), bf16),
            pltpu.VMEM((256, 1536), bf16),
            pltpu.VMEM((2, 6, 16, 1536), bf16),
            pltpu.VMEM((2, 6, 16, 1536), bf16),
            pltpu.VMEM((2, 4, 16, 1536), bf16),
            pltpu.VMEM((2, 4, 16, 1536), bf16),
            pltpu.VMEM((4, 2, 96, 768), bf16),
            pltpu.VMEM((4, 2, 192, 384), bf16),
            pltpu.VMEM((4, 96, 384), bf16),
            pltpu.VMEM((4, 96, 384), bf16),
            pltpu.VMEM((3, 96, 384), bf16),
            pltpu.VMEM((3, 96, 384), bf16),
            pltpu.VMEM((2, 96, 384), bf16),
            pltpu.VMEM((96, 384), bf16),
            pltpu.VMEM((16, 16, 384), bf16),
            pltpu.VMEM((16, 16, 384), bf16),
            pltpu.VMEM((2, 2, 16, 1536), bf16),
            pltpu.VMEM((3, 2, 2, 16, 768), bf16),
            *ring_buffers(96, 768),
            *ring_buffers(192, 384),
            pltpu.VMEM((256, 1536), bf16),
            pltpu.VMEM((256, 1536), bf16),
            pltpu.VMEM((256, 1536), bf16),
            pltpu.VMEM((2, 4, 4, 16, 1536), bf16),
            pltpu.VMEM((256, 96), bf16),
            pltpu.VMEM((HEADS, 256), jnp.int32),
            pltpu.VMEM((MEASURE, 128), bf16),
            pltpu.SemaphoreType.DMA,
            pltpu.SemaphoreType.DMA((50,)),
            pltpu.SemaphoreType.DMA((5, 3)),
            pltpu.SemaphoreType.DMA((12,)),
        ],
        compiler_params=pltpu.CompilerParams(
            collective_id=1, has_side_effects=True, vmem_limit_bytes=56 * 1024 * 1024
        ),
    )(q, kv, up, weight, windows, bucket_owner)


def per_device(queries, keys_values, upstream, out_weight, windows, bucket_owner):
    grad_query, grad_pairs, owned = run_block(
        queries.reshape(256, 1536),
        keys_values,
        upstream.reshape(256, 1536),
        out_weight,
        windows.T,
        bucket_owner,
    )
    return grad_query.reshape(queries.shape), grad_pairs, owned


def solution(mesh):
    return jax.shard_map(
        per_device,
        mesh=mesh,
        in_specs=(
            P("ta", "ha", None, None),
            P(None, "ta", "ha", None, None),
            P("ta", "ha", None, None),
            P("ha", None),
            P(),
            P(),
        ),
        out_specs=(P("ta", "ha", None, None), P(None, "ta", "ha", None, None), P("ha", "ta", None)),
        check_vma=False,
    )
```

```python
import math

import jax
import jax.numpy as jnp
from jax import lax
from jax.experimental import pallas as pl
from jax.experimental.pallas import tpu as pltpu
from jax.sharding import PartitionSpec as P

HEADS = 12
HEAD_DIM = 128
PARTS = ((0, 512), (512, 768), (1280, 256))
MEASURE = 45088
ACROSS = (((1,), (1,)), ((), ()))


def place():
    ta, ha = lax.axis_index("ta"), lax.axis_index("ha")
    return ta // 8, ta // 2 % 4, ta % 2, ha // 4, ha % 4


def at_place(z_lo, y, core, z_hi, x):
    return {"ta": z_lo * 8 + y * 2 + core, "ha": z_hi * 4 + x}


def size_of(ref):
    return math.prod(ref.shape) * (ref.dtype.itemsize // 2)


class Copies:
    def __init__(self, send, recv, measure):
        self.send, self.recv, self.measure, self.sent, self.count = send, recv, measure, 0, 0

    def group(self):
        made = Group(self, self.recv.at[self.count])
        self.count += 1
        return made

    def wait(self, sem, size):
        ref = self.measure.at[pl.ds(0, size // 128)]
        pltpu.make_async_copy(ref, ref, sem).wait()

    def drain(self):
        self.wait(self.send, self.sent)


def remote(src, dst, send, recv, device):
    return pltpu.make_async_remote_copy(
        src_ref=src,
        dst_ref=dst,
        send_sem=send,
        recv_sem=recv,
        device_id=device,
        device_id_type=pl.DeviceIdType.MESH,
    )


class Group:
    def __init__(self, copies, sem):
        self.copies, self.sem, self.size = copies, sem, 0

    def start(self, src, dst, device):
        self.size += size_of(src)
        self.copies.sent += size_of(src)
        remote(src, dst, self.copies.send, self.sem, device).start()

    def wait(self):
        self.copies.wait(self.sem, self.size)


class RowSwap:
    def __init__(self, copies, groups, relay_sems, spot, up, down, relay):
        self.x, next_row, last_row, x_after, x_before, high_after, high_before = spot
        up_group, down_group = groups
        if relay is None:
            up_group.start(*up, next_row)
            down_group.start(*down, last_row)
            return
        first, back, onward = (relay_sems.at[i] for i in range(3))
        up_group.size += size_of(up[0])
        down_group.size += size_of(down[0])
        direct = (
            remote(*up, first, up_group.sem, next_row),
            remote(*down, first, down_group.sem, last_row),
        )
        self.relayed = (
            remote(up[0], relay, first, back, x_after),
            remote(down[0], relay, first, back, x_before),
        )
        self.onward = (
            remote(relay, up[1], onward, up_group.sem, high_after),
            remote(relay, down[1], onward, down_group.sem, high_before),
        )
        self.done = lambda: copies.wait(first, size_of(up[0]) + size_of(down[0]))
        for edge, straight, relayed in zip((3, 0), direct, self.relayed):
            pl.when(self.x == edge)(relayed.start)
            pl.when(self.x != edge)(straight.start)

    def forward(self):
        for edge, relayed, onward in zip((0, 3), self.relayed, self.onward):

            @pl.when(self.x == edge)
            def _():
                relayed.wait_recv()
                onward.start()

    def drain(self):
        self.done()
        for edge, onward in zip((0, 3), self.onward):
            pl.when(self.x == edge)(onward.wait_send)


class RingSum:
    def __init__(self, copies, src, pos, after, before, bufs):
        self.copies, self.src, self.pos, self.after, self.before = copies, src, pos, after, before
        self.left, self.right, self.via_left, self.via_right, self.stage = bufs

    def start(self):
        pos, src = self.pos, self.src
        far = (pos + 2) % 4
        self.first = [self.copies.group(), self.copies.group()]
        self.rest = self.copies.group()
        self.first[0].start(src.at[far, 0], self.via_left, self.after)
        self.first[1].start(src.at[far, 1], self.via_right, self.before)
        self.rest.start(src.at[(pos + 1) % 4, 1], self.left.at[1], self.after)
        self.rest.start(src.at[(pos + 3) % 4, 0], self.right.at[0], self.before)

    def middle(self):
        pos, src = self.pos, self.src
        for index, (via, goal, dst, device) in enumerate(
            (
                (self.via_left, (pos + 1) % 4, self.left, self.after),
                (self.via_right, (pos + 3) % 4, self.right, self.before),
            )
        ):
            self.first[index].wait()
            total = via[...].astype(jnp.float32) + src[goal, index].astype(jnp.float32)
            self.stage[index] = total.astype(self.stage.dtype)
            self.rest.start(self.stage.at[index], dst.at[index], device)

    def end(self):
        self.rest.wait()
        return [
            self.src[self.pos, half].astype(jnp.float32)
            + self.left[half].astype(jnp.float32)
            + self.right[half].astype(jnp.float32)
            for half in range(2)
        ]


class DirectSum:
    def __init__(self, copies, src, pos, peers, came):
        self.copies, self.src, self.pos, self.peers, self.came = copies, src, pos, peers, came

    def start(self):
        self.group = self.copies.group()
        for i in range(3):
            self.group.start(self.src.at[(self.pos + i + 1) % 4], self.came.at[i], self.peers[i])

    def end(self):
        self.group.wait()
        return sum((self.came[i].astype(jnp.float32) for i in range(3)), self.src[self.pos].astype(jnp.float32))


def ring_buffers(rows, columns):
    return [
        pltpu.VMEM((2, rows, columns), jnp.bfloat16),
        pltpu.VMEM((2, rows, columns), jnp.bfloat16),
        pltpu.VMEM((rows, columns), jnp.bfloat16),
        pltpu.VMEM((rows, columns), jnp.bfloat16),
        pltpu.VMEM((2, rows, columns), jnp.bfloat16),
    ]


class RingGather:
    def __init__(self, copies, blocks, pos, after, before):
        self.copies, self.blocks, self.pos, self.after, self.before = copies, blocks, pos, after, before

    def send(self, group, step, begin, size, device):
        for part in self.blocks((self.pos + step) % 4, begin, size):
            group.start(part, part, device)

    def start(self):
        self.from_before, self.from_after, self.far = (self.copies.group() for _ in range(3))
        self.send(self.from_before, 0, 0, 4, self.after)
        self.send(self.from_after, 0, 0, 4, self.before)

    def middle(self):
        self.from_before.wait()
        self.send(self.far, 3, 0, 2, self.after)
        self.from_after.wait()
        self.send(self.far, 1, 2, 2, self.before)

    def end(self):
        self.far.wait()


def window_bits(need):
    time_index, height_index = lax.axis_index("ta"), lax.axis_index("ha")
    key = lax.broadcasted_iota(jnp.int32, (96, 256), 0)
    token = lax.broadcasted_iota(jnp.int32, (96, 256), 1)
    row_gap = jnp.abs((token >> 4 & 3) - (key >> 4) + 1)
    tile_gap = jnp.abs((token >> 3 & 1) - (key >> 3 & 1))
    row = height_index * 4 + (key >> 4) - 1
    base = jnp.where((row_gap > 1) | (row < 0) | (row >= 64), 8, row_gap * 2 + tile_gap * 4)
    for f in range(6):
        time_gap = jnp.abs((token >> 6) - f + 1)
        frame = time_index * 4 + f - 1
        outside = (time_gap > 1) | (frame < 0) | (frame >= 64)
        need[f * 96 : f * 96 + 96] = base | jnp.where(outside, 8, time_gap)


def window_blocks(windows, blocks):
    axis = lax.broadcasted_iota(jnp.int32, (3, HEADS), 0)
    bits = jnp.sum(jnp.where(windows[...] > 1, 1 << axis, 0), axis=0, keepdims=True)
    row = lax.broadcasted_iota(jnp.int32, (HEADS, HEADS), 0)
    lane = lax.broadcasted_iota(jnp.int32, (HEADS, HEADS), 1)
    down = jnp.sum(jnp.where(row == lane, bits, 0), axis=1, keepdims=True)
    blocks[...] = jnp.broadcast_to(15 - down, (HEADS, 256))


def slot_picks(bucket_owner, pick):
    owners = bucket_owner[...].reshape(1, 48)
    row = lax.broadcasted_iota(jnp.int32, (48, 48), 0)
    lane = lax.broadcasted_iota(jnp.int32, (48, 48), 1)
    down = jnp.sum(jnp.where(row == lane, owners, 0), axis=1, keepdims=True)
    row = lax.broadcasted_iota(jnp.int32, (48, 96), 0)
    lane = lax.broadcasted_iota(jnp.int32, (48, 96), 1)
    along = jnp.sum(jnp.where(row == lane >> 1, down, 0), axis=0, keepdims=True)
    earlier = (down == along) & (row < lane >> 1)
    ranking = jnp.sum(jnp.where(earlier, 1, 0), axis=0, keepdims=True)
    chosen = along * 16 + ranking * 2 + (lane[0:1] & 1)
    row = lax.broadcasted_iota(jnp.int32, (256, 96), 0)
    pick[...] = jnp.where(row == chosen, 1.0, 0.0).astype(jnp.bfloat16)


def block_kernel(q_in, kv_in, up_hbm, weight_in, windows, bucket_owner, dq_out, dkv_hbm, owned, *refs):
    f32, bf16 = jnp.float32, jnp.bfloat16
    kv, dkv, weight, probs_all, need, at, at_in, up_in = refs[:8]
    from_left, from_right, from_above, from_below = refs[8:12]
    first_a, first_b, second_a, second_b, came_a, came_b, pair_sums, pair_in = refs[12:20]
    slots_out, slots_in, relay_kv, relay_grad = refs[20:24]
    rings = [refs[24 + 5 * i : 29 + 5 * i] for i in range(2)]
    q, up, dq, dkv_out, pick, blocks = refs[34:40]
    measure, send, recv, relay_sems, local_sem = refs[40:]
    z_lo, y, core, z_hi, x = place()
    ta, ha = lax.axis_index("ta"), lax.axis_index("ha")
    partner = at_place(z_lo, y, 1 - core, z_hi, x)
    y_after, y_before = (at_place(z_lo, (y + s) % 4, core, z_hi, x) for s in (1, 3))
    x_peers = [at_place(z_lo, y, core, z_hi, (x + s) % 4) for s in (1, 2, 3)]
    x_after, _, x_before = x_peers
    low_peer = at_place(1 - z_lo, y, core, z_hi, x)
    high_peers = [at_place(z_lo, y, core, (z_hi + s) % 4, x) for s in (1, 2, 3)]
    next_row, last_row = ({"ta": ta, "ha": (ha + s) % 16} for s in (1, 15))
    next_frame, last_frame = ({"ta": (ta + s) % 16, "ha": ha} for s in (1, 15))
    spot = (x, next_row, last_row, x_after, x_before, high_peers[0], high_peers[2])

    own_copies = [
        pltpu.make_async_copy(src, dst, local_sem.at[i])
        for i, (src, dst) in enumerate(((kv_in, kv.at[:, pl.ds(1, 4), pl.ds(1, 4)]), (q_in, q), (up_hbm, up)))
    ]
    half_rows = pl.ds(pl.multiple_of(core * 48, 16), 48)
    tiles = [
        pl.multiple_of(jnp.where(z_hi % 2 == 0, even, odd) * 128, 128)
        for even, odd in ((y * 2, y), (y * 2 + 1, y * 2 + 4), (y + 8, y * 2 + 5))
    ]
    places = [(weight_in.at[half_rows, pl.ds(c, 128)], weight.at[z_hi // 2, z_hi % 2, x, core, :, pl.ds(c, 128)]) for c in tiles]
    weight_copies = [pltpu.make_async_copy(*place, local_sem.at[9 + i]) for i, place in enumerate(places)]
    for made in weight_copies:
        made.start()
    for made in own_copies:
        made.start()
    others = [{"ta": ta, "ha": (ha + s) % 16} for s in range(1, 16)]
    y_far = at_place(z_lo, (y + 2) % 4, core, z_hi, x)
    peers = [partner, y_after, y_far, y_before, low_peer, next_frame, last_frame, *others]
    barrier = pltpu.get_barrier_semaphore()
    for peer in peers:
        pl.semaphore_signal(barrier, inc=1, device_id=peer, device_id_type=pl.DeviceIdType.MESH)
    window_bits(need)
    window_blocks(windows, blocks)
    slot_picks(bucket_owner, pick)
    pl.semaphore_wait(barrier, len(peers))

    copies = Copies(send, recv, measure)

    def start(src, dst, device):
        group = copies.group()
        group.start(src, dst, device)
        return group

    mine = pl.ds(1, 4)

    def share(p, first, width):
        return pl.ds(pl.multiple_of(first + p * width, 128), width)

    def over_x(p, begin, size):
        zs = pl.ds(begin // 2, size // 2)
        return (weight.at[zs, 0, p, core, :, share(y, 0, 256)], weight.at[zs, 1, p, core, :, share(y, 0, 128)])

    def over_y_direct(p, begin, size):
        zs = pl.ds(begin // 2, size // 2)
        return (weight.at[zs, 0, x, core, :, share(p, 1024, 128)], weight.at[zs, 1, x, core, :, share(p, 512, 256)])

    def over_y(p, begin, size):
        xs = pl.ds(begin, size)
        return (weight.at[:, 0, xs, core, :, share(p, 0, 256)], weight.at[:, 1, xs, core, :, share(p, 0, 128)])

    def over_x_direct(p, begin, size):
        return (
            weight.at[:, 0, p, core, :, pl.ds(1024 + begin * 128, size * 128)],
            weight.at[:, 1, p, core, :, pl.ds(512 + begin * 256, size * 256)],
        )

    gather_x = RingGather(copies, over_x, x, x_after, x_before)
    gather_e = RingGather(copies, over_y_direct, y, y_after, y_before)
    gather_y = RingGather(copies, over_y, y, y_after, y_before)
    gather_d = RingGather(copies, over_x_direct, x, x_after, x_before)
    swaps = copies.group()

    def swap_parts(*steps):
        for step in steps:
            gather_d.send(swaps, step, 0, 4, partner)
            gather_y.send(swaps, step, 0, 4, partner)

    pieces = copies.group()
    for src, dst in places:
        for peer in high_peers:
            pieces.start(src, dst, peer)
    edge_groups, rows_groups = ((copies.group(), copies.group()) for _ in range(2))
    for frame in (3, 0):
        edge_groups[0].start(kv_in.at[:, frame, 3], kv.at[:, frame + 1, 0], next_row)
        edge_groups[1].start(kv_in.at[:, frame, 0], kv.at[:, frame + 1, 5], last_row)
    rows_in = [
        RowSwap(
            copies,
            rows_groups,
            relay_sems.at[i],
            spot,
            (kv_in.at[i, pl.ds(1, 2), 3], kv.at[i, pl.ds(2, 2), 0]),
            (kv_in.at[i, pl.ds(1, 2), 0], kv.at[i, pl.ds(2, 2), 5]),
            relay_kv.at[i],
        )
        for i in range(2)
    ]
    frames_in = copies.group()
    frames_in.start(kv_in.at[:, 3], kv.at[:, 0, mine], next_frame)
    frames_in.start(kv_in.at[:, 0], kv.at[:, 5, mine], last_frame)
    up_swap = start(up_hbm, up_in, partner)
    def clear(head, carry):
        probs_all[head, pl.ds(384, 192), pl.ds(0, 128)] = jnp.zeros((192, 128), f32)
        probs_all[head, pl.ds(0, 192), pl.ds(128, 128)] = jnp.zeros((192, 128), f32)
        return carry

    lax.fori_loop(0, HEADS, clear, 0)
    for made in weight_copies:
        made.wait()
    pieces.wait()
    gather_x.start()
    gather_e.start()
    rows_in[0].forward()
    rows_in[1].forward()
    gather_e.middle()
    gather_x.middle()
    for group in edge_groups:
        group.wait()
    for frame, goal, device in ((4, 0, next_frame), (1, 5, last_frame)):
        for row in (0, 5):
            frames_in.start(kv.at[:, frame, row], kv.at[:, goal, row], device)
    gather_e.end()
    gather_x.end()
    gather_y.start()
    gather_d.start()
    swap_parts(0)
    for group in rows_groups:
        group.wait()
    for made in own_copies:
        made.wait()
    frames_in.wait()

    out_row = lax.broadcasted_iota(jnp.int32, (128, 128), 0)
    feature = lax.broadcasted_iota(jnp.int32, (128, 128), 1)
    group = out_row >> 3
    turn = (group >> 2 & 1) * 8 + (group & 3) * 2 + (group >> 3)
    wanted = (out_row >> 1 & 3) * 32 + turn * 2 + (out_row & 1)
    order = (wanted == feature).astype(bf16)
    scaling = HEAD_DIM ** (-0.5)

    def forward(pair, carry):
        outs = []
        for side in range(2):
            head = pair * 2 + side
            cols = pl.ds(pl.multiple_of(head * 128, 128), 128)
            keys, values = (kv[i, :, :, :, cols].reshape(576, 128) for i in range(2))
            block = blocks[pl.ds(head, 1), :]
            for half in range(2):
                rows, tokens = pl.ds(half * 192, 384), pl.ds(half * 128, 128)
                scores = lax.dot_general(
                    keys[half * 192 : half * 192 + 384], q[tokens, cols], ACROSS, preferred_element_type=f32
                )
                scores = jnp.where((need[rows, tokens] & block[:, :128]) == 0, scores, -1e30)
                highest = jnp.max(scores, axis=0, keepdims=True)
                weights = jnp.exp2((scores - highest) * (scaling * 1.4426950408889634))
                probs_all[head, rows, tokens] = weights * (1.0 / jnp.sum(weights, axis=0, keepdims=True))
            values_t = lax.dot_general(order, values, ACROSS, preferred_element_type=f32).astype(bf16)
            out = jnp.dot(values_t, probs_all[head].astype(bf16), preferred_element_type=f32)
            outs.append(out.reshape(16, 8, 256))
        at[:, pl.ds(pl.multiple_of(pair * 16, 16), 16), :] = jnp.concatenate(outs, axis=1).astype(bf16)
        return carry

    def backward(pair, carry):
        begin = pl.multiple_of(pair * 256, 16)
        rows = weight_rows[pl.ds(begin, 256), :]
        grad_pair = lax.dot_general(up[...], rows, ACROSS, preferred_element_type=f32).astype(bf16)
        for side in range(2):
            head = pair * 2 + side
            cols = pl.ds(pl.multiple_of(head * 128, 128), 128)
            keys, values = (kv[i, :, :, :, cols].reshape(576, 128) for i in range(2))
            grad = grad_pair[:, side * 128 : side * 128 + 128]
            probs = probs_all[head]
            grad_probs = lax.dot_general(values, grad, ACROSS, preferred_element_type=f32)
            delta = jnp.sum(probs * grad_probs, axis=0, keepdims=True)
            grad_scores = (probs * (grad_probs - delta) * scaling).astype(bf16)
            keys_t = keys.T
            dq[:, cols] = jnp.dot(keys_t, grad_scores, preferred_element_type=f32).T.astype(bf16)
            grad_keys = jnp.dot(grad_scores, q[:, cols], preferred_element_type=f32).astype(bf16)
            grad_values = jnp.dot(probs.astype(bf16), grad, preferred_element_type=f32).astype(bf16)
            dkv[0, :, :, :, cols] = grad_keys.reshape(6, 6, 16, 128)
            dkv[1, :, :, :, cols] = grad_values.reshape(6, 6, 16, 128)
        return carry

    at_swaps = copies.group()

    def swap_outputs(half):
        rows = pl.ds(half * 48, 48)
        at_swaps.start(at.at[pl.ds((1 - core) * 8, 8), rows], at_in.at[:, rows], partner)

    lax.fori_loop(0, 3, forward, 0)
    swap_outputs(0)
    lax.fori_loop(3, 6, forward, 0)
    swap_outputs(1)
    gather_d.middle()
    gather_y.middle()
    swap_parts(3, 1)
    up_swap.wait()
    at_swaps.wait()

    def product(part, begin, width):
        a = at[pl.ds(core * 8 + part * 4, 4)].reshape(384, 256)
        b = at_in[part * 4 : part * 4 + 4].reshape(384, 256)
        total = jnp.dot(a, up[:, begin : begin + width], preferred_element_type=f32)
        total += jnp.dot(b, up_in[:, begin : begin + width], preferred_element_type=f32)
        return total.astype(bf16)

    ring_a = RingSum(copies, first_a, y, y_after, y_before, rings[0])
    ring_b = RingSum(copies, first_b, x, x_after, x_before, rings[1])
    sum_a = DirectSum(copies, second_a, x, x_peers, came_a)
    y_peers = [at_place(z_lo, (y + s) % 4, core, z_hi, x) for s in (1, 2, 3)]
    sum_b = DirectSum(copies, second_b, y, y_peers, came_b)
    for goal in range(4):
        block = product(1, goal * 384, 384)
        for half in range(2):
            first_b[goal, half] = block[half * 192 : half * 192 + 192]
    ring_b.start()
    for half in range(2):
        block = product(0, half * 768, 768)
        for goal in range(4):
            first_a[goal, half] = block[goal * 96 : goal * 96 + 96]
    ring_a.start()
    gather_d.end()
    gather_y.end()
    swap_parts(2)
    swaps.wait()
    weight_rows = weight.reshape(1536, 1536)
    inner, outer = pl.ds(2, 2), pl.ds(1, 2)
    rows_back = copies.group(), copies.group()

    def frames_out(third):
        cols = pl.ds(*PARTS[third])
        sides = (
            start(dkv.at[:, 5, :, :, cols], from_left.at[:, :, :, cols], next_frame),
            start(dkv.at[:, 0, :, :, cols], from_right.at[:, :, :, cols], last_frame),
        )
        rows = RowSwap(
            copies,
            rows_back,
            relay_sems.at[2 + third],
            spot,
            (dkv.at[:, inner, 5, :, cols], from_above.at[:, outer, :, cols]),
            (dkv.at[:, inner, 0, :, cols], from_below.at[:, outer, :, cols]),
            relay_grad.at[third, :, :, :, pl.ds(0, PARTS[third][1])],
        )
        return sides, rows

    def rows_out(third, sides):
        cols = pl.ds(*PARTS[third])
        for side, frame, came, goal in ((sides[0], 1, from_left, 0), (sides[1], 4, from_right, 3)):
            side.wait()
            total = dkv[:, frame, :, :, cols].astype(f32) + came[:, :, :, cols].astype(f32)
            came[:, :, :, cols] = total.astype(bf16)
            rows_back[0].start(came.at[:, 5, :, cols], from_above.at[:, goal, :, cols], next_row)
            rows_back[1].start(came.at[:, 0, :, cols], from_below.at[:, goal, :, cols], last_row)

    lax.fori_loop(0, 2, backward, 0)
    sides_0, inner_0 = frames_out(0)
    lax.fori_loop(2, 3, backward, 0)
    ring_b.middle()
    ring_a.middle()
    lax.fori_loop(3, 5, backward, 0)
    sides_1, inner_1 = frames_out(1)
    rows_out(0, sides_0)
    inner_0.forward()
    lax.fori_loop(5, 6, backward, 0)
    sides_2, inner_2 = frames_out(2)
    results = [pltpu.make_async_copy(dq, dq_out, local_sem.at[5])]
    results[0].start()
    for half, block in enumerate(ring_b.end()):
        for goal in range(2):
            second_b[half * 2 + goal] = block[goal * 96 : goal * 96 + 96].astype(bf16)
    sum_b.start()
    for half, block in enumerate(ring_a.end()):
        for goal in range(2):
            second_a[half * 2 + goal] = block[:, goal * 384 : goal * 384 + 384].astype(bf16)
    sum_a.start()
    rows_out(1, sides_1)
    inner_1.forward()
    pair_sums[1] = sum_b.end().astype(bf16)
    pair_sums[0] = sum_a.end().astype(bf16)
    low = start(pair_sums.at[1 - z_lo], pair_in, low_peer)
    rows_out(2, sides_2)
    low.wait()
    tall = (pair_sums[z_lo].astype(f32) + pair_in[...].astype(f32)).astype(bf16)
    slots_out[...] = jnp.dot(pick[...], tall, preferred_element_type=f32).astype(bf16).reshape(16, 16, 384)
    lasts = copies.group()
    for i in range(15):
        lasts.start(slots_out.at[(ha + i + 1) % 16], slots_in.at[ha], others[i])
    slots_in[ha] = slots_out[ha]
    inner_2.forward()
    for i in range(2):
        dkv_out[i, :, 1:3] = dkv[i, 1:5, 2:4]
        for f, came in ((0, from_left), (3, from_right)):
            dkv_out[i, f, 1:3] = came[i, 2:4]

    def result(index, rows):
        made = pltpu.make_async_copy(dkv_out.at[:, :, rows], dkv_hbm.at[:, :, rows], local_sem.at[index])
        made.start()
        results.append(made)

    result(6, pl.ds(1, 2))
    for group in rows_back:
        group.wait()
    for i in range(2):
        for f, own in ((0, from_left), (1, None), (2, None), (3, from_right)):
            for r, came in ((0, from_above), (3, from_below)):
                base = dkv[i, f + 1, r + 1] if own is None else own[i, r + 1]
                dkv_out[i, f, r] = (base.astype(f32) + came[i, f].astype(f32)).astype(bf16)
    result(7, pl.ds(0, 1))
    result(8, pl.ds(3, 1))
    lasts.wait()
    for goal in range(4):
        total = sum(slots_in[i * 4 + goal].astype(f32) for i in range(4)) * 0.00390625
        for slot in range(6):
            owned[slot, :, goal * 384 : goal * 384 + 384] = total[slot * 2 : slot * 2 + 2]
    for made in results:
        made.wait()
    copies.drain()
    for swap in (*rows_in, inner_0, inner_1, inner_2):
        swap.drain()


def run_block(q, kv, up, weight, windows, bucket_owner):
    bf16 = jnp.bfloat16
    vmem = pl.BlockSpec(memory_space=pltpu.VMEM)
    anywhere = pl.BlockSpec(memory_space=pl.ANY)
    return pl.pallas_call(
        block_kernel,
        out_shape=[
            jax.ShapeDtypeStruct((256, 1536), bf16),
            jax.ShapeDtypeStruct((2, 4, 4, 16, 1536), bf16),
            jax.ShapeDtypeStruct((6, 2, 1536), jnp.float32),
        ],
        in_specs=[anywhere, anywhere, anywhere, anywhere, vmem, vmem],
        out_specs=[anywhere, anywhere, vmem],
        scratch_shapes=[
            pltpu.VMEM((2, 6, 6, 16, 1536), bf16),
            pltpu.VMEM((2, 6, 6, 16, 1536), bf16),
            pltpu.VMEM((2, 2, 4, 2, 48, 1536), bf16),
            pltpu.VMEM((12, 576, 256), jnp.float32),
            pltpu.VMEM((576, 256), jnp.int32),
            pltpu.VMEM((16, 96, 256), bf16),
            pltpu.VMEM((8, 96, 256), bf16),
            pltpu.VMEM((256, 1536), bf16),
            pltpu.VMEM((2, 6, 16, 1536), bf16),
            pltpu.VMEM((2, 6, 16, 1536), bf16),
            pltpu.VMEM((2, 4, 16, 1536), bf16),
            pltpu.VMEM((2, 4, 16, 1536), bf16),
            pltpu.VMEM((4, 2, 96, 768), bf16),
            pltpu.VMEM((4, 2, 192, 384), bf16),
            pltpu.VMEM((4, 96, 384), bf16),
            pltpu.VMEM((4, 96, 384), bf16),
            pltpu.VMEM((3, 96, 384), bf16),
            pltpu.VMEM((3, 96, 384), bf16),
            pltpu.VMEM((2, 96, 384), bf16),
            pltpu.VMEM((96, 384), bf16),
            pltpu.VMEM((16, 16, 384), bf16),
            pltpu.VMEM((16, 16, 384), bf16),
            pltpu.VMEM((2, 2, 16, 1536), bf16),
            pltpu.VMEM((3, 2, 2, 16, 768), bf16),
            *ring_buffers(96, 768),
            *ring_buffers(192, 384),
            pltpu.VMEM((256, 1536), bf16),
            pltpu.VMEM((256, 1536), bf16),
            pltpu.VMEM((256, 1536), bf16),
            pltpu.VMEM((2, 4, 4, 16, 1536), bf16),
            pltpu.VMEM((256, 96), bf16),
            pltpu.VMEM((HEADS, 256), jnp.int32),
            pltpu.VMEM((MEASURE, 128), bf16),
            pltpu.SemaphoreType.DMA,
            pltpu.SemaphoreType.DMA((40,)),
            pltpu.SemaphoreType.DMA((5, 3)),
            pltpu.SemaphoreType.DMA((12,)),
        ],
        compiler_params=pltpu.CompilerParams(
            collective_id=1, has_side_effects=True, vmem_limit_bytes=56 * 1024 * 1024
        ),
    )(q, kv, up, weight, windows, bucket_owner)


def per_device(queries, keys_values, upstream, out_weight, windows, bucket_owner):
    grad_query, grad_pairs, owned = run_block(
        queries.reshape(256, 1536),
        keys_values,
        upstream.reshape(256, 1536),
        out_weight,
        windows.T,
        bucket_owner,
    )
    return grad_query.reshape(queries.shape), grad_pairs, owned


def solution(mesh):
    return jax.shard_map(
        per_device,
        mesh=mesh,
        in_specs=(
            P("ta", "ha", None, None),
            P(None, "ta", "ha", None, None),
            P("ta", "ha", None, None),
            P("ha", None),
            P(),
            P(),
        ),
        out_specs=(P("ta", "ha", None, None), P(None, "ta", "ha", None, None), P("ha", "ta", None)),
        check_vma=False,
    )
```

```python
import math

import jax
import jax.numpy as jnp
from jax import lax
from jax.experimental import pallas as pl
from jax.experimental.pallas import tpu as pltpu
from jax.sharding import PartitionSpec as P

HEADS = 12
HEAD_DIM = 128
PARTS = ((0, 512), (512, 768), (1280, 256))
MEASURE = 45088
ACROSS = (((1,), (1,)), ((), ()))


def place():
    ta, ha = lax.axis_index("ta"), lax.axis_index("ha")
    return ta // 8, ta // 2 % 4, ta % 2, ha // 4, ha % 4


def at_place(z_lo, y, core, z_hi, x):
    return {"ta": z_lo * 8 + y * 2 + core, "ha": z_hi * 4 + x}


def size_of(ref):
    return math.prod(ref.shape) * (ref.dtype.itemsize // 2)


class Copies:
    def __init__(self, send, recv, measure):
        self.send, self.recv, self.measure, self.sent, self.count = send, recv, measure, 0, 0

    def group(self):
        made = Group(self, self.recv.at[self.count])
        self.count += 1
        return made

    def wait(self, sem, size):
        ref = self.measure.at[pl.ds(0, size // 128)]
        pltpu.make_async_copy(ref, ref, sem).wait()

    def drain(self):
        self.wait(self.send, self.sent)


def remote(src, dst, send, recv, device):
    return pltpu.make_async_remote_copy(
        src_ref=src,
        dst_ref=dst,
        send_sem=send,
        recv_sem=recv,
        device_id=device,
        device_id_type=pl.DeviceIdType.MESH,
    )


class Group:
    def __init__(self, copies, sem):
        self.copies, self.sem, self.size = copies, sem, 0

    def start(self, src, dst, device):
        self.size += size_of(src)
        self.copies.sent += size_of(src)
        remote(src, dst, self.copies.send, self.sem, device).start()

    def wait(self):
        self.copies.wait(self.sem, self.size)


class RowSwap:
    def __init__(self, copies, groups, relay_sems, spot, up, down, relay):
        self.x, next_row, last_row, x_after, x_before, high_after, high_before = spot
        up_group, down_group = groups
        if relay is None:
            up_group.start(*up, next_row)
            down_group.start(*down, last_row)
            return
        first, back, onward = (relay_sems.at[i] for i in range(3))
        up_group.size += size_of(up[0])
        down_group.size += size_of(down[0])
        direct = (
            remote(*up, first, up_group.sem, next_row),
            remote(*down, first, down_group.sem, last_row),
        )
        self.relayed = (
            remote(up[0], relay, first, back, x_after),
            remote(down[0], relay, first, back, x_before),
        )
        self.onward = (
            remote(relay, up[1], onward, up_group.sem, high_after),
            remote(relay, down[1], onward, down_group.sem, high_before),
        )
        self.done = lambda: copies.wait(first, size_of(up[0]) + size_of(down[0]))
        for edge, straight, relayed in zip((3, 0), direct, self.relayed):
            pl.when(self.x == edge)(relayed.start)
            pl.when(self.x != edge)(straight.start)

    def forward(self):
        for edge, relayed, onward in zip((0, 3), self.relayed, self.onward):

            @pl.when(self.x == edge)
            def _():
                relayed.wait_recv()
                onward.start()

    def drain(self):
        self.done()
        for edge, onward in zip((0, 3), self.onward):
            pl.when(self.x == edge)(onward.wait_send)


class RingSum:
    def __init__(self, copies, src, pos, after, before, bufs):
        self.copies, self.src, self.pos, self.after, self.before = copies, src, pos, after, before
        self.left, self.right, self.via_left, self.via_right, self.stage = bufs

    def start(self):
        pos, src = self.pos, self.src
        far = (pos + 2) % 4
        self.first = [self.copies.group(), self.copies.group()]
        self.rest = self.copies.group()
        self.first[0].start(src.at[far, 0], self.via_left, self.after)
        self.first[1].start(src.at[far, 1], self.via_right, self.before)
        self.rest.start(src.at[(pos + 1) % 4, 1], self.left.at[1], self.after)
        self.rest.start(src.at[(pos + 3) % 4, 0], self.right.at[0], self.before)

    def middle(self):
        pos, src = self.pos, self.src
        for index, (via, goal, dst, device) in enumerate(
            (
                (self.via_left, (pos + 1) % 4, self.left, self.after),
                (self.via_right, (pos + 3) % 4, self.right, self.before),
            )
        ):
            self.first[index].wait()
            total = via[...].astype(jnp.float32) + src[goal, index].astype(jnp.float32)
            self.stage[index] = total.astype(self.stage.dtype)
            self.rest.start(self.stage.at[index], dst.at[index], device)

    def end(self):
        self.rest.wait()
        return [
            self.src[self.pos, half].astype(jnp.float32)
            + self.left[half].astype(jnp.float32)
            + self.right[half].astype(jnp.float32)
            for half in range(2)
        ]


class DirectSum:
    def __init__(self, copies, src, pos, peers, came):
        self.copies, self.src, self.pos, self.peers, self.came = copies, src, pos, peers, came

    def start(self):
        self.group = self.copies.group()
        for i in range(3):
            self.group.start(self.src.at[(self.pos + i + 1) % 4], self.came.at[i], self.peers[i])

    def end(self):
        self.group.wait()
        return sum((self.came[i].astype(jnp.float32) for i in range(3)), self.src[self.pos].astype(jnp.float32))


def ring_buffers(rows, columns):
    return [
        pltpu.VMEM((2, rows, columns), jnp.bfloat16),
        pltpu.VMEM((2, rows, columns), jnp.bfloat16),
        pltpu.VMEM((rows, columns), jnp.bfloat16),
        pltpu.VMEM((rows, columns), jnp.bfloat16),
        pltpu.VMEM((2, rows, columns), jnp.bfloat16),
    ]


class RingGather:
    def __init__(self, copies, blocks, pos, after, before):
        self.copies, self.blocks, self.pos, self.after, self.before = copies, blocks, pos, after, before

    def send(self, group, step, begin, size, device):
        for part in self.blocks((self.pos + step) % 4, begin, size):
            group.start(part, part, device)

    def start(self):
        self.from_before, self.from_after, self.far = (self.copies.group() for _ in range(3))
        self.send(self.from_before, 0, 0, 4, self.after)
        self.send(self.from_after, 0, 0, 4, self.before)

    def middle(self):
        self.from_before.wait()
        self.send(self.far, 3, 0, 2, self.after)
        self.from_after.wait()
        self.send(self.far, 1, 2, 2, self.before)

    def end(self):
        self.far.wait()


def window_bits(need):
    time_index, height_index = lax.axis_index("ta"), lax.axis_index("ha")
    key = lax.broadcasted_iota(jnp.int32, (96, 256), 0)
    token = lax.broadcasted_iota(jnp.int32, (96, 256), 1)
    row_gap = jnp.abs((token >> 4 & 3) - (key >> 4) + 1)
    tile_gap = jnp.abs((token >> 3 & 1) - (key >> 3 & 1))
    row = height_index * 4 + (key >> 4) - 1
    base = jnp.where((row_gap > 1) | (row < 0) | (row >= 64), 8, row_gap * 2 + tile_gap * 4)
    for f in range(6):
        time_gap = jnp.abs((token >> 6) - f + 1)
        frame = time_index * 4 + f - 1
        outside = (time_gap > 1) | (frame < 0) | (frame >= 64)
        need[f * 96 : f * 96 + 96] = base | jnp.where(outside, 8, time_gap)


def window_blocks(windows, blocks):
    axis = lax.broadcasted_iota(jnp.int32, (3, HEADS), 0)
    bits = jnp.sum(jnp.where(windows[...] > 1, 1 << axis, 0), axis=0, keepdims=True)
    row = lax.broadcasted_iota(jnp.int32, (HEADS, HEADS), 0)
    lane = lax.broadcasted_iota(jnp.int32, (HEADS, HEADS), 1)
    down = jnp.sum(jnp.where(row == lane, bits, 0), axis=1, keepdims=True)
    blocks[...] = jnp.broadcast_to(15 - down, (HEADS, 256))


def slot_picks(bucket_owner, pick):
    owners = bucket_owner[...].reshape(1, 48)
    row = lax.broadcasted_iota(jnp.int32, (48, 48), 0)
    lane = lax.broadcasted_iota(jnp.int32, (48, 48), 1)
    down = jnp.sum(jnp.where(row == lane, owners, 0), axis=1, keepdims=True)
    row = lax.broadcasted_iota(jnp.int32, (48, 96), 0)
    lane = lax.broadcasted_iota(jnp.int32, (48, 96), 1)
    along = jnp.sum(jnp.where(row == lane >> 1, down, 0), axis=0, keepdims=True)
    earlier = (down == along) & (row < lane >> 1)
    ranking = jnp.sum(jnp.where(earlier, 1, 0), axis=0, keepdims=True)
    chosen = along * 16 + ranking * 2 + (lane[0:1] & 1)
    row = lax.broadcasted_iota(jnp.int32, (256, 96), 0)
    pick[...] = jnp.where(row == chosen, 1.0, 0.0).astype(jnp.bfloat16)


def block_kernel(q_in, kv_in, up_hbm, weight_in, windows, bucket_owner, dq_out, dkv_hbm, owned, *refs):
    f32, bf16 = jnp.float32, jnp.bfloat16
    kv, dkv, weight, probs_all, need, at, at_in, up_in = refs[:8]
    from_left, from_right, from_above, from_below = refs[8:12]
    first_a, first_b, second_a, second_b, came_a, came_b, pair_sums, pair_in = refs[12:20]
    slots_out, slots_in, relay_kv, relay_grad = refs[20:24]
    rings = [refs[24 + 5 * i : 29 + 5 * i] for i in range(2)]
    q, up, dq, dkv_out, pick, blocks = refs[34:40]
    measure, send, recv, relay_sems, local_sem = refs[40:]
    z_lo, y, core, z_hi, x = place()
    ta, ha = lax.axis_index("ta"), lax.axis_index("ha")
    partner = at_place(z_lo, y, 1 - core, z_hi, x)
    y_after, y_before = (at_place(z_lo, (y + s) % 4, core, z_hi, x) for s in (1, 3))
    x_peers = [at_place(z_lo, y, core, z_hi, (x + s) % 4) for s in (1, 2, 3)]
    x_after, _, x_before = x_peers
    low_peer = at_place(1 - z_lo, y, core, z_hi, x)
    high_peers = [at_place(z_lo, y, core, (z_hi + s) % 4, x) for s in (1, 2, 3)]
    next_row, last_row = ({"ta": ta, "ha": (ha + s) % 16} for s in (1, 15))
    next_frame, last_frame = ({"ta": (ta + s) % 16, "ha": ha} for s in (1, 15))
    spot = (x, next_row, last_row, x_after, x_before, high_peers[0], high_peers[2])

    own_copies = [
        pltpu.make_async_copy(src, dst, local_sem.at[i])
        for i, (src, dst) in enumerate(((kv_in, kv.at[:, pl.ds(1, 4), pl.ds(1, 4)]), (q_in, q), (up_hbm, up)))
    ]
    half_rows = pl.ds(pl.multiple_of(core * 48, 16), 48)
    tiles = [
        pl.multiple_of(jnp.where(z_hi % 2 == 0, even, odd) * 128, 128)
        for even, odd in ((y * 2, y), (y * 2 + 1, y * 2 + 4), (y + 8, y * 2 + 5))
    ]
    places = [(weight_in.at[half_rows, pl.ds(c, 128)], weight.at[z_hi // 2, z_hi % 2, x, core, :, pl.ds(c, 128)]) for c in tiles]
    weight_copies = [pltpu.make_async_copy(*place, local_sem.at[9 + i]) for i, place in enumerate(places)]
    for made in weight_copies:
        made.start()
    for made in own_copies:
        made.start()
    others = [{"ta": ta, "ha": (ha + s) % 16} for s in range(1, 16)]
    y_far = at_place(z_lo, (y + 2) % 4, core, z_hi, x)
    peers = [partner, y_after, y_far, y_before, low_peer, next_frame, last_frame, *others]
    barrier = pltpu.get_barrier_semaphore()
    for peer in peers:
        pl.semaphore_signal(barrier, inc=1, device_id=peer, device_id_type=pl.DeviceIdType.MESH)
    window_bits(need)
    window_blocks(windows, blocks)
    slot_picks(bucket_owner, pick)
    pl.semaphore_wait(barrier, len(peers))

    copies = Copies(send, recv, measure)

    def start(src, dst, device):
        group = copies.group()
        group.start(src, dst, device)
        return group

    mine = pl.ds(1, 4)

    def share(p, first, width):
        return pl.ds(pl.multiple_of(first + p * width, 128), width)

    def over_x(p, begin, size):
        zs = pl.ds(begin // 2, size // 2)
        return (weight.at[zs, 0, p, core, :, share(y, 0, 256)], weight.at[zs, 1, p, core, :, share(y, 0, 128)])

    def over_y_direct(p, begin, size):
        zs = pl.ds(begin // 2, size // 2)
        return (weight.at[zs, 0, x, core, :, share(p, 1024, 128)], weight.at[zs, 1, x, core, :, share(p, 512, 256)])

    def over_y(p, begin, size):
        xs = pl.ds(begin, size)
        return (weight.at[:, 0, xs, core, :, share(p, 0, 256)], weight.at[:, 1, xs, core, :, share(p, 0, 128)])

    def over_x_direct(p, begin, size):
        return (
            weight.at[:, 0, p, core, :, pl.ds(1024 + begin * 128, size * 128)],
            weight.at[:, 1, p, core, :, pl.ds(512 + begin * 256, size * 256)],
        )

    gather_x = RingGather(copies, over_x, x, x_after, x_before)
    gather_e = RingGather(copies, over_y_direct, y, y_after, y_before)
    gather_y = RingGather(copies, over_y, y, y_after, y_before)
    gather_d = RingGather(copies, over_x_direct, x, x_after, x_before)
    swaps = copies.group()

    def swap_parts(*steps):
        for step in steps:
            gather_d.send(swaps, step, 0, 4, partner)
            gather_y.send(swaps, step, 0, 4, partner)

    pieces = copies.group()
    for src, dst in places:
        for peer in high_peers:
            pieces.start(src, dst, peer)
    edge_groups, rows_groups = ((copies.group(), copies.group()) for _ in range(2))
    for frame in (3, 0):
        edge_groups[0].start(kv_in.at[:, frame, 3], kv.at[:, frame + 1, 0], next_row)
        edge_groups[1].start(kv_in.at[:, frame, 0], kv.at[:, frame + 1, 5], last_row)
    rows_in = [
        RowSwap(
            copies,
            rows_groups,
            relay_sems.at[i],
            spot,
            (kv_in.at[i, pl.ds(1, 2), 3], kv.at[i, pl.ds(2, 2), 0]),
            (kv_in.at[i, pl.ds(1, 2), 0], kv.at[i, pl.ds(2, 2), 5]),
            relay_kv.at[i],
        )
        for i in range(2)
    ]
    frames_in = copies.group()
    frames_in.start(kv_in.at[:, 3], kv.at[:, 0, mine], next_frame)
    frames_in.start(kv_in.at[:, 0], kv.at[:, 5, mine], last_frame)
    up_swap = start(up_hbm, up_in, partner)
    def clear(head, carry):
        probs_all[head, pl.ds(384, 192), pl.ds(0, 128)] = jnp.zeros((192, 128), f32)
        probs_all[head, pl.ds(0, 192), pl.ds(128, 128)] = jnp.zeros((192, 128), f32)
        return carry

    lax.fori_loop(0, HEADS, clear, 0)
    for made in weight_copies:
        made.wait()
    pieces.wait()
    gather_x.start()
    gather_e.start()
    rows_in[0].forward()
    rows_in[1].forward()
    gather_e.middle()
    gather_x.middle()
    for group in edge_groups:
        group.wait()
    for frame, goal, device in ((4, 0, next_frame), (1, 5, last_frame)):
        for row in (0, 5):
            frames_in.start(kv.at[:, frame, row], kv.at[:, goal, row], device)
    gather_e.end()
    gather_x.end()
    gather_y.start()
    gather_d.start()
    swap_parts(0)
    for group in rows_groups:
        group.wait()
    for made in own_copies:
        made.wait()
    frames_in.wait()

    out_row = lax.broadcasted_iota(jnp.int32, (128, 128), 0)
    feature = lax.broadcasted_iota(jnp.int32, (128, 128), 1)
    group = out_row >> 3
    turn = (group >> 2 & 1) * 8 + (group & 3) * 2 + (group >> 3)
    wanted = (out_row >> 1 & 3) * 32 + turn * 2 + (out_row & 1)
    order = (wanted == feature).astype(bf16)
    scaling = HEAD_DIM ** (-0.5)

    def forward(pair, carry):
        outs = []
        for side in range(2):
            head = pair * 2 + side
            cols = pl.ds(pl.multiple_of(head * 128, 128), 128)
            keys, values = (kv[i, :, :, :, cols].reshape(576, 128) for i in range(2))
            block = blocks[pl.ds(head, 1), :]
            for half in range(2):
                rows, tokens = pl.ds(half * 192, 384), pl.ds(half * 128, 128)
                scores = lax.dot_general(
                    keys[half * 192 : half * 192 + 384], q[tokens, cols], ACROSS, preferred_element_type=f32
                )
                scores = jnp.where((need[rows, tokens] & block[:, :128]) == 0, scores, -1e30)
                highest = jnp.max(scores, axis=0, keepdims=True)
                weights = jnp.exp2((scores - highest) * (scaling * 1.4426950408889634))
                probs_all[head, rows, tokens] = weights * (1.0 / jnp.sum(weights, axis=0, keepdims=True))
            values_t = lax.dot_general(order, values, ACROSS, preferred_element_type=f32).astype(bf16)
            out = jnp.dot(values_t, probs_all[head].astype(bf16), preferred_element_type=f32)
            outs.append(out.reshape(16, 8, 256))
        at[:, pl.ds(pl.multiple_of(pair * 16, 16), 16), :] = jnp.concatenate(outs, axis=1).astype(bf16)
        return carry

    def backward(pair, carry):
        begin = pl.multiple_of(pair * 256, 16)
        rows = weight_rows[pl.ds(begin, 256), :]
        grad_pair = lax.dot_general(up[...], rows, ACROSS, preferred_element_type=f32).astype(bf16)
        for side in range(2):
            head = pair * 2 + side
            cols = pl.ds(pl.multiple_of(head * 128, 128), 128)
            keys, values = (kv[i, :, :, :, cols].reshape(576, 128) for i in range(2))
            grad = grad_pair[:, side * 128 : side * 128 + 128]
            probs = probs_all[head]
            grad_probs = lax.dot_general(values, grad, ACROSS, preferred_element_type=f32)
            delta = jnp.sum(probs * grad_probs, axis=0, keepdims=True)
            grad_scores = (probs * (grad_probs - delta) * scaling).astype(bf16)
            keys_t = keys.T
            dq[:, cols] = jnp.dot(keys_t, grad_scores, preferred_element_type=f32).T.astype(bf16)
            grad_keys = jnp.dot(grad_scores, q[:, cols], preferred_element_type=f32).astype(bf16)
            grad_values = jnp.dot(probs.astype(bf16), grad, preferred_element_type=f32).astype(bf16)
            dkv[0, :, :, :, cols] = grad_keys.reshape(6, 6, 16, 128)
            dkv[1, :, :, :, cols] = grad_values.reshape(6, 6, 16, 128)
        return carry

    at_swaps = copies.group()

    def swap_outputs(half):
        rows = pl.ds(half * 48, 48)
        at_swaps.start(at.at[pl.ds((1 - core) * 8, 8), rows], at_in.at[:, rows], partner)

    lax.fori_loop(0, 3, forward, 0)
    swap_outputs(0)
    lax.fori_loop(3, 6, forward, 0)
    swap_outputs(1)
    gather_d.middle()
    gather_y.middle()
    swap_parts(3, 1)
    up_swap.wait()
    at_swaps.wait()

    def product(part, begin, width):
        a = at[pl.ds(core * 8 + part * 4, 4)].reshape(384, 256)
        b = at_in[part * 4 : part * 4 + 4].reshape(384, 256)
        total = jnp.dot(a, up[:, begin : begin + width], preferred_element_type=f32)
        total += jnp.dot(b, up_in[:, begin : begin + width], preferred_element_type=f32)
        return total.astype(bf16)

    ring_a = RingSum(copies, first_a, y, y_after, y_before, rings[0])
    ring_b = RingSum(copies, first_b, x, x_after, x_before, rings[1])
    sum_a = DirectSum(copies, second_a, x, x_peers, came_a)
    y_peers = [at_place(z_lo, (y + s) % 4, core, z_hi, x) for s in (1, 2, 3)]
    sum_b = DirectSum(copies, second_b, y, y_peers, came_b)
    for goal in range(4):
        block = product(1, goal * 384, 384)
        for half in range(2):
            first_b[goal, half] = block[half * 192 : half * 192 + 192]
    ring_b.start()
    for half in range(2):
        block = product(0, half * 768, 768)
        for goal in range(4):
            first_a[goal, half] = block[goal * 96 : goal * 96 + 96]
    ring_a.start()
    gather_d.end()
    gather_y.end()
    swap_parts(2)
    swaps.wait()
    weight_rows = weight.reshape(1536, 1536)
    inner, outer = pl.ds(2, 2), pl.ds(1, 2)
    rows_back = copies.group(), copies.group()

    def frames_out(third):
        cols = pl.ds(*PARTS[third])
        sides = (
            start(dkv.at[:, 5, :, :, cols], from_left.at[:, :, :, cols], next_frame),
            start(dkv.at[:, 0, :, :, cols], from_right.at[:, :, :, cols], last_frame),
        )
        rows = RowSwap(
            copies,
            rows_back,
            relay_sems.at[2 + third],
            spot,
            (dkv.at[:, inner, 5, :, cols], from_above.at[:, outer, :, cols]),
            (dkv.at[:, inner, 0, :, cols], from_below.at[:, outer, :, cols]),
            relay_grad.at[third, :, :, :, pl.ds(0, PARTS[third][1])],
        )
        return sides, rows

    def rows_out(third, sides):
        cols = pl.ds(*PARTS[third])
        for side, frame, came, goal in ((sides[0], 1, from_left, 0), (sides[1], 4, from_right, 3)):
            side.wait()
            total = dkv[:, frame, :, :, cols].astype(f32) + came[:, :, :, cols].astype(f32)
            came[:, :, :, cols] = total.astype(bf16)
            rows_back[0].start(came.at[:, 5, :, cols], from_above.at[:, goal, :, cols], next_row)
            rows_back[1].start(came.at[:, 0, :, cols], from_below.at[:, goal, :, cols], last_row)

    lax.fori_loop(0, 2, backward, 0)
    sides_0, inner_0 = frames_out(0)
    lax.fori_loop(2, 3, backward, 0)
    ring_b.middle()
    ring_a.middle()
    lax.fori_loop(3, 5, backward, 0)
    sides_1, inner_1 = frames_out(1)
    inner_0.forward()
    rows_out(0, sides_0)
    lax.fori_loop(5, 6, backward, 0)
    sides_2, inner_2 = frames_out(2)
    results = [pltpu.make_async_copy(dq, dq_out, local_sem.at[5])]
    results[0].start()
    for half, block in enumerate(ring_b.end()):
        for goal in range(2):
            second_b[half * 2 + goal] = block[goal * 96 : goal * 96 + 96].astype(bf16)
    sum_b.start()
    for half, block in enumerate(ring_a.end()):
        for goal in range(2):
            second_a[half * 2 + goal] = block[:, goal * 384 : goal * 384 + 384].astype(bf16)
    sum_a.start()
    inner_1.forward()
    rows_out(1, sides_1)
    inner_2.forward()
    pair_sums[1] = sum_b.end().astype(bf16)
    pair_sums[0] = sum_a.end().astype(bf16)
    low = start(pair_sums.at[1 - z_lo], pair_in, low_peer)
    rows_out(2, sides_2)
    low.wait()
    tall = (pair_sums[z_lo].astype(f32) + pair_in[...].astype(f32)).astype(bf16)
    slots_out[...] = jnp.dot(pick[...], tall, preferred_element_type=f32).astype(bf16).reshape(16, 16, 384)
    lasts = copies.group()
    for i in range(15):
        lasts.start(slots_out.at[(ha + i + 1) % 16], slots_in.at[ha], others[i])
    slots_in[ha] = slots_out[ha]
    for i in range(2):
        dkv_out[i, :, 1:3] = dkv[i, 1:5, 2:4]
        for f, came in ((0, from_left), (3, from_right)):
            dkv_out[i, f, 1:3] = came[i, 2:4]

    def result(index, rows):
        made = pltpu.make_async_copy(dkv_out.at[:, :, rows], dkv_hbm.at[:, :, rows], local_sem.at[index])
        made.start()
        results.append(made)

    result(6, pl.ds(1, 2))
    for group in rows_back:
        group.wait()
    for i in range(2):
        for f, own in ((0, from_left), (1, None), (2, None), (3, from_right)):
            for r, came in ((0, from_above), (3, from_below)):
                base = dkv[i, f + 1, r + 1] if own is None else own[i, r + 1]
                dkv_out[i, f, r] = (base.astype(f32) + came[i, f].astype(f32)).astype(bf16)
    result(7, pl.ds(0, 1))
    result(8, pl.ds(3, 1))
    lasts.wait()
    for goal in range(4):
        total = sum(slots_in[i * 4 + goal].astype(f32) for i in range(4)) * 0.00390625
        for slot in range(6):
            owned[slot, :, goal * 384 : goal * 384 + 384] = total[slot * 2 : slot * 2 + 2]
    for made in results:
        made.wait()
    copies.drain()
    for swap in (*rows_in, inner_0, inner_1, inner_2):
        swap.drain()


def run_block(q, kv, up, weight, windows, bucket_owner):
    bf16 = jnp.bfloat16
    vmem = pl.BlockSpec(memory_space=pltpu.VMEM)
    anywhere = pl.BlockSpec(memory_space=pl.ANY)
    return pl.pallas_call(
        block_kernel,
        out_shape=[
            jax.ShapeDtypeStruct((256, 1536), bf16),
            jax.ShapeDtypeStruct((2, 4, 4, 16, 1536), bf16),
            jax.ShapeDtypeStruct((6, 2, 1536), jnp.float32),
        ],
        in_specs=[anywhere, anywhere, anywhere, anywhere, vmem, vmem],
        out_specs=[anywhere, anywhere, vmem],
        scratch_shapes=[
            pltpu.VMEM((2, 6, 6, 16, 1536), bf16),
            pltpu.VMEM((2, 6, 6, 16, 1536), bf16),
            pltpu.VMEM((2, 2, 4, 2, 48, 1536), bf16),
            pltpu.VMEM((12, 576, 256), jnp.float32),
            pltpu.VMEM((576, 256), jnp.int32),
            pltpu.VMEM((16, 96, 256), bf16),
            pltpu.VMEM((8, 96, 256), bf16),
            pltpu.VMEM((256, 1536), bf16),
            pltpu.VMEM((2, 6, 16, 1536), bf16),
            pltpu.VMEM((2, 6, 16, 1536), bf16),
            pltpu.VMEM((2, 4, 16, 1536), bf16),
            pltpu.VMEM((2, 4, 16, 1536), bf16),
            pltpu.VMEM((4, 2, 96, 768), bf16),
            pltpu.VMEM((4, 2, 192, 384), bf16),
            pltpu.VMEM((4, 96, 384), bf16),
            pltpu.VMEM((4, 96, 384), bf16),
            pltpu.VMEM((3, 96, 384), bf16),
            pltpu.VMEM((3, 96, 384), bf16),
            pltpu.VMEM((2, 96, 384), bf16),
            pltpu.VMEM((96, 384), bf16),
            pltpu.VMEM((16, 16, 384), bf16),
            pltpu.VMEM((16, 16, 384), bf16),
            pltpu.VMEM((2, 2, 16, 1536), bf16),
            pltpu.VMEM((3, 2, 2, 16, 768), bf16),
            *ring_buffers(96, 768),
            *ring_buffers(192, 384),
            pltpu.VMEM((256, 1536), bf16),
            pltpu.VMEM((256, 1536), bf16),
            pltpu.VMEM((256, 1536), bf16),
            pltpu.VMEM((2, 4, 4, 16, 1536), bf16),
            pltpu.VMEM((256, 96), bf16),
            pltpu.VMEM((HEADS, 256), jnp.int32),
            pltpu.VMEM((MEASURE, 128), bf16),
            pltpu.SemaphoreType.DMA,
            pltpu.SemaphoreType.DMA((40,)),
            pltpu.SemaphoreType.DMA((5, 3)),
            pltpu.SemaphoreType.DMA((12,)),
        ],
        compiler_params=pltpu.CompilerParams(
            collective_id=1, has_side_effects=True, vmem_limit_bytes=56 * 1024 * 1024
        ),
    )(q, kv, up, weight, windows, bucket_owner)


def per_device(queries, keys_values, upstream, out_weight, windows, bucket_owner):
    grad_query, grad_pairs, owned = run_block(
        queries.reshape(256, 1536),
        keys_values,
        upstream.reshape(256, 1536),
        out_weight,
        windows.T,
        bucket_owner,
    )
    return grad_query.reshape(queries.shape), grad_pairs, owned


def solution(mesh):
    return jax.shard_map(
        per_device,
        mesh=mesh,
        in_specs=(
            P("ta", "ha", None, None),
            P(None, "ta", "ha", None, None),
            P("ta", "ha", None, None),
            P("ha", None),
            P(),
            P(),
        ),
        out_specs=(P("ta", "ha", None, None), P(None, "ta", "ha", None, None), P("ha", "ta", None)),
        check_vma=False,
    )
```

```python
import math

import jax
import jax.numpy as jnp
from jax import lax
from jax.experimental import pallas as pl
from jax.experimental.pallas import tpu as pltpu
from jax.sharding import PartitionSpec as P

HEADS = 12
HEAD_DIM = 128
PARTS = ((0, 512), (512, 768), (1280, 256))
MEASURE = 45088
ACROSS = (((1,), (1,)), ((), ()))


def place():
    ta, ha = lax.axis_index("ta"), lax.axis_index("ha")
    return ta // 8, ta // 2 % 4, ta % 2, ha // 4, ha % 4


def at_place(z_lo, y, core, z_hi, x):
    return {"ta": z_lo * 8 + y * 2 + core, "ha": z_hi * 4 + x}


def size_of(ref):
    return math.prod(ref.shape) * (ref.dtype.itemsize // 2)


class Copies:
    def __init__(self, send, recv, measure):
        self.send, self.recv, self.measure, self.sent, self.count = send, recv, measure, 0, 0

    def group(self):
        made = Group(self, self.recv.at[self.count])
        self.count += 1
        return made

    def wait(self, sem, size):
        ref = self.measure.at[pl.ds(0, size // 128)]
        pltpu.make_async_copy(ref, ref, sem).wait()

    def drain(self):
        self.wait(self.send, self.sent)


def remote(src, dst, send, recv, device):
    return pltpu.make_async_remote_copy(
        src_ref=src,
        dst_ref=dst,
        send_sem=send,
        recv_sem=recv,
        device_id=device,
        device_id_type=pl.DeviceIdType.MESH,
    )


class Group:
    def __init__(self, copies, sem):
        self.copies, self.sem, self.size = copies, sem, 0

    def start(self, src, dst, device):
        self.size += size_of(src)
        self.copies.sent += size_of(src)
        remote(src, dst, self.copies.send, self.sem, device).start()

    def wait(self):
        self.copies.wait(self.sem, self.size)


class RowSwap:
    def __init__(self, copies, groups, relay_sems, spot, up, down, relay):
        self.x, next_row, last_row, x_after, x_before, high_after, high_before = spot
        up_group, down_group = groups
        if relay is None:
            up_group.start(*up, next_row)
            down_group.start(*down, last_row)
            return
        first, back, onward = (relay_sems.at[i] for i in range(3))
        up_group.size += size_of(up[0])
        down_group.size += size_of(down[0])
        direct = (
            remote(*up, first, up_group.sem, next_row),
            remote(*down, first, down_group.sem, last_row),
        )
        self.relayed = (
            remote(up[0], relay, first, back, x_after),
            remote(down[0], relay, first, back, x_before),
        )
        self.onward = (
            remote(relay, up[1], onward, up_group.sem, high_after),
            remote(relay, down[1], onward, down_group.sem, high_before),
        )
        self.done = lambda: copies.wait(first, size_of(up[0]) + size_of(down[0]))
        for edge, straight, relayed in zip((3, 0), direct, self.relayed):
            pl.when(self.x == edge)(relayed.start)
            pl.when(self.x != edge)(straight.start)

    def forward(self):
        for edge, relayed, onward in zip((0, 3), self.relayed, self.onward):

            @pl.when(self.x == edge)
            def _():
                relayed.wait_recv()
                onward.start()

    def drain(self):
        self.done()
        for edge, onward in zip((0, 3), self.onward):
            pl.when(self.x == edge)(onward.wait_send)


class RingSum:
    def __init__(self, copies, src, pos, after, before, bufs):
        self.copies, self.src, self.pos, self.after, self.before = copies, src, pos, after, before
        self.left, self.right, self.via_left, self.via_right, self.stage = bufs

    def start(self):
        pos, src = self.pos, self.src
        far = (pos + 2) % 4
        self.first = [self.copies.group(), self.copies.group()]
        self.rest = self.copies.group()
        self.first[0].start(src.at[far, 0], self.via_left, self.after)
        self.first[1].start(src.at[far, 1], self.via_right, self.before)
        self.rest.start(src.at[(pos + 1) % 4, 1], self.left.at[1], self.after)
        self.rest.start(src.at[(pos + 3) % 4, 0], self.right.at[0], self.before)

    def middle(self):
        pos, src = self.pos, self.src
        for index, (via, goal, dst, device) in enumerate(
            (
                (self.via_left, (pos + 1) % 4, self.left, self.after),
                (self.via_right, (pos + 3) % 4, self.right, self.before),
            )
        ):
            self.first[index].wait()
            total = via[...].astype(jnp.float32) + src[goal, index].astype(jnp.float32)
            self.stage[index] = total.astype(self.stage.dtype)
            self.rest.start(self.stage.at[index], dst.at[index], device)

    def end(self):
        self.rest.wait()
        return [
            self.src[self.pos, half].astype(jnp.float32)
            + self.left[half].astype(jnp.float32)
            + self.right[half].astype(jnp.float32)
            for half in range(2)
        ]


class DirectSum:
    def __init__(self, copies, src, pos, peers, came):
        self.copies, self.src, self.pos, self.peers, self.came = copies, src, pos, peers, came

    def start(self):
        self.group = self.copies.group()
        for i in range(3):
            self.group.start(self.src.at[(self.pos + i + 1) % 4], self.came.at[i], self.peers[i])

    def end(self):
        self.group.wait()
        return sum((self.came[i].astype(jnp.float32) for i in range(3)), self.src[self.pos].astype(jnp.float32))


def ring_buffers(rows, columns):
    return [
        pltpu.VMEM((2, rows, columns), jnp.bfloat16),
        pltpu.VMEM((2, rows, columns), jnp.bfloat16),
        pltpu.VMEM((rows, columns), jnp.bfloat16),
        pltpu.VMEM((rows, columns), jnp.bfloat16),
        pltpu.VMEM((2, rows, columns), jnp.bfloat16),
    ]


class RingGather:
    def __init__(self, copies, blocks, pos, after, before):
        self.copies, self.blocks, self.pos, self.after, self.before = copies, blocks, pos, after, before

    def send(self, group, step, begin, size, device):
        for part in self.blocks((self.pos + step) % 4, begin, size):
            group.start(part, part, device)

    def start(self):
        self.from_before, self.from_after, self.far = (self.copies.group() for _ in range(3))
        self.send(self.from_before, 0, 0, 4, self.after)
        self.send(self.from_after, 0, 0, 4, self.before)

    def middle(self):
        self.from_before.wait()
        self.send(self.far, 3, 0, 2, self.after)
        self.from_after.wait()
        self.send(self.far, 1, 2, 2, self.before)

    def end(self):
        self.far.wait()


def window_bits(need):
    time_index, height_index = lax.axis_index("ta"), lax.axis_index("ha")
    key = lax.broadcasted_iota(jnp.int32, (96, 256), 0)
    token = lax.broadcasted_iota(jnp.int32, (96, 256), 1)
    row_gap = jnp.abs((token >> 4 & 3) - (key >> 4) + 1)
    tile_gap = jnp.abs((token >> 3 & 1) - (key >> 3 & 1))
    row = height_index * 4 + (key >> 4) - 1
    base = jnp.where((row_gap > 1) | (row < 0) | (row >= 64), 8, row_gap * 2 + tile_gap * 4)
    for f in range(6):
        time_gap = jnp.abs((token >> 6) - f + 1)
        frame = time_index * 4 + f - 1
        outside = (time_gap > 1) | (frame < 0) | (frame >= 64)
        need[f * 96 : f * 96 + 96] = base | jnp.where(outside, 8, time_gap)


def window_blocks(windows, blocks):
    axis = lax.broadcasted_iota(jnp.int32, (3, HEADS), 0)
    bits = jnp.sum(jnp.where(windows[...] > 1, 1 << axis, 0), axis=0, keepdims=True)
    row = lax.broadcasted_iota(jnp.int32, (HEADS, HEADS), 0)
    lane = lax.broadcasted_iota(jnp.int32, (HEADS, HEADS), 1)
    down = jnp.sum(jnp.where(row == lane, bits, 0), axis=1, keepdims=True)
    blocks[...] = jnp.broadcast_to(15 - down, (HEADS, 256))


def slot_picks(bucket_owner, pick):
    owners = bucket_owner[...].reshape(1, 48)
    row = lax.broadcasted_iota(jnp.int32, (48, 48), 0)
    lane = lax.broadcasted_iota(jnp.int32, (48, 48), 1)
    down = jnp.sum(jnp.where(row == lane, owners, 0), axis=1, keepdims=True)
    row = lax.broadcasted_iota(jnp.int32, (48, 96), 0)
    lane = lax.broadcasted_iota(jnp.int32, (48, 96), 1)
    along = jnp.sum(jnp.where(row == lane >> 1, down, 0), axis=0, keepdims=True)
    earlier = (down == along) & (row < lane >> 1)
    ranking = jnp.sum(jnp.where(earlier, 1, 0), axis=0, keepdims=True)
    chosen = along * 16 + ranking * 2 + (lane[0:1] & 1)
    row = lax.broadcasted_iota(jnp.int32, (256, 96), 0)
    pick[...] = jnp.where(row == chosen, 1.0, 0.0).astype(jnp.bfloat16)


def block_kernel(q_in, kv_in, up_hbm, weight_in, windows, bucket_owner, dq_out, dkv_hbm, owned, *refs):
    f32, bf16 = jnp.float32, jnp.bfloat16
    kv, dkv, weight, probs_all, need, at, at_in, up_in = refs[:8]
    from_left, from_right, from_above, from_below = refs[8:12]
    first_a, first_b, second_a, second_b, came_a, came_b, pair_sums, pair_in = refs[12:20]
    slots_out, slots_in, relay_kv, relay_grad = refs[20:24]
    rings = [refs[24 + 5 * i : 29 + 5 * i] for i in range(2)]
    q, up, dq, dkv_out, pick, blocks = refs[34:40]
    measure, send, recv, relay_sems, local_sem = refs[40:]
    z_lo, y, core, z_hi, x = place()
    ta, ha = lax.axis_index("ta"), lax.axis_index("ha")
    partner = at_place(z_lo, y, 1 - core, z_hi, x)
    y_after, y_before = (at_place(z_lo, (y + s) % 4, core, z_hi, x) for s in (1, 3))
    x_peers = [at_place(z_lo, y, core, z_hi, (x + s) % 4) for s in (1, 2, 3)]
    x_after, _, x_before = x_peers
    low_peer = at_place(1 - z_lo, y, core, z_hi, x)
    high_peers = [at_place(z_lo, y, core, (z_hi + s) % 4, x) for s in (1, 2, 3)]
    next_row, last_row = ({"ta": ta, "ha": (ha + s) % 16} for s in (1, 15))
    next_frame, last_frame = ({"ta": (ta + s) % 16, "ha": ha} for s in (1, 15))
    spot = (x, next_row, last_row, x_after, x_before, high_peers[0], high_peers[2])

    own_copies = [
        pltpu.make_async_copy(src, dst, local_sem.at[i])
        for i, (src, dst) in enumerate(((kv_in, kv.at[:, pl.ds(1, 4), pl.ds(1, 4)]), (q_in, q), (up_hbm, up)))
    ]
    half_rows = pl.ds(pl.multiple_of(core * 48, 16), 48)
    tiles = [
        pl.multiple_of(jnp.where(z_hi % 2 == 0, even, odd) * 128, 128)
        for even, odd in ((y * 2, y), (y * 2 + 1, y * 2 + 4), (y + 8, y * 2 + 5))
    ]
    places = [(weight_in.at[half_rows, pl.ds(c, 128)], weight.at[z_hi // 2, z_hi % 2, x, core, :, pl.ds(c, 128)]) for c in tiles]
    weight_copies = [pltpu.make_async_copy(*place, local_sem.at[9 + i]) for i, place in enumerate(places)]
    for made in weight_copies:
        made.start()
    for made in own_copies:
        made.start()
    others = [{"ta": ta, "ha": (ha + s) % 16} for s in range(1, 16)]
    y_far = at_place(z_lo, (y + 2) % 4, core, z_hi, x)
    peers = [partner, y_after, y_far, y_before, low_peer, next_frame, last_frame, *others]
    barrier = pltpu.get_barrier_semaphore()
    for peer in peers:
        pl.semaphore_signal(barrier, inc=1, device_id=peer, device_id_type=pl.DeviceIdType.MESH)
    window_bits(need)
    window_blocks(windows, blocks)
    slot_picks(bucket_owner, pick)
    pl.semaphore_wait(barrier, len(peers))

    copies = Copies(send, recv, measure)

    def start(src, dst, device):
        group = copies.group()
        group.start(src, dst, device)
        return group

    mine = pl.ds(1, 4)

    def share(p, first, width):
        return pl.ds(pl.multiple_of(first + p * width, 128), width)

    def over_x(p, begin, size):
        zs = pl.ds(begin // 2, size // 2)
        return (weight.at[zs, 0, p, core, :, share(y, 0, 256)], weight.at[zs, 1, p, core, :, share(y, 0, 128)])

    def over_y_direct(p, begin, size):
        zs = pl.ds(begin // 2, size // 2)
        return (weight.at[zs, 0, x, core, :, share(p, 1024, 128)], weight.at[zs, 1, x, core, :, share(p, 512, 256)])

    def over_y(p, begin, size):
        xs = pl.ds(begin, size)
        return (weight.at[:, 0, xs, core, :, share(p, 0, 256)], weight.at[:, 1, xs, core, :, share(p, 0, 128)])

    def over_x_direct(p, begin, size):
        return (
            weight.at[:, 0, p, core, :, pl.ds(1024 + begin * 128, size * 128)],
            weight.at[:, 1, p, core, :, pl.ds(512 + begin * 256, size * 256)],
        )

    gather_x = RingGather(copies, over_x, x, x_after, x_before)
    gather_e = RingGather(copies, over_y_direct, y, y_after, y_before)
    gather_y = RingGather(copies, over_y, y, y_after, y_before)
    gather_d = RingGather(copies, over_x_direct, x, x_after, x_before)
    swaps = copies.group()

    def swap_parts(*steps):
        for step in steps:
            gather_d.send(swaps, step, 0, 4, partner)
            gather_y.send(swaps, step, 0, 4, partner)

    pieces = copies.group()
    for src, dst in places:
        for peer in high_peers:
            pieces.start(src, dst, peer)
    edge_groups, rows_groups = ((copies.group(), copies.group()) for _ in range(2))
    for frame in (3, 0):
        edge_groups[0].start(kv_in.at[:, frame, 3], kv.at[:, frame + 1, 0], next_row)
        edge_groups[1].start(kv_in.at[:, frame, 0], kv.at[:, frame + 1, 5], last_row)
    rows_in = [
        RowSwap(
            copies,
            rows_groups,
            relay_sems.at[i],
            spot,
            (kv_in.at[i, pl.ds(1, 2), 3], kv.at[i, pl.ds(2, 2), 0]),
            (kv_in.at[i, pl.ds(1, 2), 0], kv.at[i, pl.ds(2, 2), 5]),
            relay_kv.at[i],
        )
        for i in range(2)
    ]
    frames_in = copies.group()
    frames_in.start(kv_in.at[:, 3], kv.at[:, 0, mine], next_frame)
    frames_in.start(kv_in.at[:, 0], kv.at[:, 5, mine], last_frame)
    up_swap = start(up_hbm, up_in, partner)
    def clear(head, carry):
        probs_all[head, pl.ds(384, 192), pl.ds(0, 128)] = jnp.zeros((192, 128), f32)
        probs_all[head, pl.ds(0, 192), pl.ds(128, 128)] = jnp.zeros((192, 128), f32)
        return carry

    lax.fori_loop(0, HEADS, clear, 0)
    for made in weight_copies:
        made.wait()
    pieces.wait()
    gather_x.start()
    gather_e.start()
    rows_in[0].forward()
    rows_in[1].forward()
    gather_e.middle()
    gather_x.middle()
    for group in edge_groups:
        group.wait()
    for frame, goal, device in ((4, 0, next_frame), (1, 5, last_frame)):
        for row in (0, 5):
            frames_in.start(kv.at[:, frame, row], kv.at[:, goal, row], device)
    gather_e.end()
    gather_x.end()
    gather_y.start()
    gather_d.start()
    swap_parts(0)
    for group in rows_groups:
        group.wait()
    for made in own_copies:
        made.wait()
    frames_in.wait()

    out_row = lax.broadcasted_iota(jnp.int32, (128, 128), 0)
    feature = lax.broadcasted_iota(jnp.int32, (128, 128), 1)
    group = out_row >> 3
    turn = (group >> 2 & 1) * 8 + (group & 3) * 2 + (group >> 3)
    wanted = (out_row >> 1 & 3) * 32 + turn * 2 + (out_row & 1)
    order = (wanted == feature).astype(bf16)
    scaling = HEAD_DIM ** (-0.5)

    def forward(pair, carry):
        outs = []
        for side in range(2):
            head = pair * 2 + side
            cols = pl.ds(pl.multiple_of(head * 128, 128), 128)
            keys, values = (kv[i, :, :, :, cols].reshape(576, 128) for i in range(2))
            block = blocks[pl.ds(head, 1), :]
            for half in range(2):
                rows, tokens = pl.ds(half * 192, 384), pl.ds(half * 128, 128)
                scores = lax.dot_general(
                    keys[half * 192 : half * 192 + 384], q[tokens, cols], ACROSS, preferred_element_type=f32
                )
                scores = jnp.where((need[rows, tokens] & block[:, :128]) == 0, scores, -1e30)
                highest = jnp.max(scores, axis=0, keepdims=True)
                weights = jnp.exp2((scores - highest) * (scaling * 1.4426950408889634))
                probs_all[head, rows, tokens] = weights * (1.0 / jnp.sum(weights, axis=0, keepdims=True))
            values_t = lax.dot_general(order, values, ACROSS, preferred_element_type=f32).astype(bf16)
            out = jnp.dot(values_t, probs_all[head].astype(bf16), preferred_element_type=f32)
            outs.append(out.reshape(16, 8, 256))
        at[:, pl.ds(pl.multiple_of(pair * 16, 16), 16), :] = jnp.concatenate(outs, axis=1).astype(bf16)
        return carry

    def backward(pair, carry):
        begin = pl.multiple_of(pair * 256, 16)
        rows = weight_rows[pl.ds(begin, 256), :]
        grad_pair = lax.dot_general(up[...], rows, ACROSS, preferred_element_type=f32).astype(bf16)
        for side in range(2):
            head = pair * 2 + side
            cols = pl.ds(pl.multiple_of(head * 128, 128), 128)
            keys, values = (kv[i, :, :, :, cols].reshape(576, 128) for i in range(2))
            grad = grad_pair[:, side * 128 : side * 128 + 128]
            probs = probs_all[head]
            grad_probs = lax.dot_general(values, grad, ACROSS, preferred_element_type=f32)
            delta = jnp.sum(probs * grad_probs, axis=0, keepdims=True)
            grad_scores = (probs * (grad_probs - delta) * scaling).astype(bf16)
            keys_t = keys.T
            dq[:, cols] = jnp.dot(keys_t, grad_scores, preferred_element_type=f32).T.astype(bf16)
            grad_keys = jnp.dot(grad_scores, q[:, cols], preferred_element_type=f32).astype(bf16)
            grad_values = jnp.dot(probs.astype(bf16), grad, preferred_element_type=f32).astype(bf16)
            dkv[0, :, :, :, cols] = grad_keys.reshape(6, 6, 16, 128)
            dkv[1, :, :, :, cols] = grad_values.reshape(6, 6, 16, 128)
        return carry

    at_swaps = copies.group()

    def swap_outputs(half):
        rows = pl.ds(half * 48, 48)
        at_swaps.start(at.at[pl.ds((1 - core) * 8, 8), rows], at_in.at[:, rows], partner)

    lax.fori_loop(0, 3, forward, 0)
    swap_outputs(0)
    lax.fori_loop(3, 6, forward, 0)
    swap_outputs(1)
    gather_d.middle()
    gather_y.middle()
    swap_parts(3, 1)
    up_swap.wait()
    at_swaps.wait()

    def product(part, begin, width):
        a = at[pl.ds(core * 8 + part * 4, 4)].reshape(384, 256)
        b = at_in[part * 4 : part * 4 + 4].reshape(384, 256)
        total = jnp.dot(a, up[:, begin : begin + width], preferred_element_type=f32)
        total += jnp.dot(b, up_in[:, begin : begin + width], preferred_element_type=f32)
        return total.astype(bf16)

    ring_a = RingSum(copies, first_a, y, y_after, y_before, rings[0])
    ring_b = RingSum(copies, first_b, x, x_after, x_before, rings[1])
    sum_a = DirectSum(copies, second_a, x, x_peers, came_a)
    y_peers = [at_place(z_lo, (y + s) % 4, core, z_hi, x) for s in (1, 2, 3)]
    sum_b = DirectSum(copies, second_b, y, y_peers, came_b)
    for goal in range(4):
        block = product(1, goal * 384, 384)
        for half in range(2):
            first_b[goal, half] = block[half * 192 : half * 192 + 192]
    ring_b.start()
    for half in range(2):
        block = product(0, half * 768, 768)
        for goal in range(4):
            first_a[goal, half] = block[goal * 96 : goal * 96 + 96]
    ring_a.start()
    gather_d.end()
    gather_d.send(swaps, 2, 0, 4, partner)
    gather_y.end()
    gather_y.send(swaps, 2, 0, 4, partner)
    swaps.wait()
    weight_rows = weight.reshape(1536, 1536)
    inner, outer = pl.ds(2, 2), pl.ds(1, 2)
    rows_back = copies.group(), copies.group()

    def frames_out(third):
        cols = pl.ds(*PARTS[third])
        sides = (
            start(dkv.at[:, 5, :, :, cols], from_left.at[:, :, :, cols], next_frame),
            start(dkv.at[:, 0, :, :, cols], from_right.at[:, :, :, cols], last_frame),
        )
        rows = RowSwap(
            copies,
            rows_back,
            relay_sems.at[2 + third],
            spot,
            (dkv.at[:, inner, 5, :, cols], from_above.at[:, outer, :, cols]),
            (dkv.at[:, inner, 0, :, cols], from_below.at[:, outer, :, cols]),
            relay_grad.at[third, :, :, :, pl.ds(0, PARTS[third][1])],
        )
        return sides, rows

    def rows_out(third, sides):
        cols = pl.ds(*PARTS[third])
        for side, frame, came, goal in ((sides[0], 1, from_left, 0), (sides[1], 4, from_right, 3)):
            side.wait()
            total = dkv[:, frame, :, :, cols].astype(f32) + came[:, :, :, cols].astype(f32)
            came[:, :, :, cols] = total.astype(bf16)
            rows_back[0].start(came.at[:, 5, :, cols], from_above.at[:, goal, :, cols], next_row)
            rows_back[1].start(came.at[:, 0, :, cols], from_below.at[:, goal, :, cols], last_row)

    lax.fori_loop(0, 2, backward, 0)
    sides_0, inner_0 = frames_out(0)
    lax.fori_loop(2, 3, backward, 0)
    ring_b.middle()
    ring_a.middle()
    lax.fori_loop(3, 5, backward, 0)
    sides_1, inner_1 = frames_out(1)
    inner_0.forward()
    rows_out(0, sides_0)
    lax.fori_loop(5, 6, backward, 0)
    sides_2, inner_2 = frames_out(2)
    results = [pltpu.make_async_copy(dq, dq_out, local_sem.at[5])]
    results[0].start()
    for half, block in enumerate(ring_b.end()):
        for goal in range(2):
            second_b[half * 2 + goal] = block[goal * 96 : goal * 96 + 96].astype(bf16)
    sum_b.start()
    for half, block in enumerate(ring_a.end()):
        for goal in range(2):
            second_a[half * 2 + goal] = block[:, goal * 384 : goal * 384 + 384].astype(bf16)
    sum_a.start()
    inner_1.forward()
    rows_out(1, sides_1)
    inner_2.forward()
    pair_sums[1] = sum_b.end().astype(bf16)
    pair_sums[0] = sum_a.end().astype(bf16)
    low = start(pair_sums.at[1 - z_lo], pair_in, low_peer)
    rows_out(2, sides_2)
    low.wait()
    tall = (pair_sums[z_lo].astype(f32) + pair_in[...].astype(f32)).astype(bf16)
    slots_out[...] = jnp.dot(pick[...], tall, preferred_element_type=f32).astype(bf16).reshape(16, 16, 384)
    lasts = copies.group()
    for i in range(15):
        lasts.start(slots_out.at[(ha + i + 1) % 16], slots_in.at[ha], others[i])
    slots_in[ha] = slots_out[ha]
    for i in range(2):
        dkv_out[i, :, 1:3] = dkv[i, 1:5, 2:4]
        for f, came in ((0, from_left), (3, from_right)):
            dkv_out[i, f, 1:3] = came[i, 2:4]

    def result(index, rows):
        made = pltpu.make_async_copy(dkv_out.at[:, :, rows], dkv_hbm.at[:, :, rows], local_sem.at[index])
        made.start()
        results.append(made)

    result(6, pl.ds(1, 2))
    for group in rows_back:
        group.wait()
    for i in range(2):
        for f, own in ((0, from_left), (1, None), (2, None), (3, from_right)):
            for r, came in ((0, from_above), (3, from_below)):
                base = dkv[i, f + 1, r + 1] if own is None else own[i, r + 1]
                dkv_out[i, f, r] = (base.astype(f32) + came[i, f].astype(f32)).astype(bf16)
    result(7, pl.ds(0, 1))
    result(8, pl.ds(3, 1))
    lasts.wait()
    for goal in range(4):
        total = sum(slots_in[i * 4 + goal].astype(f32) for i in range(4)) * 0.00390625
        for slot in range(6):
            owned[slot, :, goal * 384 : goal * 384 + 384] = total[slot * 2 : slot * 2 + 2]
    for made in results:
        made.wait()
    copies.drain()
    for swap in (*rows_in, inner_0, inner_1, inner_2):
        swap.drain()


def run_block(q, kv, up, weight, windows, bucket_owner):
    bf16 = jnp.bfloat16
    vmem = pl.BlockSpec(memory_space=pltpu.VMEM)
    anywhere = pl.BlockSpec(memory_space=pl.ANY)
    return pl.pallas_call(
        block_kernel,
        out_shape=[
            jax.ShapeDtypeStruct((256, 1536), bf16),
            jax.ShapeDtypeStruct((2, 4, 4, 16, 1536), bf16),
            jax.ShapeDtypeStruct((6, 2, 1536), jnp.float32),
        ],
        in_specs=[anywhere, anywhere, anywhere, anywhere, vmem, vmem],
        out_specs=[anywhere, anywhere, vmem],
        scratch_shapes=[
            pltpu.VMEM((2, 6, 6, 16, 1536), bf16),
            pltpu.VMEM((2, 6, 6, 16, 1536), bf16),
            pltpu.VMEM((2, 2, 4, 2, 48, 1536), bf16),
            pltpu.VMEM((12, 576, 256), jnp.float32),
            pltpu.VMEM((576, 256), jnp.int32),
            pltpu.VMEM((16, 96, 256), bf16),
            pltpu.VMEM((8, 96, 256), bf16),
            pltpu.VMEM((256, 1536), bf16),
            pltpu.VMEM((2, 6, 16, 1536), bf16),
            pltpu.VMEM((2, 6, 16, 1536), bf16),
            pltpu.VMEM((2, 4, 16, 1536), bf16),
            pltpu.VMEM((2, 4, 16, 1536), bf16),
            pltpu.VMEM((4, 2, 96, 768), bf16),
            pltpu.VMEM((4, 2, 192, 384), bf16),
            pltpu.VMEM((4, 96, 384), bf16),
            pltpu.VMEM((4, 96, 384), bf16),
            pltpu.VMEM((3, 96, 384), bf16),
            pltpu.VMEM((3, 96, 384), bf16),
            pltpu.VMEM((2, 96, 384), bf16),
            pltpu.VMEM((96, 384), bf16),
            pltpu.VMEM((16, 16, 384), bf16),
            pltpu.VMEM((16, 16, 384), bf16),
            pltpu.VMEM((2, 2, 16, 1536), bf16),
            pltpu.VMEM((3, 2, 2, 16, 768), bf16),
            *ring_buffers(96, 768),
            *ring_buffers(192, 384),
            pltpu.VMEM((256, 1536), bf16),
            pltpu.VMEM((256, 1536), bf16),
            pltpu.VMEM((256, 1536), bf16),
            pltpu.VMEM((2, 4, 4, 16, 1536), bf16),
            pltpu.VMEM((256, 96), bf16),
            pltpu.VMEM((HEADS, 256), jnp.int32),
            pltpu.VMEM((MEASURE, 128), bf16),
            pltpu.SemaphoreType.DMA,
            pltpu.SemaphoreType.DMA((40,)),
            pltpu.SemaphoreType.DMA((5, 3)),
            pltpu.SemaphoreType.DMA((12,)),
        ],
        compiler_params=pltpu.CompilerParams(
            collective_id=1, has_side_effects=True, vmem_limit_bytes=56 * 1024 * 1024
        ),
    )(q, kv, up, weight, windows, bucket_owner)


def per_device(queries, keys_values, upstream, out_weight, windows, bucket_owner):
    grad_query, grad_pairs, owned = run_block(
        queries.reshape(256, 1536),
        keys_values,
        upstream.reshape(256, 1536),
        out_weight,
        windows.T,
        bucket_owner,
    )
    return grad_query.reshape(queries.shape), grad_pairs, owned


def solution(mesh):
    return jax.shard_map(
        per_device,
        mesh=mesh,
        in_specs=(
            P("ta", "ha", None, None),
            P(None, "ta", "ha", None, None),
            P("ta", "ha", None, None),
            P("ha", None),
            P(),
            P(),
        ),
        out_specs=(P("ta", "ha", None, None), P(None, "ta", "ha", None, None), P("ha", "ta", None)),
        check_vma=False,
    )
```
